32 devices in a mesh: seq: 16 (over z, y, x), rows: 2 (over core).
Axes of the slice: x: 2, y: 2, z: 4, core: 2. Of those that a mesh axis runs over, the one named last changes fastest.
Arguments:
- inputs: float32 [2, 8192, 1024], P('rows', 'seq'), may hold values from -6 to 6
- lengths: int32 [2, 8], P('rows'), may hold values from 1 to 7681, as said below
- norm_gain: float32 [2, 1024], replicated, may hold values from 0.5 to 1.5
- in_weight: bfloat16 [2, 1024, 4384], replicated, may hold values from -0.1875 to 0.1875
- conv_weight: float32 [2, 2304, 4], replicated, may hold values from -3 to 3
- conv_bias: float32 [2, 2304], replicated, may hold values from -3 to 3
- log_decay: float32 [2, 32], replicated, may hold values from -0.7 to 0.7
- dt_bias: float32 [2, 32], replicated, may hold values from -11 to -3
- skip: float32 [2, 32], replicated, may hold values from 0.5 to 1.5
- gate_gain: float32 [2, 2048], replicated, may hold values from 0.5 to 1.5
- out_weight: bfloat16 [2, 2048, 1024], replicated, may hold values from -0.125 to 0.125
- cotangent: float32 [2, 8192, 1024], P('rows', 'seq'), may hold values from -6 to 6
Outputs:
- output: float32 [2, 8192, 1024], P('rows', 'seq')
- input_grad: float32 [2, 8192, 1024], P('rows', 'seq')
- norm_gain_grad: float32 [2, 1024], P(None, ('seq', 'rows'))
- in_weight_grad: float32 [2, 1024, 4384], P(None, ('seq', 'rows'))
- conv_weight_grad: float32 [2, 2304, 4], P(None, ('seq', 'rows'))
- conv_bias_grad: float32 [2, 2304], P(None, ('seq', 'rows'))
- log_decay_grad: float32 [2, 32], replicated
- dt_bias_grad: float32 [2, 32], replicated
- skip_grad: float32 [2, 32], replicated
- gate_gain_grad: float32 [2, 2048], P(None, ('seq', 'rows'))
- out_weight_grad: float32 [2, 2048, 1024], P(None, ('seq', 'rows'))
The draws below stay inside these ranges and needn't reach their ends.
Inputs may be any that keep to these rules, and one draw needn't show every extreme that they name: Each row's lengths sum to 8192; one of them is 7681, the others add up to 511; its place in the row varies.
All inputs are finite; a program needn't handle non-finite values.
Results may differ from the reference program's by a relative error of at most 0.0074.
Values sent between devices are 32-bit elements; how exact they have to be, the bound alone decides.
A program may use at most 320 MiB of HBM per device.

```python
import jax
import jax.numpy as jnp
from jax import lax

D = 1024
DI = 2048
STATE = 128
HEAD_DIM = 64
KW = 4
GROUP = 256
LAYERS = 2
NDOC = 8
TOK_DEV = 512
HEADS = 32
CC = 2304
PROJ = 4384
LEN = 8192
ROWS = 2


def draw_lengths(key, part):
    key = jax.random.fold_in(key, 11)
    row_keys = jax.random.split(key, ROWS)

    def one_row(row_key):
        first_key, second_key = jax.random.split(row_key, 2)
        cuts = jnp.sort(jax.random.permutation(first_key, TOK_DEV - 2)[:NDOC - 2] + 1)
        edges = jnp.concatenate([jnp.zeros((1,), jnp.int32), cuts.astype(jnp.int32), jnp.full((1,), TOK_DEV - 1, jnp.int32)])
        pieces = edges[1:] - edges[:-1]
        place = jax.random.randint(second_key, (), 0, NDOC)
        index = jnp.arange(NDOC)
        direct = pieces[jnp.clip(index, 0, NDOC - 2)]
        shifted = pieces[jnp.clip(index - 1, 0, NDOC - 2)]
        longest = jnp.full((NDOC,), LEN - TOK_DEV + 1, jnp.int32)
        return jnp.where(index < place, direct, jnp.where(index == place, longest, shifted)).astype(jnp.int32)
    return jax.vmap(one_row)(row_keys)


def steps_of(stream_key, dims, cuts, smallest, high):
    def one(axis_at, shards_of):
        heights = jax.random.uniform(jax.random.fold_in(jax.random.fold_in(stream_key, 6), axis_at), (shards_of,), jnp.float32, smallest / len(cuts), high / len(cuts))
        return jnp.repeat(jnp.exp(heights), dims[axis_at] // shards_of).reshape((-1,) + (1,) * (len(dims) - axis_at - 1))

    level = one(*cuts[0])
    for cut in cuts[1:]:
        level = level * one(*cut)
    return level


def noise(rng, extent, deviation, bound, cuts=(), kind=jnp.bfloat16):
    values = jax.random.normal(rng, extent, jnp.float32) * deviation
    if len(cuts) > 0:
        values = steps_of(rng, extent, cuts, -0.22, 0.18) * values
    return jnp.clip(values, min=-bound, max=bound).astype(kind)


def setup_inputs(seed: int = 0) -> dict:
    seeds = jax.random.split(jax.random.key(seed), 13)
    inputs = noise(seeds[0], (ROWS, LEN, D), 1.0, 6.0, ((0, 2), (1, 16)), jnp.float32)
    lengths = draw_lengths(jax.random.fold_in(seeds[12], 71), 0)
    norm_gain = jnp.clip(1.0 + 0.1 * jax.random.normal(seeds[2], (LAYERS, D), jnp.float32), 0.5, 1.5)
    in_weight = noise(seeds[3], (LAYERS, D, PROJ), D ** -0.5, 0.1875)
    conv_weight = noise(seeds[4], (LAYERS, CC, KW), KW ** -0.5, 3.0, (), jnp.float32)
    conv_bias = noise(seeds[5], (LAYERS, CC), 0.5, 3.0, (), jnp.float32)
    log_decay = jnp.clip(jax.random.uniform(seeds[6], (LAYERS, HEADS), jnp.float32, -0.7, 0.7), -0.7, 0.7)
    dt_bias = jnp.clip(jax.random.uniform(seeds[7], (LAYERS, HEADS), jnp.float32, -11.0, -3.0), -11.0, -3.0)
    skip = jnp.clip(jax.random.uniform(seeds[8], (LAYERS, HEADS), jnp.float32, 0.5, 1.5), 0.5, 1.5)
    gate_gain = jnp.clip(1.0 + 0.1 * jax.random.normal(seeds[9], (LAYERS, DI), jnp.float32), 0.5, 1.5)
    out_weight = noise(seeds[10], (LAYERS, DI, D), DI ** -0.5, 0.125)
    cotangent = noise(seeds[11], (ROWS, LEN, D), 1.0, 6.0, ((0, 2), (1, 16)), jnp.float32)
    return dict(inputs=inputs, lengths=lengths, norm_gain=norm_gain, in_weight=in_weight, conv_weight=conv_weight, conv_bias=conv_bias, log_decay=log_decay, dt_bias=dt_bias, skip=skip, gate_gain=gate_gain, out_weight=out_weight, cotangent=cotangent)


@jax.custom_vjp
def low(v):
    return lax.optimization_barrier(v.astype(jnp.bfloat16)).astype(jnp.float32)

@jax.custom_vjp
def low_back(v):
    return v

def low_keep(v):
    return (low(v), None)

def low_pass(kept, grad):
    return (grad,)

def back_keep(v):
    return (v, None)

def back_low(kept, grad):
    return (low(grad),)
low.defvjp(low_keep, low_pass)
low_back.defvjp(back_keep, back_low)
EPS = 1e-05
HIGHEST = lax.Precision.HIGHEST

def norm_rows(values, gain):
    return values * lax.rsqrt(lax.optimization_barrier(jnp.mean(values * values, -1, keepdims=True)) + EPS) * gain

def group_step(carried, block):
    values, in_map, out_map, step_size, log_rate, docs, prior = block
    cumul = jnp.cumsum(log_rate, 1)
    lower = jnp.tri(GROUP, dtype=bool)
    same = (docs[:, :, None] == docs[:, None, :]) & lower[None]
    masks = same[..., None]
    spread = cumul[:, :, None, :] - cumul[:, None, :, :]
    weights = jnp.where(masks, jnp.exp(jnp.where(masks, spread, 0.0)), 0.0)
    scores = jnp.einsum('rin,rjn->rij', out_map, in_map, precision=HIGHEST)
    mixing = scores[..., None] * weights * step_size[:, None, :, :]
    result = jnp.einsum('rijh,rjhp->rihp', mixing, values, precision=HIGHEST)
    entering = jnp.exp(cumul) * (docs == prior[:, None]).astype(jnp.float32)[..., None]
    result = result + jnp.einsum('rin,rhpn->rihp', out_map, carried, precision=HIGHEST) * entering[..., None]
    final_doc = docs[:, -1:]
    tail = jnp.exp(cumul[:, -1:, :] - cumul) * (docs == final_doc).astype(jnp.float32)[..., None] * step_size
    keeping = jnp.exp(cumul[:, -1, :]) * (final_doc == prior[:, None]).astype(jnp.float32)
    carried = keeping[:, :, None, None] * carried + jnp.einsum('rjh,rjhp,rjn->rhpn', tail, values, in_map, precision=HIGHEST)
    return (carried, result)

def state_space(values, in_map, out_map, step_size, log_rate, docs):
    count = LEN // GROUP

    def blocks(array):
        return jnp.moveaxis(array.reshape((ROWS, count, GROUP) + array.shape[2:]), 1, 0)
    priors = jnp.concatenate([jnp.full((ROWS, 1), -1, jnp.int32), docs[:, GROUP - 1::GROUP][:, :-1].astype(jnp.int32)], 1)
    start = jnp.zeros((ROWS, HEADS, HEAD_DIM, STATE), jnp.float32)
    inputs_all = (blocks(values), blocks(in_map), blocks(out_map), blocks(step_size), blocks(log_rate), blocks(docs), jnp.moveaxis(priors, 1, 0))
    _, outputs = lax.scan(jax.checkpoint(group_step), start, inputs_all)
    return jnp.moveaxis(outputs, 0, 1).reshape(ROWS, LEN, HEADS, HEAD_DIM)

def mixer_layer(hidden, docs, params, depth):
    norm_gain, in_weight, conv_weight, conv_bias, log_decay, dt_bias, skip, gate_gain, out_weight = params
    normed = low(norm_rows(hidden, norm_gain[depth]))
    projected = low_back(jnp.einsum('rld,dp->rlp', normed, in_weight[depth], precision=HIGHEST))
    gate_in = projected[..., :DI]
    mixed_in = projected[..., DI:DI + CC]
    rate_in = projected[..., DI + CC:]
    padded = jnp.pad(mixed_in, ((0, 0), (KW - 1, 0), (0, 0)))
    padded_docs = jnp.pad(docs, ((0, 0), (KW - 1, 0)), constant_values=-1)
    conv = jnp.zeros_like(mixed_in) + conv_bias[depth]
    for offset in range(KW):
        match = (padded_docs[:, offset:offset + LEN] == docs).astype(jnp.float32)[..., None]
        conv = conv + conv_weight[depth][:, offset] * padded[:, offset:offset + LEN] * match
    active = jax.nn.silu(conv)
    values = active[..., :DI].reshape(ROWS, LEN, HEADS, HEAD_DIM)
    in_map = active[..., DI:DI + STATE]
    out_map = active[..., DI + STATE:]
    step_size = jax.nn.softplus(rate_in + dt_bias[depth])
    log_rate = -jnp.exp(log_decay[depth]) * step_size
    result = state_space(values, in_map, out_map, step_size, log_rate, docs) + skip[depth][:, None] * values
    gated = result.reshape(ROWS, LEN, DI) * jax.nn.silu(gate_in)
    normed_out = low(norm_rows(gated, gate_gain[depth]))
    branch = low_back(jnp.einsum('rle,ed->rld', normed_out, out_weight[depth], precision=HIGHEST))
    return hidden + branch

def reference(inputs, lengths, norm_gain, in_weight, conv_weight, conv_bias, log_decay, dt_bias, skip, gate_gain, out_weight, cotangent):
    starts = (jnp.cumsum(lengths, -1) - lengths).astype(jnp.int32)
    places = jnp.arange(LEN, dtype=jnp.int32)
    docs = (lax.optimization_barrier(jnp.sum((starts[:, None, :] <= places[None, :, None]).astype(jnp.int32), -1)) - 1).astype(jnp.int32)
    params = (norm_gain, in_weight.astype(jnp.float32), conv_weight, conv_bias, log_decay, dt_bias, skip, gate_gain, out_weight.astype(jnp.float32))

    def forward(hidden, weights):
        for depth in range(LAYERS):
            hidden = mixer_layer(hidden, docs, weights, depth)
        return hidden
    output, pull = jax.vjp(forward, inputs, params)
    input_grad, grads = pull(cotangent)
    return (output, input_grad, grads[0], grads[1], grads[2], grads[3], grads[4], grads[5], grads[6], grads[7], grads[8])
```

```python
from functools import partial

import jax
import jax.numpy as jnp
from jax import lax
from jax.sharding import PartitionSpec as P

DI = 2048
STATE = 128
HEAD_DIM = 64
KW = 4
GROUP = 256
LAYERS = 2


EPS = 1e-05
HIGHEST = lax.Precision.HIGHEST


AXES = ("seq", "rows")


def scattered(total):
    return lax.psum_scatter(total, AXES, scatter_dimension=0, tiled=True)


def shifted(value, axis, steps):
    count = lax.axis_size(axis)
    leading, last = (max(0, -steps), min(count, count - steps))
    return lax.ppermute(value, axis, [(source, source + steps) for source in range(leading, last)])


def exchange(parts):
    return lax.all_to_all(parts, "seq", split_axis=0, concat_axis=0, tiled=True)


def entering_states(keep, state):
    peers = lax.axis_size("seq")
    row_count, heads = keep.shape
    share = heads // peers
    lead = jnp.moveaxis(state, 0, 1)
    tag = jnp.broadcast_to(jnp.moveaxis(keep, 0, 1)[..., None, None], lead.shape[:2] + (8, STATE))
    mine = exchange(jnp.concatenate([lead, tag], 2))
    mine = mine.reshape((peers, share, row_count, HEAD_DIM + 8, STATE))
    keeps = mine[:, :, :, HEAD_DIM, 0]
    carried = jnp.zeros(mine.shape[1:3] + (HEAD_DIM, STATE), jnp.float32)
    before = []
    for peer in range(peers):
        before.append(carried)
        carried = keeps[peer][..., None, None] * carried + mine[peer, :, :, :HEAD_DIM]
    back = exchange(jnp.stack(before).reshape(lead.shape))
    return jnp.moveaxis(back, 0, 1), keeps


def entering_grads(keeps, grad):
    peers, share, row_count = keeps.shape
    lead = jnp.moveaxis(grad, 0, 1)
    mine = exchange(lead).reshape((peers, share, row_count, HEAD_DIM, STATE))
    carried = jnp.zeros(mine.shape[1:], jnp.float32)
    after = [None] * peers
    for peer in reversed(range(peers)):
        after[peer] = carried
        carried = keeps[peer][..., None, None] * carried + mine[peer]
    back = exchange(jnp.stack(after).reshape(lead.shape))
    return jnp.moveaxis(back, 0, 1)


def norm_rows(values, gain):
    return values * lax.rsqrt(jnp.mean(values * values, -1, keepdims=True) + EPS) * gain


def doc_table(lengths, first, count):
    starts = jnp.cumsum(lengths, -1) - lengths
    places = first + jnp.arange(count, dtype=jnp.int32)
    return jnp.sum((starts[:, None, :] <= places[None, :, None]).astype(jnp.int32), -1) - 1


def local_scan(values, in_map, out_map, step_size, log_rate, docs, before_doc):
    row_count, span = docs.shape
    count = span // GROUP

    def blocks(array):
        return array.reshape((row_count, count, GROUP) + array.shape[2:])

    values_c = blocks(values)
    in_c = blocks(in_map)
    out_c = blocks(out_map)
    step_c = blocks(step_size)
    docs_c = blocks(docs)
    cumul = jnp.cumsum(blocks(log_rate), 2)
    prior = jnp.concatenate([before_doc[:, None], docs_c[:, :-1, -1]], 1)
    lower = jnp.tri(GROUP, dtype=bool)
    same = (docs_c[:, :, :, None] == docs_c[:, :, None, :]) & lower
    masks = same[..., None]
    spread = cumul[:, :, :, None, :] - cumul[:, :, None, :, :]
    weights = jnp.where(masks, jnp.exp(jnp.where(masks, spread, 0.0)), 0.0)
    scores = jnp.einsum("rcin,rcjn->rcij", out_c, in_c, precision=HIGHEST)
    mixing = scores[..., None] * weights * step_c[:, :, None, :, :]
    inner = jnp.einsum("rcijh,rcjhp->rcihp", mixing, values_c, precision=HIGHEST)
    final_doc = docs_c[:, :, -1:]
    tail = (
        jnp.exp(cumul[:, :, -1:, :] - cumul)
        * (docs_c == final_doc).astype(jnp.float32)[..., None]
        * step_c
    )
    made = jnp.einsum("rcjh,rcjhp,rcjn->rchpn", tail, values_c, in_c, precision=HIGHEST)
    keeping = (
        jnp.exp(cumul[:, :, -1, :]) * (final_doc[:, :, 0] == prior).astype(jnp.float32)[..., None]
    )
    entering = jnp.exp(cumul) * (docs_c == prior[:, :, None]).astype(jnp.float32)[..., None]
    carried = jnp.zeros(made.shape[:1] + made.shape[2:], jnp.float32)
    through = jnp.ones(keeping.shape[:1] + keeping.shape[2:], jnp.float32)
    carried_list = []
    through_list = []
    for block_index in range(count):
        carried_list.append(carried)
        through_list.append(through)
        carried = keeping[:, block_index, :, None, None] * carried + made[:, block_index]
        through = through * keeping[:, block_index]
    before_blocks = jnp.stack(carried_list, 1)
    through_blocks = jnp.stack(through_list, 1)
    outer = (
        jnp.einsum("rcin,rchpn->rcihp", out_c, before_blocks, precision=HIGHEST)
        * entering[..., None]
    )
    scanned = (inner + outer).reshape(values.shape)
    entering_all = (entering * through_blocks[:, :, None, :]).reshape(step_size.shape)
    return (scanned, carried, through, entering_all)


def mixer_local(docs_ext, extended, conv_weight, conv_bias, rate_in, dt_bias, log_decay):
    row_count, span = (rate_in.shape[0], rate_in.shape[1])
    docs = docs_ext[:, KW - 1 :]
    conv = jnp.zeros((row_count, span, conv_bias.shape[0]), jnp.float32) + conv_bias
    for offset in range(KW):
        match = (docs_ext[:, offset : offset + span] == docs).astype(jnp.float32)[..., None]
        conv = conv + conv_weight[:, offset] * extended[:, offset : offset + span] * match
    active = jax.nn.silu(conv)
    values = active[..., :DI].reshape(row_count, span, DI // HEAD_DIM, HEAD_DIM)
    in_map = active[..., DI : DI + STATE]
    out_map = active[..., DI + STATE :]
    step_size = jax.nn.softplus(rate_in + dt_bias)
    log_rate = -jnp.exp(log_decay) * step_size
    scanned, final_state, total_keep, entering = local_scan(
        values, in_map, out_map, step_size, log_rate, docs, docs_ext[:, KW - 2]
    )
    return (values, out_map, scanned, final_state, total_keep, entering)


def finish(values, out_map, scanned, entering, state_in, gate_in, skip, gate_gain):
    carried_part = (
        jnp.einsum("rtn,rhpn->rthp", out_map, state_in, precision=HIGHEST) * entering[..., None]
    )
    result = scanned + carried_part + skip[:, None] * values
    gated = result.reshape(gate_in.shape) * jax.nn.silu(gate_in)
    return norm_rows(gated, gate_gain)


def local(
    inputs,
    lengths,
    norm_gain,
    in_weight,
    conv_weight,
    conv_bias,
    log_decay,
    dt_bias,
    skip,
    gate_gain,
    out_weight,
    cotangent,
):
    row_count, span, width = inputs.shape
    position = lax.axis_index("seq")
    docs_ext = doc_table(lengths, position * span - (KW - 1), span + KW - 1)
    channels = DI + 2 * STATE
    hidden = inputs
    saved = []
    for depth in range(LAYERS):
        normed, norm_pull = jax.vjp(norm_rows, hidden, norm_gain[depth])
        normed_low = normed.astype(jnp.bfloat16).reshape(row_count * span, width)
        projected = jnp.dot(
            normed_low, in_weight[depth], preferred_element_type=jnp.float32
        ).reshape(row_count, span, -1)
        gate_in = projected[..., :DI]
        mixed_in = projected[..., DI : DI + channels]
        rate_in = projected[..., DI + channels :]
        before = shifted(mixed_in[:, span - (KW - 1) :], "seq", 1)
        extended = jnp.concatenate([before, mixed_in], 1)
        mixer_out, mixer_pull = jax.vjp(
            partial(mixer_local, docs_ext),
            extended,
            conv_weight[depth],
            conv_bias[depth],
            rate_in,
            dt_bias[depth],
            log_decay[depth],
        )
        values, out_map, scanned, final_state, total_keep, entering = mixer_out
        state_in, keeps = entering_states(total_keep, final_state)
        normed_out, finish_pull = jax.vjp(
            finish,
            values,
            out_map,
            scanned,
            entering,
            state_in,
            gate_in,
            skip[depth],
            gate_gain[depth],
        )
        out_low = normed_out.astype(jnp.bfloat16).reshape(row_count * span, DI)
        branch = jnp.dot(out_low, out_weight[depth], preferred_element_type=jnp.float32).reshape(
            row_count, span, width
        )
        saved.append(
            (
                norm_pull,
                normed_low,
                mixer_pull,
                keeps,
                state_in,
                finish_pull,
                out_low,
            )
        )
        hidden = hidden + branch
    gradient = cotangent
    collected = [None] * LAYERS
    big_in = [None] * LAYERS
    big_out = [None] * LAYERS
    for depth in reversed(range(LAYERS)):
        norm_pull, normed_low, mixer_pull, keeps, state_in, finish_pull, out_low = (
            saved[depth]
        )
        grad_low = gradient.astype(jnp.bfloat16).reshape(row_count * span, width)
        out_weight_grad = jnp.einsum(
            "te,td->ed", out_low, grad_low, preferred_element_type=jnp.float32
        )
        grad_normed = jnp.einsum(
            "td,ed->te", grad_low, out_weight[depth], preferred_element_type=jnp.float32
        ).reshape(row_count, span, DI)
        (
            grad_values,
            grad_map,
            grad_scanned,
            grad_entering,
            grad_state,
            grad_gate,
            grad_skip,
            grad_gain,
        ) = finish_pull(grad_normed)
        grad_final = entering_grads(keeps, grad_state)
        grad_total = jnp.sum(grad_final * state_in, axis=(2, 3))
        grad_ext, grad_conv_w, grad_conv_b, grad_rate, grad_bias, grad_decay = mixer_pull(
            (grad_values, grad_map, grad_scanned, grad_final, grad_total, grad_entering)
        )
        returned = shifted(grad_ext[:, : KW - 1], "seq", -1)
        grad_mixed = grad_ext[:, KW - 1 :] + jnp.pad(
            returned, ((0, 0), (span - (KW - 1), 0), (0, 0))
        )
        grad_proj = (
            jnp.concatenate([grad_gate, grad_mixed, grad_rate], -1)
            .astype(jnp.bfloat16)
            .reshape(row_count * span, -1)
        )
        in_weight_grad = jnp.einsum(
            "td,tp->dp", normed_low, grad_proj, preferred_element_type=jnp.float32
        )
        grad_normed_in = jnp.einsum(
            "tp,dp->td", grad_proj, in_weight[depth], preferred_element_type=jnp.float32
        ).reshape(row_count, span, width)
        grad_hidden, grad_norm_gain = norm_pull(grad_normed_in)
        gradient = gradient + grad_hidden
        sums = (grad_norm_gain, grad_conv_w, grad_conv_b, grad_gain, grad_decay, grad_bias, grad_skip)
        collected[depth] = sums
        big_in[depth] = scattered(in_weight_grad)
        big_out[depth] = scattered(out_weight_grad)
    flat = jnp.concatenate([part.reshape(-1) for sums in collected for part in sums])
    flat = lax.psum(flat, AXES)
    index = position * lax.axis_size("rows") + lax.axis_index("rows")
    small = []
    at = 0
    for sums in collected:
        row = []
        for member, part in enumerate(sums):
            total = flat[at : at + part.size].reshape(part.shape)
            at += part.size
            if member < 4:
                size = part.shape[0] // lax.axis_size(AXES)
                total = lax.dynamic_slice_in_dim(total, index * size, size)
            row.append(total)
        small.append(row)
    stacked = [jnp.stack([small[level][member] for level in range(LAYERS)]) for member in range(7)]
    norm_gain_grad, conv_w_grad, conv_b_grad, gain_grad, decay_grad, bias_grad, skip_grad = stacked
    return (
        hidden,
        gradient,
        norm_gain_grad,
        jnp.stack(big_in),
        conv_w_grad,
        conv_b_grad,
        decay_grad,
        bias_grad,
        skip_grad,
        gain_grad,
        jnp.stack(big_out),
    )


def solution(mesh):
    in_specs = (
        P("rows", "seq", None),
        P("rows", None),
        P(),
        P(),
        P(),
        P(),
        P(),
        P(),
        P(),
        P(),
        P(),
        P("rows", "seq", None),
    )
    out_specs = (
        P("rows", "seq", None),
        P("rows", "seq", None),
        P(None, ("seq", "rows")),
        P(None, ("seq", "rows"), None),
        P(None, ("seq", "rows"), None),
        P(None, ("seq", "rows")),
        P(),
        P(),
        P(),
        P(None, ("seq", "rows")),
        P(None, ("seq", "rows"), None),
    )
    return jax.shard_map(local, mesh=mesh, in_specs=in_specs, out_specs=out_specs, check_vma=False)
```

```python
from functools import partial

import jax
import jax.numpy as jnp
from jax import lax
from jax.experimental import pallas as pl
from jax.experimental.pallas import tpu as pltpu
from jax.sharding import PartitionSpec as P

DI = 2048
STATE = 128
HEAD_DIM = 64
HEADS = DI // HEAD_DIM
KW = 4
GROUP = 256
LAYERS = 2
CHANNELS = DI + 2 * STATE
TILE = 256
HALO = 8
ROWS_AT = 64
VMEM_BYTES = 48 * 1024 * 1024

EPS = 1e-05
HIGHEST = lax.Precision.HIGHEST
AXES = ("seq", "rows")


def pcall(body, grid, in_specs, out_specs, out_shape, scratch, args, flops=0, nbytes=0):
    return pl.pallas_call(
        body,
        grid=grid,
        in_specs=in_specs,
        out_specs=out_specs,
        out_shape=out_shape,
        scratch_shapes=scratch,
        compiler_params=pltpu.CompilerParams(vmem_limit_bytes=VMEM_BYTES),
        cost_estimate=pl.CostEstimate(flops=flops, bytes_accessed=nbytes, transcendentals=0),
    )(*args)


def dot(a, b, dims=(((1,), (0,)), ((), ()))):
    return lax.dot_general(
        a.astype(jnp.bfloat16), b.astype(jnp.bfloat16), dims, preferred_element_type=jnp.float32
    )


def dot_nt(a, b):
    return dot(a, b, (((1,), (1,)), ((), ())))


def dot_exact(a, b):
    return jnp.dot(a, b, precision=HIGHEST, preferred_element_type=jnp.float32)


def sigmoid(v):
    return 1.0 / (1.0 + jnp.exp(-v))


def lane_iota(shape):
    return lax.broadcasted_iota(jnp.int32, shape, 1)


def low_half(rows):
    return lane_iota((rows, 128)) < HEAD_DIM


def to_heads(cols, first, pairs):
    rows = cols.shape[0]
    low = low_half(rows)
    parts = []
    for pair in range(pairs):
        at = first + 2 * pair
        parts.append(
            jnp.where(
                low,
                jnp.broadcast_to(cols[:, at : at + 1], (rows, 128)),
                jnp.broadcast_to(cols[:, at + 1 : at + 2], (rows, 128)),
            )
        )
    return jnp.concatenate(parts, 1) if pairs > 1 else parts[0]


def group_lanes(cols, group):
    return pltpu.roll(cols, (128 - 4 * group) % 128, 1)


def head_sums(group):
    channel = lax.broadcasted_iota(jnp.int32, (TILE, 128), 0)
    return (channel // HEAD_DIM + 4 * group == lane_iota((TILE, 128))).astype(jnp.float32)


def conv_rows(x_ref, w_ref, aux_ref, first, count):
    total = jnp.broadcast_to(w_ref[4:5, :], (count, w_ref.shape[1]))
    for tap in range(KW - 1):
        match = aux_ref[first : first + count, tap : tap + 1]
        total = total + w_ref[tap : tap + 1, :] * x_ref[first + 5 + tap : first + 5 + tap + count, :] * match
    return total + w_ref[3:4, :] * x_ref[first + 8 : first + 8 + count, :]


def states_kernel(
    x_ref, xbc_ref, rate_ref, aux_ref, w_ref, wbc_ref, hp_ref,
    v_ref, bc_ref, col_ref, cumr_ref, made_ref, kx_ref, pay_ref,
    bt_ref,
):
    group = pl.program_id(0)
    span = rate_ref.shape[0]
    count = span // GROUP

    @pl.when(group == 0)
    def _():
        for first in range(0, span, ROWS_AT):
            conv = conv_rows(xbc_ref, wbc_ref, aux_ref, first, ROWS_AT)
            bc_ref[first : first + ROWS_AT, :] = conv * sigmoid(conv)
        tri = (
            lax.broadcasted_iota(jnp.int32, (GROUP, GROUP), 0) >= lane_iota((GROUP, GROUP))
        ).astype(jnp.float32)
        for block in range(count):
            rows = slice(block * GROUP, (block + 1) * GROUP)
            bt_ref[block] = bc_ref[rows, :STATE].T.astype(jnp.bfloat16)
            raw = rate_ref[rows, :] + hp_ref[0:1, :]
            step = jnp.maximum(raw, 0.0) + jnp.log1p(jnp.exp(-jnp.abs(raw)))
            cum = dot_exact(tri, hp_ref[1:2, :] * step)
            last = cum[GROUP - 1 :, :]
            col_ref[0, rows, :] = cum
            col_ref[1, rows, :] = step
            col_ref[2, rows, :] = jnp.exp(cum) * aux_ref[rows, 3:4]
            col_ref[3, rows, :] = jnp.exp(last - cum) * aux_ref[rows, 4:5]
            cumr_ref[:, rows] = cum.T

    for first in range(0, span, ROWS_AT):
        conv = conv_rows(x_ref, w_ref, aux_ref, first, ROWS_AT)
        v_ref[first : first + ROWS_AT, :] = conv * sigmoid(conv)
    made = []
    keep = []
    for block in range(count):
        rows = slice(block * GROUP, (block + 1) * GROUP)
        weight = to_heads(group_lanes(col_ref[3, rows, :] * col_ref[1, rows, :], group), 0, 2)
        made.append(dot(bt_ref[block], weight * v_ref[rows, :]))
        ends = group_lanes(col_ref[2, (block + 1) * GROUP - 8 : (block + 1) * GROUP, :], group)
        keep.append(to_heads(ends, 0, 2)[7:8, :])
    made_ref[...] = made[0]
    kx_ref[...] = jnp.concatenate([keep[0], keep[1], jnp.zeros((6, TILE), jnp.float32)], 0)
    final = keep[1] * made[0] + made[1]
    total = jnp.broadcast_to(keep[0] * keep[1], (8, TILE))
    chunks = pay_ref.shape[0] // 2
    size = STATE // chunks
    for pair in range(2):
        lanes = slice(pair * 128, (pair + 1) * 128)
        for chunk in range(chunks):
            pay_ref[pair * chunks + chunk, :size, :] = final[chunk * size : (chunk + 1) * size, lanes]
            pay_ref[pair * chunks + chunk, size:, :] = total[:, lanes]


def inner_kernel(bc_ref, v_ref, col_ref, cumr_ref, aux_ref, auxr_ref, y_ref, g_ref):
    group = pl.program_id(1)

    @pl.when(group == 0)
    def _():
        scores = dot_nt(bc_ref[:, STATE:], bc_ref[:, :STATE])
        allowed = (aux_ref[:, 5:6] == auxr_ref[0:1, :]) & (
            lax.broadcasted_iota(jnp.int32, (GROUP, GROUP), 0) >= lane_iota((GROUP, GROUP))
        )
        g_ref[...] = jnp.where(allowed, scores, 0.0)

    cum = group_lanes(col_ref[0], group)
    step = group_lanes(col_ref[1], group)
    low = low_half(GROUP)
    for pair in range(2):
        lanes = slice(pair * 128, (pair + 1) * 128)
        scaled = to_heads(step, 2 * pair, 1) * v_ref[:, lanes]
        result = None
        for half in range(2):
            head = 2 * pair + half
            row = cumr_ref[pl.ds(4 * group + head, 1), :]
            parts = []
            for first in range(0, GROUP, 64):
                spread = cum[first : first + 64, head : head + 1] - row
                decay = jnp.exp(jnp.minimum(spread, 0.0))
                parts.append((g_ref[first : first + 64, :] * decay).astype(jnp.bfloat16))
            mixing = jnp.concatenate(parts, 0)
            picked = jnp.where(low if half == 0 else ~low, scaled, 0.0)
            part = dot(mixing, picked)
            result = part if result is None else result + part
        y_ref[:, lanes] = result


def finish_kernel(
    yi_ref, v_ref, gate_ref, bc_ref, col_ref, sin_ref, made_ref, kx_ref, ch_ref,
    y_ref, out_ref,
    gated_ref,
):
    block = pl.program_id(0)
    out_map = bc_ref[:, STATE:].astype(jnp.bfloat16)
    total = jnp.zeros((GROUP, 128), jnp.float32)
    pairs = v_ref.shape[1] // 128
    for pair in range(pairs):
        lanes = slice(pair * 128, (pair + 1) * 128)
        state = sin_ref[pair]
        state = jnp.where(block == 0, state, kx_ref[0:1, lanes] * state + made_ref[:, lanes])
        outer = to_heads(col_ref[2], 2 * pair, 1) * dot(out_map, state)
        result = yi_ref[:, lanes] + outer + ch_ref[0:1, lanes] * v_ref[:, lanes]
        y_ref[:, lanes] = result
        gate = gate_ref[:, lanes]
        gated = result * gate * sigmoid(gate)
        gated_ref[:, lanes] = gated
        total = total + gated * gated
    scale = lax.rsqrt(jnp.sum(total, 1, keepdims=True) / (pairs * 128) + EPS)
    for pair in range(pairs):
        lanes = slice(pair * 128, (pair + 1) * 128)
        out_ref[:, lanes] = (gated_ref[:, lanes] * scale * ch_ref[1:2, lanes]).astype(jnp.bfloat16)


def gate_back_kernel(
    dno_ref, y_ref, gate_ref, v_ref, bc_ref, col_ref, kx_ref, ch_ref,
    dy_ref, dgate_ref, sum_ref, d1_ref, pay_ref,
    gated_ref,
):
    block = pl.program_id(0)
    pairs = v_ref.shape[1] // 128
    square = jnp.zeros((GROUP, 128), jnp.float32)
    cross = jnp.zeros((GROUP, 128), jnp.float32)
    for pair in range(pairs):
        lanes = slice(pair * 128, (pair + 1) * 128)
        gate = gate_ref[:, lanes]
        gated = y_ref[:, lanes] * gate * sigmoid(gate)
        gated_ref[:, lanes] = gated
        square = square + gated * gated
        cross = cross + gated * dno_ref[:, lanes] * ch_ref[1:2, lanes]
    width = pairs * 128
    scale = lax.rsqrt(jnp.sum(square, 1, keepdims=True) / width + EPS)
    pull = scale * scale * scale * (jnp.sum(cross, 1, keepdims=True) / width)
    out_t = bc_ref[:, STATE:].T.astype(jnp.bfloat16)
    chunks = pay_ref.shape[0] // pairs
    size = STATE // chunks
    for pair in range(pairs):
        lanes = slice(pair * 128, (pair + 1) * 128)
        gate = gate_ref[:, lanes]
        gated = gated_ref[:, lanes]
        dno = dno_ref[:, lanes]
        sig = sigmoid(gate)
        dgated = scale * dno * ch_ref[1:2, lanes] - gated * pull
        dy = dgated * gate * sig
        dy_ref[:, lanes] = dy
        dgate_ref[:, lanes] = (dgated * y_ref[:, lanes] * sig * (1.0 + gate * (1.0 - sig))).astype(
            jnp.bfloat16
        )
        sums = jnp.concatenate(
            [
                jnp.sum(dno * gated * scale, 0, keepdims=True),
                jnp.sum(dy * v_ref[:, lanes], 0, keepdims=True),
                jnp.zeros((6, 128), jnp.float32),
            ],
            0,
        )
        fresh = dot(out_t, to_heads(col_ref[2], 2 * pair, 1) * dy)
        d1_ref[:, lanes] = fresh

        @pl.when(block == 0)
        def _():
            sum_ref[:, lanes] = sums
            for chunk in range(chunks):
                pay_ref[pair * chunks + chunk] = fresh[chunk * size : (chunk + 1) * size]

        @pl.when(block > 0)
        def _():
            sum_ref[:, lanes] += sums
            more = kx_ref[0:1, lanes] * fresh
            for chunk in range(chunks):
                pay_ref[pair * chunks + chunk] += more[chunk * size : (chunk + 1) * size]


def inner_back_kernel(
    bc_ref, v_ref, dy_ref, col_ref, cumr_ref, aux_ref, auxr_ref,
    x_ref, dbc_ref, dcum_ref,
    g_ref, dg_ref, cols_ref, rows_ref,
):
    group = pl.program_id(1)
    groups = pl.num_programs(1)

    def allowed():
        return (aux_ref[:, 5:6] == auxr_ref[0:1, :]) & (
            lax.broadcasted_iota(jnp.int32, (GROUP, GROUP), 0) <= lane_iota((GROUP, GROUP))
        )

    @pl.when(group == 0)
    def _():
        scores = dot_nt(bc_ref[:, :STATE], bc_ref[:, STATE:])
        g_ref[...] = jnp.where(allowed(), scores, 0.0)
        dg_ref[...] = jnp.zeros_like(dg_ref)
        cols_ref[...] = jnp.zeros_like(cols_ref)
        rows_ref[...] = jnp.zeros_like(rows_ref)

    cum = group_lanes(col_ref[0], group)
    step = group_lanes(col_ref[1], group)
    low = low_half(GROUP)
    lane = lane_iota((GROUP, 128))
    for pair in range(2):
        lanes = slice(pair * 128, (pair + 1) * 128)
        scaled = to_heads(step, 2 * pair, 1) * v_ref[:, lanes]
        dy = dy_ref[:, lanes]
        dy_low = dy.astype(jnp.bfloat16)
        result = None
        for half in range(2):
            head = 2 * pair + half
            row = cumr_ref[pl.ds(4 * group + head, 1), :]
            mine = low if half == 0 else ~low
            picked = jnp.where(mine, scaled, 0.0).astype(jnp.bfloat16)
            products = dot_nt(picked, dy_low)
            parts = []
            row_sum = jnp.zeros((8, GROUP), jnp.float32)
            col_sums = []
            for first in range(0, GROUP, 64):
                rows = slice(first, first + 64)
                spread = row - cum[rows, head : head + 1]
                decay = jnp.exp(jnp.minimum(spread, 0.0))
                scores = g_ref[rows, :]
                parts.append((scores * decay).astype(jnp.bfloat16))
                part = products[rows, :] * decay
                dg_ref[rows, :] += part
                both = part * scores
                row_sum = row_sum + jnp.sum(both.reshape(8, 8, GROUP), 0)
                col_sums.append(jnp.sum(both, 1, keepdims=True))
            mixing = jnp.concatenate(parts, 0)
            part = dot(mixing, jnp.where(mine, dy, 0.0))
            result = part if result is None else result + part
            rows_ref[pl.ds(4 * group + head, 1), :] = jnp.sum(row_sum, 0, keepdims=True)
            col_sum = jnp.concatenate(col_sums, 0)
            cols_ref[...] += jnp.where(lane == 4 * group + head, col_sum, 0.0)
        x_ref[:, lanes] = result

    @pl.when(group == groups - 1)
    def _():
        dg = jnp.where(allowed(), dg_ref[...], 0.0)
        dbc_ref[:, :STATE] = dot(dg, bc_ref[:, STATE:])
        dbc_ref[:, STATE:] = dot(dg.T, bc_ref[:, :STATE])
        dcum_ref[...] = rows_ref[...].T - cols_ref[...]


def states_back_kernel(
    xi_ref, v_ref, dy_ref, x_ref, xbc_ref, bc_ref, col_ref, dso_ref, sin_ref, made_ref, d1_ref,
    kx_ref, dbc_ref, dcum_ref, aux_ref, w_ref, wbc_ref, ch_ref, hp_ref, rate_ref,
    dconv_ref, dconv_bc_ref, drate_ref, sum_ref,
    ds_ref, dc_ref, z_ref, kd_ref, dmap_ref,
):
    group = pl.program_id(0)
    groups = pl.num_programs(0)
    span = v_ref.shape[0]
    count = span // GROUP

    @pl.when(group == 0)
    def _():
        ds_ref[...] = jnp.zeros_like(ds_ref)
        dc_ref[...] = dcum_ref[...]
        z_ref[...] = jnp.zeros_like(z_ref)
        kd_ref[...] = jnp.zeros_like(kd_ref)
        dmap_ref[...] = dbc_ref[...]

    sums = head_sums(group)
    end_grad = jnp.concatenate([dso_ref[0], dso_ref[1]], 1)
    state = jnp.concatenate([sin_ref[0], sin_ref[1]], 1)
    ends = [d1_ref[...] + kx_ref[1:2, :] * end_grad, end_grad]
    starts = [state, kx_ref[0:1, :] * state + made_ref[...]]
    for block in range(count):
        rows = slice(block * GROUP, (block + 1) * GROUP)
        step = to_heads(group_lanes(col_ref[1, rows, :], group), 0, 2)
        entering = to_heads(group_lanes(col_ref[2, rows, :], group), 0, 2)
        tail = to_heads(group_lanes(col_ref[3, rows, :], group), 0, 2)
        values = v_ref[rows, :]
        dy = dy_ref[rows, :]
        from_end = tail * dot(bc_ref[rows, :STATE], ends[block])
        outer = entering * dot(bc_ref[rows, STATE:], starts[block])
        pulled = xi_ref[rows, :] + from_end
        ds_ref[rows, :] += dot(values * pulled, sums)
        z_ref[rows, :] += dot(step * values * from_end, sums)
        dc_ref[rows, :] += dot(dy * outer, sums)
        dmap_ref[rows, :STATE] += dot_nt(tail * step * values, ends[block])
        dmap_ref[rows, STATE:] += dot_nt(entering * dy, starts[block])
        kept = kx_ref[block : block + 1, :] * jnp.sum(ends[block] * starts[block], 0, keepdims=True)
        kd_ref[block] += dot_exact(jnp.broadcast_to(kept, (8, TILE)), sums)
        grad = step * pulled + ch_ref[0:1, :] * dy
        conv = conv_rows(x_ref, w_ref, aux_ref, block * GROUP, GROUP)
        sig = sigmoid(conv)
        dconv_ref[rows, :] = grad * sig * (1.0 + conv * (1.0 - sig))

    @pl.when(group == groups - 1)
    def _():
        after = (
            lax.broadcasted_iota(jnp.int32, (GROUP, GROUP), 0) <= lane_iota((GROUP, GROUP))
        ).astype(jnp.float32)
        before = (
            lax.broadcasted_iota(jnp.int32, (GROUP, GROUP), 0) > lane_iota((GROUP, GROUP))
        ).astype(jnp.float32)
        bias_sum = jnp.zeros((1, 128), jnp.float32)
        decay_sum = jnp.zeros((1, 128), jnp.float32)
        for block in range(count):
            rows = slice(block * GROUP, (block + 1) * GROUP)
            conv = conv_rows(xbc_ref, wbc_ref, aux_ref, block * GROUP, GROUP)
            sig = sigmoid(conv)
            dconv_bc_ref[rows, :] = dmap_ref[rows, :] * sig * (1.0 + conv * (1.0 - sig))
            z = z_ref[rows, :]
            da = dot_exact(after, dc_ref[rows, :]) + kd_ref[block, 0:1, :]
            da = da + dot_exact(before, z)
            ds = ds_ref[rows, :] + hp_ref[1:2, :] * da
            drate = ds * sigmoid(rate_ref[rows, :] + hp_ref[0:1, :])
            drate_ref[rows, :] = drate.astype(jnp.bfloat16)
            bias_sum = bias_sum + jnp.sum(drate, 0, keepdims=True)
            decay_sum = decay_sum + jnp.sum(da * hp_ref[1:2, :] * col_ref[1, rows, :], 0, keepdims=True)
        sum_ref[...] = jnp.concatenate([bias_sum, decay_sum, jnp.zeros((6, 128), jnp.float32)], 0)


def conv_back_kernel(dconv_ref, dconv_bc_ref, next_ref, x_ref, aux_ref, w_ref, dx_ref, sum_ref, ext_ref):
    tile = pl.program_id(0)
    span = dconv_ref.shape[0]

    @pl.when(tile < pl.num_programs(0) - 1)
    def _():
        ext_ref[:span, :] = dconv_ref[...]

    @pl.when(tile == pl.num_programs(0) - 1)
    def _():
        ext_ref[:span, :] = dconv_bc_ref[...]

    ext_ref[span:, :] = next_ref[...]
    sums = [jnp.zeros((1, TILE), jnp.float32) for _ in range(KW + 1)]
    for first in range(0, span, ROWS_AT):
        here = ext_ref[first : first + ROWS_AT, :]
        grad = w_ref[3:4, :] * here
        for ahead in range(1, KW):
            match = aux_ref[first : first + ROWS_AT, 5 + ahead : 6 + ahead]
            grad = grad + w_ref[3 - ahead : 4 - ahead, :] * ext_ref[first + ahead : first + ahead + ROWS_AT, :] * match
        dx_ref[first : first + ROWS_AT, :] = grad.astype(jnp.bfloat16)
        for tap in range(KW):
            term = here * x_ref[first + 5 + tap : first + 5 + tap + ROWS_AT, :]
            if tap < KW - 1:
                term = term * aux_ref[first : first + ROWS_AT, tap : tap + 1]
            sums[tap] = sums[tap] + jnp.sum(term, 0, keepdims=True)
        sums[KW] = sums[KW] + jnp.sum(here, 0, keepdims=True)
    sum_ref[...] = jnp.concatenate(sums + [jnp.zeros((3, TILE), jnp.float32)], 0)


def scan_kernel(reverse, rows, in_ref, keep_ref, out_ref):
    peers = out_ref.shape[0]
    carried = jnp.zeros((rows, 128), jnp.float32)
    for at in range(peers):
        peer = peers - 1 - at if reverse else at
        out_ref[peer] = carried
        carried = keep_ref[peer, 0:1, :] * carried + in_ref[peer, :rows, :]


def full(shape):
    return pl.BlockSpec(shape, lambda *at: (0,) * len(shape))


def shape_of(dims, dtype=jnp.float32):
    return jax.ShapeDtypeStruct(dims, dtype)


def vmem(dims, dtype=jnp.float32):
    return pltpu.VMEM(dims, dtype)


def make_states(peers, mixed_ext, rate, aux, conv, hp):
    span = rate.shape[0]
    groups = DI // TILE
    chunks = peers * 128 // DI
    tile = lambda rows: pl.BlockSpec((rows, TILE), lambda g: (0, g))
    maps = lambda rows: pl.BlockSpec((rows, TILE), lambda g: (0, groups))
    pay = (2 * chunks, STATE // chunks + 8, 128)
    return pcall(
        states_kernel,
        (groups,),
        [tile(span + HALO), maps(span + HALO), full((span, 128)), full((span, 128)), tile(8), maps(8), full((8, 128))],
        [
            tile(span),
            full((span, TILE)),
            full((4, span, 128)),
            full((128, span)),
            tile(STATE),
            tile(8),
            pl.BlockSpec(pay, lambda g: (g, 0, 0)),
        ],
        [
            shape_of((span, DI)),
            shape_of((span, TILE)),
            shape_of((4, span, 128)),
            shape_of((128, span)),
            shape_of((STATE, DI)),
            shape_of((8, DI)),
            shape_of((peers,) + pay[1:]),
        ],
        [vmem((span // GROUP, STATE, GROUP), jnp.bfloat16)],
        (mixed_ext, mixed_ext, rate, aux, conv, conv, hp),
        flops=2 * span * DI * STATE,
        nbytes=12 * span * DI,
    )


def block_specs(span):
    blocks = span // GROUP
    tile = pl.BlockSpec((GROUP, TILE), lambda b, g: (b, g))
    maps = pl.BlockSpec((GROUP, TILE), lambda b, g: (b, 0))
    col = pl.BlockSpec((4, GROUP, 128), lambda b, g: (0, b, 0))
    row = pl.BlockSpec((128, GROUP), lambda b, g: (0, b))
    aux = pl.BlockSpec((GROUP, 128), lambda b, g: (b, 0))
    auxr = pl.BlockSpec((8, GROUP), lambda b, g: (0, b))
    return (blocks, DI // TILE), tile, maps, col, row, aux, auxr


def inner(bc, values, col, cumr, aux, auxr):
    span = values.shape[0]
    grid, tile, maps, cols, row, auxs, auxrs = block_specs(span)
    return pcall(
        inner_kernel,
        grid,
        [maps, tile, cols, row, auxs, auxrs],
        tile,
        shape_of((span, DI)),
        [vmem((GROUP, GROUP))],
        (bc, values, col, cumr, aux, auxr),
        flops=2 * span * GROUP * DI * 4,
        nbytes=8 * span * DI,
    )


def finish(yi, values, gate, bc, col, state_in, made, kx, ch):
    span = values.shape[0]
    wide = pl.BlockSpec((GROUP, DI), lambda b: (b, 0))
    maps = pl.BlockSpec((GROUP, TILE), lambda b: (b, 0))
    cols = pl.BlockSpec((4, GROUP, 128), lambda b: (0, b, 0))
    return pcall(
        finish_kernel,
        (span // GROUP,),
        [wide, wide, wide, maps, cols, full((DI // 128, STATE, 128)), full((STATE, DI)), full((8, DI)), full((8, DI))],
        [wide, wide],
        [shape_of((span, DI)), shape_of((span, DI), jnp.bfloat16)],
        [vmem((GROUP, DI))],
        (yi, values, gate, bc, col, state_in, made, kx, ch),
        flops=2 * span * DI * STATE,
        nbytes=18 * span * DI,
    )


def gate_back(peers, dno, y, gate, values, bc, col, kx, ch):
    span = values.shape[0]
    chunks = peers * 128 // DI
    wide = pl.BlockSpec((GROUP, DI), lambda b: (b, 0))
    maps = pl.BlockSpec((GROUP, TILE), lambda b: (b, 0))
    cols = pl.BlockSpec((4, GROUP, 128), lambda b: (0, b, 0))
    pay = (peers, STATE // chunks, 128)
    return pcall(
        gate_back_kernel,
        (span // GROUP,),
        [wide, wide, wide, wide, maps, cols, full((8, DI)), full((8, DI))],
        [wide, wide, full((8, DI)), full((STATE, DI)), full(pay)],
        [
            shape_of((span, DI)),
            shape_of((span, DI), jnp.bfloat16),
            shape_of((8, DI)),
            shape_of((STATE, DI)),
            shape_of(pay),
        ],
        [vmem((GROUP, DI))],
        (dno, y, gate, values, bc, col, kx, ch),
        flops=2 * span * DI * STATE,
        nbytes=22 * span * DI,
    )


def inner_back(bc, values, dy, col, cumr, aux, auxr):
    span = values.shape[0]
    grid, tile, maps, cols, row, auxs, auxrs = block_specs(span)
    return pcall(
        inner_back_kernel,
        grid,
        [maps, tile, tile, cols, row, auxs, auxrs],
        [tile, maps, auxs],
        [shape_of((span, DI)), shape_of((span, TILE)), shape_of((span, 128))],
        [vmem((GROUP, GROUP)), vmem((GROUP, GROUP)), vmem((GROUP, 128)), vmem((128, GROUP))],
        (bc, values, dy, col, cumr, aux, auxr),
        flops=2 * span * GROUP * DI * 8,
        nbytes=12 * span * DI,
    )


def states_back(xi, values, dy, mixed_ext, bc, col, dso, state_in, made, d1, kx, dbc, dcum, aux, conv, ch, hp, rate):
    span = values.shape[0]
    groups = DI // TILE
    tile = lambda rows: pl.BlockSpec((rows, TILE), lambda g: (0, g))
    maps = lambda rows: pl.BlockSpec((rows, TILE), lambda g: (0, groups))
    state = pl.BlockSpec((2, STATE, 128), lambda g: (g, 0, 0))
    small = full((span, 128))
    return pcall(
        states_back_kernel,
        (groups,),
        [
            tile(span), tile(span), tile(span), tile(span + HALO), maps(span + HALO), full((span, TILE)),
            full((4, span, 128)), state, state, tile(STATE), tile(STATE), tile(8), full((span, TILE)), small,
            small, tile(8), maps(8), tile(8), full((8, 128)), small,
        ],
        [tile(span), full((span, TILE)), small, full((8, 128))],
        [shape_of((span, DI)), shape_of((span, TILE)), shape_of((span, 128), jnp.bfloat16), shape_of((8, 128))],
        [vmem((span, 128)), vmem((span, 128)), vmem((span, 128)), vmem((span // GROUP, 8, 128)), vmem((span, TILE))],
        (xi, values, dy, mixed_ext, mixed_ext, bc, col, dso, state_in, made, d1, kx, dbc, dcum, aux, conv, conv, ch, hp, rate),
        flops=8 * span * DI * STATE,
        nbytes=20 * span * DI,
    )


def conv_back(dconv, dconv_bc, following, mixed_ext, aux, conv):
    span = dconv.shape[0]
    groups = DI // TILE
    tile = lambda rows: pl.BlockSpec((rows, TILE), lambda g: (0, g))
    return pcall(
        conv_back_kernel,
        (groups + 1,),
        [
            pl.BlockSpec((span, TILE), lambda g: (0, jnp.minimum(g, groups - 1))),
            full((span, TILE)), tile(HALO), tile(span + HALO), full((span, 128)), tile(8),
        ],
        [tile(span), tile(8)],
        [shape_of((span, CHANNELS), jnp.bfloat16), shape_of((8, CHANNELS))],
        [vmem((span + HALO, TILE))],
        (dconv, dconv_bc, following, mixed_ext, aux, conv),
        flops=8 * span * DI,
        nbytes=10 * span * DI,
    )


def scan_states(received, keeps, reverse):
    peers = received.shape[0]
    rows = STATE * DI // 128 // peers
    return pcall(
        partial(scan_kernel, reverse, rows),
        (1,),
        [full(received.shape), full(keeps.shape)],
        full((peers, rows, 128)),
        shape_of((peers, rows, 128)),
        [],
        (received, keeps),
        nbytes=8 * peers * rows * 128,
    )


def exchange(parts):
    return lax.all_to_all(parts, "seq", split_axis=0, concat_axis=0, tiled=True)


def shifted(value, steps):
    count = lax.axis_size("seq")
    first, last = max(0, -steps), min(count, count - steps)
    return lax.ppermute(value, "seq", [(source, source + steps) for source in range(first, last)])


def doc_table(lengths, first, count):
    starts = jnp.cumsum(lengths, -1) - lengths
    places = first + jnp.arange(count, dtype=jnp.int32)
    return jnp.sum((starts[None, :] <= places[:, None]).astype(jnp.int32), -1) - 1


def token_marks(lengths, span):
    docs_all = doc_table(lengths, lax.axis_index("seq") * span - HALO, span + 2 * HALO)
    docs = docs_all[HALO : HALO + span]
    ends = docs_all[HALO - 1 : HALO + span : GROUP]
    prior, final = jnp.repeat(ends[:-1], GROUP), jnp.repeat(ends[1:], GROUP)
    near = lambda step: docs_all[HALO + step : HALO + step + span] == docs
    marks = [near(-3), near(-2), near(-1), docs == prior, docs == final, docs, near(1), near(2), near(3)]
    marks = jnp.stack([mark.astype(jnp.float32) for mark in marks], 1)
    aux = jnp.pad(marks, ((0, 0), (0, 128 - marks.shape[1])))
    auxr = jnp.broadcast_to(docs.astype(jnp.float32)[None, :], (8, span))
    return aux, auxr


def scattered(total):
    return lax.psum_scatter(total, AXES, scatter_dimension=0, tiled=True)


def matmul(a, b):
    return jnp.dot(a, b, preferred_element_type=jnp.float32)


def matmul_tn(a, b):
    return jnp.einsum("tn,tm->nm", a, b, preferred_element_type=jnp.float32)


def matmul_nt(a, b):
    return jnp.einsum("tn,mn->tm", a, b, preferred_element_type=jnp.float32)


def normalise(values, gain):
    scale = lax.rsqrt(jnp.mean(values * values, -1, keepdims=True) + EPS)
    return (values * scale * gain).astype(jnp.bfloat16)


def normalise_back(values, gain, grad):
    scale = lax.rsqrt(jnp.mean(values * values, -1, keepdims=True) + EPS)
    gain_grad = jnp.sum(grad * values * scale, 0)
    pulled = grad * gain
    return scale * pulled - values * (scale**3 * jnp.mean(pulled * values, -1, keepdims=True)), gain_grad


def padded(rows, width):
    table = jnp.stack([jnp.pad(row, (0, width - row.shape[0])) for row in rows])
    return jnp.pad(table, ((0, 8 - len(rows)), (0, 0)))


def local(
    inputs,
    lengths,
    norm_gain,
    in_weight,
    conv_weight,
    conv_bias,
    log_decay,
    dt_bias,
    skip,
    gate_gain,
    out_weight,
    cotangent,
):
    _, span, width = inputs.shape
    peers = lax.axis_size("seq")
    aux, auxr = token_marks(lengths[0], span)
    hidden = inputs[0]
    saved = []
    for depth in range(LAYERS):
        conv = jnp.concatenate([conv_weight[depth].T, conv_bias[depth][None], jnp.zeros((3, CHANNELS), jnp.float32)])
        hp = padded([dt_bias[depth], -jnp.exp(log_decay[depth])], 128)
        ch = padded([jnp.repeat(skip[depth], HEAD_DIM), gate_gain[depth]], DI)
        gate_weight = in_weight[depth][:, :DI]
        mixed_weight = in_weight[depth][:, DI : DI + CHANNELS]
        rate_weight = jnp.pad(in_weight[depth][:, DI + CHANNELS :], ((0, 0), (0, 128 - HEADS)))
        before = shifted(hidden[span - HALO :], 1)
        normed = normalise(hidden, norm_gain[depth])
        normed_ext = jnp.concatenate([normalise(before, norm_gain[depth]), normed])
        mixed_ext = matmul(normed_ext, mixed_weight)
        rate = matmul(normed, rate_weight)
        gate = matmul(normed, gate_weight)
        values, bc, col, cumr, made, kx, pay = make_states(peers, mixed_ext, rate, aux, conv, hp)
        received = exchange(pay)
        yi = inner(bc, values, col, cumr, aux, auxr)
        keeps = received[:, -8:]
        state_in = exchange(scan_states(received, keeps, False)).reshape(DI // 128, STATE, 128)
        y, out_low = finish(yi, values, gate, bc, col, state_in, made, kx, ch)
        saved.append(
            (hidden, normed, mixed_ext, rate, gate, values, bc, col, cumr, made, kx, keeps, state_in, y, out_low)
            + (conv, hp, ch, gate_weight, mixed_weight, rate_weight)
        )
        hidden = hidden + matmul(out_low, out_weight[depth])
    gradient = cotangent[0]
    collected = [None] * LAYERS
    big_in = [None] * LAYERS
    big_out = [None] * LAYERS
    for depth in reversed(range(LAYERS)):
        entry, normed, mixed_ext, rate, gate, values, bc, col, cumr, made, kx, keeps, state_in, y, out_low = saved[depth][:15]
        conv, hp, ch, gate_weight, mixed_weight, rate_weight = saved[depth][15:]
        grad_low = gradient.astype(jnp.bfloat16)
        big_out[depth] = scattered(matmul_tn(out_low, grad_low))
        dno = matmul_nt(grad_low, out_weight[depth])
        dy, dgate, gate_sums, d1, pay = gate_back(peers, dno, y, gate, values, bc, col, kx, ch)
        received = exchange(pay)
        xi, dbc, dcum = inner_back(bc, values, dy, col, cumr, aux, auxr)
        dso = exchange(scan_states(received, keeps, True)).reshape(DI // 128, STATE, 128)
        dconv, dconv_bc, drate, head_rows = states_back(
            xi, values, dy, mixed_ext, bc, col, dso, state_in, made, d1, kx, dbc, dcum, aux, conv, ch, hp, rate
        )
        following = shifted(jnp.concatenate([dconv[:HALO], dconv_bc[:HALO]], 1), -1)
        dmixed, conv_sums = conv_back(dconv, dconv_bc, following, mixed_ext, aux, conv)
        dprojected = jnp.concatenate([dgate, dmixed, drate[:, :HEADS]], 1)
        big_in[depth] = scattered(matmul_tn(normed, dprojected))
        grad_normed = matmul_nt(dprojected, in_weight[depth])
        grad_hidden, gain_grad = normalise_back(entry, norm_gain[depth], grad_normed)
        gradient = gradient + grad_hidden
        collected[depth] = (
            gain_grad,
            conv_sums[:KW].T,
            conv_sums[KW],
            gate_sums[0],
            head_rows[1, :HEADS],
            head_rows[0, :HEADS],
            jnp.sum(gate_sums[1].reshape(HEADS, HEAD_DIM), 1),
        )
    flat = jnp.concatenate([part.reshape(-1) for sums in collected for part in sums])
    flat = lax.psum(flat, AXES)
    index = lax.axis_index("seq") * lax.axis_size("rows") + lax.axis_index("rows")
    small = []
    at = 0
    for sums in collected:
        row = []
        for member, part in enumerate(sums):
            total = flat[at : at + part.size].reshape(part.shape)
            at += part.size
            if member < 4:
                size = part.shape[0] // lax.axis_size(AXES)
                total = lax.dynamic_slice_in_dim(total, index * size, size)
            row.append(total)
        small.append(row)
    stacked = [jnp.stack([small[level][member] for level in range(LAYERS)]) for member in range(7)]
    norm_gain_grad, conv_w_grad, conv_b_grad, gain_grad, decay_grad, bias_grad, skip_grad = stacked
    return (
        hidden[None],
        gradient[None],
        norm_gain_grad,
        jnp.stack(big_in),
        conv_w_grad,
        conv_b_grad,
        decay_grad,
        bias_grad,
        skip_grad,
        gain_grad,
        jnp.stack(big_out),
    )


def solution(mesh):
    in_specs = (
        P("rows", "seq", None),
        P("rows", None),
        P(),
        P(),
        P(),
        P(),
        P(),
        P(),
        P(),
        P(),
        P(),
        P("rows", "seq", None),
    )
    out_specs = (
        P("rows", "seq", None),
        P("rows", "seq", None),
        P(None, ("seq", "rows")),
        P(None, ("seq", "rows"), None),
        P(None, ("seq", "rows"), None),
        P(None, ("seq", "rows")),
        P(),
        P(),
        P(),
        P(None, ("seq", "rows")),
        P(None, ("seq", "rows"), None),
    )
    return jax.shard_map(local, mesh=mesh, in_specs=in_specs, out_specs=out_specs, check_vma=False)
```

```python
from functools import partial

import jax
import jax.numpy as jnp
from jax import lax
from jax.experimental import pallas as pl
from jax.experimental.pallas import tpu as pltpu
from jax.sharding import PartitionSpec as P

DI = 2048
STATE = 128
HEAD_DIM = 64
HEADS = DI // HEAD_DIM
KW = 4
GROUP = 256
LAYERS = 2
CHANNELS = DI + 2 * STATE
TILE = 256
HALO = 8
ROWS_AT = 64
VMEM_BYTES = 48 * 1024 * 1024

EPS = 1e-05
HIGHEST = lax.Precision.HIGHEST
AXES = ("seq", "rows")


def pcall(body, grid, in_specs, out_specs, out_shape, scratch, args, flops=0, nbytes=0):
    return pl.pallas_call(
        body,
        grid=grid,
        in_specs=in_specs,
        out_specs=out_specs,
        out_shape=out_shape,
        scratch_shapes=scratch,
        compiler_params=pltpu.CompilerParams(vmem_limit_bytes=VMEM_BYTES),
        cost_estimate=pl.CostEstimate(flops=flops, bytes_accessed=nbytes, transcendentals=0),
    )(*args)


def dot(a, b, dims=(((1,), (0,)), ((), ()))):
    return lax.dot_general(
        a.astype(jnp.bfloat16), b.astype(jnp.bfloat16), dims, preferred_element_type=jnp.float32
    )


def dot_nt(a, b):
    return dot(a, b, (((1,), (1,)), ((), ())))


def dot_exact(a, b):
    return jnp.dot(a, b, precision=HIGHEST, preferred_element_type=jnp.float32)


def sigmoid(v):
    return 1.0 / (1.0 + jnp.exp(-v))


def lane_iota(shape):
    return lax.broadcasted_iota(jnp.int32, shape, 1)


def low_half(rows):
    return lane_iota((rows, 128)) < HEAD_DIM


def to_heads(cols, first, pairs):
    rows = cols.shape[0]
    low = low_half(rows)
    parts = []
    for pair in range(pairs):
        at = first + 2 * pair
        parts.append(
            jnp.where(
                low,
                jnp.broadcast_to(cols[:, at : at + 1], (rows, 128)),
                jnp.broadcast_to(cols[:, at + 1 : at + 2], (rows, 128)),
            )
        )
    return jnp.concatenate(parts, 1) if pairs > 1 else parts[0]


def group_lanes(cols, group):
    return pltpu.roll(cols, (128 - 4 * group) % 128, 1)


def head_sums(group):
    channel = lax.broadcasted_iota(jnp.int32, (TILE, 128), 0)
    return (channel // HEAD_DIM + 4 * group == lane_iota((TILE, 128))).astype(jnp.float32)


def conv_rows(x_ref, w_ref, aux_ref, first, count):
    total = jnp.broadcast_to(w_ref[4:5, :], (count, w_ref.shape[1]))
    for tap in range(KW - 1):
        match = aux_ref[first : first + count, tap : tap + 1]
        total = total + w_ref[tap : tap + 1, :] * x_ref[first + 5 + tap : first + 5 + tap + count, :] * match
    return total + w_ref[3:4, :] * x_ref[first + 8 : first + 8 + count, :]


def states_kernel(
    x_ref, xbc_ref, rate_ref, aux_ref, w_ref, wbc_ref, hp_ref,
    v_ref, bc_ref, col_ref, cumr_ref, made_ref, kx_ref, pay_ref,
    bt_ref,
):
    group = pl.program_id(0)
    span = rate_ref.shape[0]
    count = span // GROUP

    @pl.when(group == 0)
    def _():
        for first in range(0, span, ROWS_AT):
            conv = conv_rows(xbc_ref, wbc_ref, aux_ref, first, ROWS_AT)
            bc_ref[first : first + ROWS_AT, :] = conv * sigmoid(conv)
        tri = (
            lax.broadcasted_iota(jnp.int32, (GROUP, GROUP), 0) >= lane_iota((GROUP, GROUP))
        ).astype(jnp.float32)
        for block in range(count):
            rows = slice(block * GROUP, (block + 1) * GROUP)
            bt_ref[block] = bc_ref[rows, :STATE].T.astype(jnp.bfloat16)
            raw = rate_ref[rows, :] + hp_ref[0:1, :]
            step = jnp.maximum(raw, 0.0) + jnp.log1p(jnp.exp(-jnp.abs(raw)))
            cum = dot_exact(tri, hp_ref[1:2, :] * step)
            last = cum[GROUP - 1 :, :]
            col_ref[0, rows, :] = cum
            col_ref[1, rows, :] = step
            col_ref[2, rows, :] = jnp.exp(cum) * aux_ref[rows, 3:4]
            col_ref[3, rows, :] = jnp.exp(last - cum) * aux_ref[rows, 4:5]
            cumr_ref[:, rows] = cum.T

    for first in range(0, span, ROWS_AT):
        conv = conv_rows(x_ref, w_ref, aux_ref, first, ROWS_AT)
        v_ref[first : first + ROWS_AT, :] = conv * sigmoid(conv)
    made = []
    keep = []
    for block in range(count):
        rows = slice(block * GROUP, (block + 1) * GROUP)
        weight = to_heads(group_lanes(col_ref[3, rows, :] * col_ref[1, rows, :], group), 0, 2)
        made.append(dot(bt_ref[block], weight * v_ref[rows, :]))
        ends = group_lanes(col_ref[2, (block + 1) * GROUP - 8 : (block + 1) * GROUP, :], group)
        keep.append(to_heads(ends, 0, 2)[7:8, :])
    made_ref[...] = made[0]
    kx_ref[...] = jnp.concatenate([keep[0], keep[1], jnp.zeros((6, TILE), jnp.float32)], 0)
    final = keep[1] * made[0] + made[1]
    total = jnp.broadcast_to(keep[0] * keep[1], (8, TILE))
    chunks = pay_ref.shape[0] // 2
    size = STATE // chunks
    for pair in range(2):
        lanes = slice(pair * 128, (pair + 1) * 128)
        for chunk in range(chunks):
            pay_ref[pair * chunks + chunk, :size, :] = final[chunk * size : (chunk + 1) * size, lanes]
            pay_ref[pair * chunks + chunk, size:, :] = total[:, lanes]


def inner_kernel(bc_ref, v_ref, col_ref, cumr_ref, aux_ref, auxr_ref, y_ref, g_ref):
    group = pl.program_id(1)

    @pl.when(group == 0)
    def _():
        scores = dot_nt(bc_ref[:, STATE:], bc_ref[:, :STATE])
        allowed = (aux_ref[:, 5:6] == auxr_ref[0:1, :]) & (
            lax.broadcasted_iota(jnp.int32, (GROUP, GROUP), 0) >= lane_iota((GROUP, GROUP))
        )
        g_ref[...] = jnp.where(allowed, scores, 0.0)

    cum = group_lanes(col_ref[0], group)
    step = group_lanes(col_ref[1], group)
    low = low_half(GROUP)
    for pair in range(2):
        lanes = slice(pair * 128, (pair + 1) * 128)
        scaled = to_heads(step, 2 * pair, 1) * v_ref[:, lanes]
        result = None
        for half in range(2):
            head = 2 * pair + half
            row = cumr_ref[pl.ds(4 * group + head, 1), :]
            parts = []
            for first in range(0, GROUP, 64):
                spread = cum[first : first + 64, head : head + 1] - row
                decay = jnp.exp(jnp.minimum(spread, 0.0))
                parts.append((g_ref[first : first + 64, :] * decay).astype(jnp.bfloat16))
            mixing = jnp.concatenate(parts, 0)
            picked = jnp.where(low if half == 0 else ~low, scaled, 0.0)
            part = dot(mixing, picked)
            result = part if result is None else result + part
        y_ref[:, lanes] = result


def finish_kernel(
    yi_ref, v_ref, gate_ref, bc_ref, col_ref, sin_ref, made_ref, kx_ref, ch_ref,
    y_ref, out_ref,
    gated_ref,
):
    block = pl.program_id(0)
    out_map = bc_ref[:, STATE:].astype(jnp.bfloat16)
    total = jnp.zeros((GROUP, 128), jnp.float32)
    pairs = v_ref.shape[1] // 128
    for pair in range(pairs):
        lanes = slice(pair * 128, (pair + 1) * 128)
        state = sin_ref[pair]
        state = jnp.where(block == 0, state, kx_ref[0:1, lanes] * state + made_ref[:, lanes])
        outer = to_heads(col_ref[2], 2 * pair, 1) * dot(out_map, state)
        result = yi_ref[:, lanes] + outer + ch_ref[0:1, lanes] * v_ref[:, lanes]
        y_ref[:, lanes] = result
        gate = gate_ref[:, lanes]
        gated = result * gate * sigmoid(gate)
        gated_ref[:, lanes] = gated
        total = total + gated * gated
    scale = lax.rsqrt(jnp.sum(total, 1, keepdims=True) / (pairs * 128) + EPS)
    for pair in range(pairs):
        lanes = slice(pair * 128, (pair + 1) * 128)
        out_ref[:, lanes] = (gated_ref[:, lanes] * scale * ch_ref[1:2, lanes]).astype(jnp.bfloat16)


def gate_back_kernel(
    dno_ref, y_ref, gate_ref, v_ref, bc_ref, col_ref, kx_ref, ch_ref,
    dy_ref, dgate_ref, sum_ref, d1_ref, pay_ref,
    gated_ref,
):
    block = pl.program_id(0)
    pairs = v_ref.shape[1] // 128
    square = jnp.zeros((GROUP, 128), jnp.float32)
    cross = jnp.zeros((GROUP, 128), jnp.float32)
    for pair in range(pairs):
        lanes = slice(pair * 128, (pair + 1) * 128)
        gate = gate_ref[:, lanes]
        gated = y_ref[:, lanes] * gate * sigmoid(gate)
        gated_ref[:, lanes] = gated
        square = square + gated * gated
        cross = cross + gated * dno_ref[:, lanes] * ch_ref[1:2, lanes]
    width = pairs * 128
    scale = lax.rsqrt(jnp.sum(square, 1, keepdims=True) / width + EPS)
    pull = scale * scale * scale * (jnp.sum(cross, 1, keepdims=True) / width)
    out_t = bc_ref[:, STATE:].T.astype(jnp.bfloat16)
    chunks = pay_ref.shape[0] // pairs
    size = STATE // chunks
    for pair in range(pairs):
        lanes = slice(pair * 128, (pair + 1) * 128)
        gate = gate_ref[:, lanes]
        gated = gated_ref[:, lanes]
        dno = dno_ref[:, lanes]
        sig = sigmoid(gate)
        dgated = scale * dno * ch_ref[1:2, lanes] - gated * pull
        dy = dgated * gate * sig
        dy_ref[:, lanes] = dy
        dgate_ref[:, lanes] = (dgated * y_ref[:, lanes] * sig * (1.0 + gate * (1.0 - sig))).astype(
            jnp.bfloat16
        )
        sums = jnp.concatenate(
            [
                jnp.sum(dno * gated * scale, 0, keepdims=True),
                jnp.sum(dy * v_ref[:, lanes], 0, keepdims=True),
                jnp.zeros((6, 128), jnp.float32),
            ],
            0,
        )
        fresh = dot(out_t, to_heads(col_ref[2], 2 * pair, 1) * dy)
        d1_ref[:, lanes] = fresh

        @pl.when(block == 0)
        def _():
            sum_ref[:, lanes] = sums
            for chunk in range(chunks):
                pay_ref[pair * chunks + chunk] = fresh[chunk * size : (chunk + 1) * size]

        @pl.when(block > 0)
        def _():
            sum_ref[:, lanes] += sums
            more = kx_ref[0:1, lanes] * fresh
            for chunk in range(chunks):
                pay_ref[pair * chunks + chunk] += more[chunk * size : (chunk + 1) * size]


def inner_back_kernel(
    bc_ref, v_ref, dy_ref, col_ref, cumr_ref, aux_ref, auxr_ref,
    x_ref, dbc_ref, dcum_ref,
    g_ref, dg_ref, cols_ref, rows_ref,
):
    group = pl.program_id(1)
    groups = pl.num_programs(1)

    def allowed():
        return (aux_ref[:, 5:6] == auxr_ref[0:1, :]) & (
            lax.broadcasted_iota(jnp.int32, (GROUP, GROUP), 0) <= lane_iota((GROUP, GROUP))
        )

    @pl.when(group == 0)
    def _():
        scores = dot_nt(bc_ref[:, :STATE], bc_ref[:, STATE:])
        g_ref[...] = jnp.where(allowed(), scores, 0.0)
        dg_ref[...] = jnp.zeros_like(dg_ref)
        cols_ref[...] = jnp.zeros_like(cols_ref)
        rows_ref[...] = jnp.zeros_like(rows_ref)

    cum = group_lanes(col_ref[0], group)
    step = group_lanes(col_ref[1], group)
    low = low_half(GROUP)
    lane = lane_iota((GROUP, 128))
    for pair in range(2):
        lanes = slice(pair * 128, (pair + 1) * 128)
        scaled = to_heads(step, 2 * pair, 1) * v_ref[:, lanes]
        dy = dy_ref[:, lanes]
        dy_low = dy.astype(jnp.bfloat16)
        result = None
        for half in range(2):
            head = 2 * pair + half
            row = cumr_ref[pl.ds(4 * group + head, 1), :]
            mine = low if half == 0 else ~low
            picked = jnp.where(mine, scaled, 0.0).astype(jnp.bfloat16)
            products = dot_nt(picked, dy_low)
            parts = []
            row_sum = jnp.zeros((8, GROUP), jnp.float32)
            col_sums = []
            for first in range(0, GROUP, 64):
                rows = slice(first, first + 64)
                spread = row - cum[rows, head : head + 1]
                decay = jnp.exp(jnp.minimum(spread, 0.0))
                scores = g_ref[rows, :]
                parts.append((scores * decay).astype(jnp.bfloat16))
                part = products[rows, :] * decay
                dg_ref[rows, :] += part
                both = part * scores
                row_sum = row_sum + jnp.sum(both.reshape(8, 8, GROUP), 0)
                col_sums.append(jnp.sum(both, 1, keepdims=True))
            mixing = jnp.concatenate(parts, 0)
            part = dot(mixing, jnp.where(mine, dy, 0.0))
            result = part if result is None else result + part
            rows_ref[pl.ds(4 * group + head, 1), :] = jnp.sum(row_sum, 0, keepdims=True)
            col_sum = jnp.concatenate(col_sums, 0)
            cols_ref[...] += jnp.where(lane == 4 * group + head, col_sum, 0.0)
        x_ref[:, lanes] = result

    @pl.when(group == groups - 1)
    def _():
        dg = jnp.where(allowed(), dg_ref[...], 0.0)
        dbc_ref[:, :STATE] = dot(dg, bc_ref[:, STATE:])
        dbc_ref[:, STATE:] = dot(dg.T, bc_ref[:, :STATE])
        dcum_ref[...] = rows_ref[...].T - cols_ref[...]


def states_back_kernel(
    xi_ref, v_ref, dy_ref, x_ref, xbc_ref, bc_ref, col_ref, dso_ref, sin_ref, made_ref, d1_ref,
    kx_ref, dbc_ref, dcum_ref, aux_ref, w_ref, wbc_ref, ch_ref, hp_ref, rate_ref,
    dconv_ref, dconv_bc_ref, drate_ref, sum_ref,
    ds_ref, dc_ref, z_ref, kd_ref, dmap_ref,
):
    group = pl.program_id(0)
    groups = pl.num_programs(0)
    span = v_ref.shape[0]
    count = span // GROUP

    @pl.when(group == 0)
    def _():
        ds_ref[...] = jnp.zeros_like(ds_ref)
        dc_ref[...] = dcum_ref[...]
        z_ref[...] = jnp.zeros_like(z_ref)
        kd_ref[...] = jnp.zeros_like(kd_ref)
        dmap_ref[...] = dbc_ref[...]

    sums = head_sums(group)
    end_grad = jnp.concatenate([dso_ref[0], dso_ref[1]], 1)
    state = jnp.concatenate([sin_ref[0], sin_ref[1]], 1)
    ends = [d1_ref[...] + kx_ref[1:2, :] * end_grad, end_grad]
    starts = [state, kx_ref[0:1, :] * state + made_ref[...]]
    for block in range(count):
        rows = slice(block * GROUP, (block + 1) * GROUP)
        step = to_heads(group_lanes(col_ref[1, rows, :], group), 0, 2)
        entering = to_heads(group_lanes(col_ref[2, rows, :], group), 0, 2)
        tail = to_heads(group_lanes(col_ref[3, rows, :], group), 0, 2)
        values = v_ref[rows, :]
        dy = dy_ref[rows, :]
        from_end = tail * dot(bc_ref[rows, :STATE], ends[block])
        outer = entering * dot(bc_ref[rows, STATE:], starts[block])
        pulled = xi_ref[rows, :] + from_end
        ds_ref[rows, :] += dot(values * pulled, sums)
        z_ref[rows, :] += dot(step * values * from_end, sums)
        dc_ref[rows, :] += dot(dy * outer, sums)
        dmap_ref[rows, :STATE] += dot_nt(tail * step * values, ends[block])
        dmap_ref[rows, STATE:] += dot_nt(entering * dy, starts[block])
        kept = kx_ref[block : block + 1, :] * jnp.sum(ends[block] * starts[block], 0, keepdims=True)
        kd_ref[block] += dot_exact(jnp.broadcast_to(kept, (8, TILE)), sums)
        grad = step * pulled + ch_ref[0:1, :] * dy
        conv = conv_rows(x_ref, w_ref, aux_ref, block * GROUP, GROUP)
        sig = sigmoid(conv)
        dconv_ref[rows, :] = grad * sig * (1.0 + conv * (1.0 - sig))

    @pl.when(group == groups - 1)
    def _():
        after = (
            lax.broadcasted_iota(jnp.int32, (GROUP, GROUP), 0) <= lane_iota((GROUP, GROUP))
        ).astype(jnp.float32)
        before = (
            lax.broadcasted_iota(jnp.int32, (GROUP, GROUP), 0) > lane_iota((GROUP, GROUP))
        ).astype(jnp.float32)
        bias_sum = jnp.zeros((1, 128), jnp.float32)
        decay_sum = jnp.zeros((1, 128), jnp.float32)
        for block in range(count):
            rows = slice(block * GROUP, (block + 1) * GROUP)
            conv = conv_rows(xbc_ref, wbc_ref, aux_ref, block * GROUP, GROUP)
            sig = sigmoid(conv)
            dconv_bc_ref[rows, :] = dmap_ref[rows, :] * sig * (1.0 + conv * (1.0 - sig))
            z = z_ref[rows, :]
            da = dot_exact(after, dc_ref[rows, :]) + kd_ref[block, 0:1, :]
            da = da + dot_exact(before, z)
            ds = ds_ref[rows, :] + hp_ref[1:2, :] * da
            drate = ds * sigmoid(rate_ref[rows, :] + hp_ref[0:1, :])
            drate_ref[rows, :] = drate.astype(jnp.bfloat16)
            bias_sum = bias_sum + jnp.sum(drate, 0, keepdims=True)
            decay_sum = decay_sum + jnp.sum(da * hp_ref[1:2, :] * col_ref[1, rows, :], 0, keepdims=True)
        sum_ref[...] = jnp.concatenate([bias_sum, decay_sum, jnp.zeros((6, 128), jnp.float32)], 0)


def conv_back_kernel(dconv_ref, dconv_bc_ref, next_ref, x_ref, aux_ref, w_ref, dx_ref, sum_ref, ext_ref):
    tile = pl.program_id(0)
    span = dconv_ref.shape[0]

    @pl.when(tile < pl.num_programs(0) - 1)
    def _():
        ext_ref[:span, :] = dconv_ref[...]

    @pl.when(tile == pl.num_programs(0) - 1)
    def _():
        ext_ref[:span, :] = dconv_bc_ref[...]

    ext_ref[span:, :] = next_ref[...]
    sums = [jnp.zeros((1, TILE), jnp.float32) for _ in range(KW + 1)]
    for first in range(0, span, ROWS_AT):
        here = ext_ref[first : first + ROWS_AT, :]
        grad = w_ref[3:4, :] * here
        for ahead in range(1, KW):
            match = aux_ref[first : first + ROWS_AT, 5 + ahead : 6 + ahead]
            grad = grad + w_ref[3 - ahead : 4 - ahead, :] * ext_ref[first + ahead : first + ahead + ROWS_AT, :] * match
        dx_ref[first : first + ROWS_AT, :] = grad.astype(jnp.bfloat16)
        for tap in range(KW):
            term = here * x_ref[first + 5 + tap : first + 5 + tap + ROWS_AT, :]
            if tap < KW - 1:
                term = term * aux_ref[first : first + ROWS_AT, tap : tap + 1]
            sums[tap] = sums[tap] + jnp.sum(term, 0, keepdims=True)
        sums[KW] = sums[KW] + jnp.sum(here, 0, keepdims=True)
    sum_ref[...] = jnp.concatenate(sums + [jnp.zeros((3, TILE), jnp.float32)], 0)


def scan_kernel(reverse, rows, in_ref, keep_ref, out_ref):
    peers = out_ref.shape[0]
    carried = jnp.zeros((rows, 128), jnp.float32)
    for at in range(peers):
        peer = peers - 1 - at if reverse else at
        out_ref[peer] = carried
        carried = keep_ref[peer, 0:1, :] * carried + in_ref[peer, :rows, :]


def full(shape):
    return pl.BlockSpec(shape, lambda *at: (0,) * len(shape))


def shape_of(dims, dtype=jnp.float32):
    return jax.ShapeDtypeStruct(dims, dtype)


def vmem(dims, dtype=jnp.float32):
    return pltpu.VMEM(dims, dtype)


def make_states(peers, mixed_ext, rate, aux, conv, hp):
    span = rate.shape[0]
    groups = DI // TILE
    chunks = peers * 128 // DI
    tile = lambda rows: pl.BlockSpec((rows, TILE), lambda g: (0, g))
    maps = lambda rows: pl.BlockSpec((rows, TILE), lambda g: (0, groups))
    pay = (2 * chunks, STATE // chunks + 8, 128)
    return pcall(
        states_kernel,
        (groups,),
        [tile(span + HALO), maps(span + HALO), full((span, 128)), full((span, 128)), tile(8), maps(8), full((8, 128))],
        [
            tile(span),
            full((span, TILE)),
            full((4, span, 128)),
            full((128, span)),
            tile(STATE),
            tile(8),
            pl.BlockSpec(pay, lambda g: (g, 0, 0)),
        ],
        [
            shape_of((span, DI)),
            shape_of((span, TILE)),
            shape_of((4, span, 128)),
            shape_of((128, span)),
            shape_of((STATE, DI)),
            shape_of((8, DI)),
            shape_of((peers,) + pay[1:]),
        ],
        [vmem((span // GROUP, STATE, GROUP), jnp.bfloat16)],
        (mixed_ext, mixed_ext, rate, aux, conv, conv, hp),
        flops=2 * span * DI * STATE,
        nbytes=12 * span * DI,
    )


def block_specs(span):
    blocks = span // GROUP
    tile = pl.BlockSpec((GROUP, TILE), lambda b, g: (b, g))
    maps = pl.BlockSpec((GROUP, TILE), lambda b, g: (b, 0))
    col = pl.BlockSpec((4, GROUP, 128), lambda b, g: (0, b, 0))
    row = pl.BlockSpec((128, GROUP), lambda b, g: (0, b))
    aux = pl.BlockSpec((GROUP, 128), lambda b, g: (b, 0))
    auxr = pl.BlockSpec((8, GROUP), lambda b, g: (0, b))
    return (blocks, DI // TILE), tile, maps, col, row, aux, auxr


def inner(bc, values, col, cumr, aux, auxr):
    span = values.shape[0]
    grid, tile, maps, cols, row, auxs, auxrs = block_specs(span)
    return pcall(
        inner_kernel,
        grid,
        [maps, tile, cols, row, auxs, auxrs],
        tile,
        shape_of((span, DI)),
        [vmem((GROUP, GROUP))],
        (bc, values, col, cumr, aux, auxr),
        flops=2 * span * GROUP * DI * 4,
        nbytes=8 * span * DI,
    )


def finish(yi, values, gate, bc, col, state_in, made, kx, ch):
    span = values.shape[0]
    wide = pl.BlockSpec((GROUP, DI), lambda b: (b, 0))
    maps = pl.BlockSpec((GROUP, TILE), lambda b: (b, 0))
    cols = pl.BlockSpec((4, GROUP, 128), lambda b: (0, b, 0))
    return pcall(
        finish_kernel,
        (span // GROUP,),
        [wide, wide, wide, maps, cols, full((DI // 128, STATE, 128)), full((STATE, DI)), full((8, DI)), full((8, DI))],
        [wide, wide],
        [shape_of((span, DI)), shape_of((span, DI), jnp.bfloat16)],
        [vmem((GROUP, DI))],
        (yi, values, gate, bc, col, state_in, made, kx, ch),
        flops=2 * span * DI * STATE,
        nbytes=18 * span * DI,
    )


def gate_back(peers, dno, y, gate, values, bc, col, kx, ch):
    span = values.shape[0]
    chunks = peers * 128 // DI
    wide = pl.BlockSpec((GROUP, DI), lambda b: (b, 0))
    maps = pl.BlockSpec((GROUP, TILE), lambda b: (b, 0))
    cols = pl.BlockSpec((4, GROUP, 128), lambda b: (0, b, 0))
    pay = (peers, STATE // chunks, 128)
    return pcall(
        gate_back_kernel,
        (span // GROUP,),
        [wide, wide, wide, wide, maps, cols, full((8, DI)), full((8, DI))],
        [wide, wide, full((8, DI)), full((STATE, DI)), full(pay)],
        [
            shape_of((span, DI)),
            shape_of((span, DI), jnp.bfloat16),
            shape_of((8, DI)),
            shape_of((STATE, DI)),
            shape_of(pay),
        ],
        [vmem((GROUP, DI))],
        (dno, y, gate, values, bc, col, kx, ch),
        flops=2 * span * DI * STATE,
        nbytes=22 * span * DI,
    )


def inner_back(bc, values, dy, col, cumr, aux, auxr):
    span = values.shape[0]
    grid, tile, maps, cols, row, auxs, auxrs = block_specs(span)
    return pcall(
        inner_back_kernel,
        grid,
        [maps, tile, tile, cols, row, auxs, auxrs],
        [tile, maps, auxs],
        [shape_of((span, DI)), shape_of((span, TILE)), shape_of((span, 128))],
        [vmem((GROUP, GROUP)), vmem((GROUP, GROUP)), vmem((GROUP, 128)), vmem((128, GROUP))],
        (bc, values, dy, col, cumr, aux, auxr),
        flops=2 * span * GROUP * DI * 8,
        nbytes=12 * span * DI,
    )


def states_back(xi, values, dy, mixed_ext, bc, col, dso, state_in, made, d1, kx, dbc, dcum, aux, conv, ch, hp, rate):
    span = values.shape[0]
    groups = DI // TILE
    tile = lambda rows: pl.BlockSpec((rows, TILE), lambda g: (0, g))
    maps = lambda rows: pl.BlockSpec((rows, TILE), lambda g: (0, groups))
    state = pl.BlockSpec((2, STATE, 128), lambda g: (g, 0, 0))
    small = full((span, 128))
    return pcall(
        states_back_kernel,
        (groups,),
        [
            tile(span), tile(span), tile(span), tile(span + HALO), maps(span + HALO), full((span, TILE)),
            full((4, span, 128)), state, state, tile(STATE), tile(STATE), tile(8), full((span, TILE)), small,
            small, tile(8), maps(8), tile(8), full((8, 128)), small,
        ],
        [tile(span), full((span, TILE)), small, full((8, 128))],
        [shape_of((span, DI)), shape_of((span, TILE)), shape_of((span, 128), jnp.bfloat16), shape_of((8, 128))],
        [vmem((span, 128)), vmem((span, 128)), vmem((span, 128)), vmem((span // GROUP, 8, 128)), vmem((span, TILE))],
        (xi, values, dy, mixed_ext, mixed_ext, bc, col, dso, state_in, made, d1, kx, dbc, dcum, aux, conv, conv, ch, hp, rate),
        flops=8 * span * DI * STATE,
        nbytes=20 * span * DI,
    )


def conv_back(dconv, dconv_bc, following, mixed_ext, aux, conv):
    span = dconv.shape[0]
    groups = DI // TILE
    tile = lambda rows: pl.BlockSpec((rows, TILE), lambda g: (0, g))
    return pcall(
        conv_back_kernel,
        (groups + 1,),
        [
            pl.BlockSpec((span, TILE), lambda g: (0, jnp.minimum(g, groups - 1))),
            full((span, TILE)), tile(HALO), tile(span + HALO), full((span, 128)), tile(8),
        ],
        [tile(span), tile(8)],
        [shape_of((span, CHANNELS), jnp.bfloat16), shape_of((8, CHANNELS))],
        [vmem((span + HALO, TILE))],
        (dconv, dconv_bc, following, mixed_ext, aux, conv),
        flops=8 * span * DI,
        nbytes=10 * span * DI,
    )


def scan_states(received, keeps, reverse):
    peers = received.shape[0]
    rows = STATE * DI // 128 // peers
    return pcall(
        partial(scan_kernel, reverse, rows),
        (1,),
        [full(received.shape), full(keeps.shape)],
        full((peers, rows, 128)),
        shape_of((peers, rows, 128)),
        [],
        (received, keeps),
        nbytes=8 * peers * rows * 128,
    )


def exchange(parts):
    return lax.all_to_all(parts, "seq", split_axis=0, concat_axis=0, tiled=True)


def shifted(value, steps):
    count = lax.axis_size("seq")
    first, last = max(0, -steps), min(count, count - steps)
    return lax.ppermute(value, "seq", [(source, source + steps) for source in range(first, last)])


def doc_table(lengths, first, count):
    starts = jnp.cumsum(lengths, -1) - lengths
    places = first + jnp.arange(count, dtype=jnp.int32)
    return jnp.sum((starts[None, :] <= places[:, None]).astype(jnp.int32), -1) - 1


def token_marks(lengths, span):
    docs_all = doc_table(lengths, lax.axis_index("seq") * span - HALO, span + 2 * HALO)
    docs = docs_all[HALO : HALO + span]
    ends = docs_all[HALO - 1 : HALO + span : GROUP]
    prior, final = jnp.repeat(ends[:-1], GROUP), jnp.repeat(ends[1:], GROUP)
    near = lambda step: docs_all[HALO + step : HALO + step + span] == docs
    marks = [near(-3), near(-2), near(-1), docs == prior, docs == final, docs, near(1), near(2), near(3)]
    marks = jnp.stack([mark.astype(jnp.float32) for mark in marks], 1)
    aux = jnp.pad(marks, ((0, 0), (0, 128 - marks.shape[1])))
    auxr = jnp.broadcast_to(docs.astype(jnp.float32)[None, :], (8, span))
    return aux, auxr


def halving(count, rows):
    def seq_masks(odd):
        masks = [rows << bit for bit in range(count.bit_length() - 1)]
        return masks[1::-1] + masks[2:] if odd else masks

    return [1 << bit for bit in range(rows.bit_length() - 1)], seq_masks(False), seq_masks(True)


def slab_order():
    count, rows = lax.axis_size("seq"), lax.axis_size("rows")
    row_masks, even, odd = halving(count, rows)
    stages = len(row_masks) + len(even)
    place = jnp.arange(count * rows, dtype=jnp.int32)
    bit = lambda stage: (place >> (stages - 1 - stage)) & 1
    slab = lax.axis_index("seq") * rows + lax.axis_index("rows") + 0 * place
    for stage, mask in enumerate(row_masks):
        slab = slab ^ (bit(stage) * mask)
    swapped = slab & 1
    for at, (one, two) in enumerate(zip(even, odd)):
        slab = slab ^ (bit(len(row_masks) + at) * jnp.where(swapped == 1, two, one))
    return slab


def in_order(values, order):
    width = values.shape[1]
    size = width // order.shape[0]
    source = (order[:, None] * size + jnp.arange(size, dtype=jnp.int32)[None, :]).reshape(-1)
    pick = (jnp.arange(width, dtype=jnp.int32)[:, None] == source[None, :]).astype(jnp.bfloat16)
    return jnp.dot(values, pick, preferred_element_type=jnp.float32).astype(jnp.bfloat16)


def scattered(left, right):
    count, rows = lax.axis_size("seq"), lax.axis_size("rows")
    row_masks, even, odd = halving(count, rows)
    half = left.shape[1] // 2
    send = matmul_tn(left[:, half:], right)
    keep = matmul_tn(left[:, :half], right)
    pairs = [(mask, mask) for mask in row_masks] + list(zip(even, odd))
    for stage, masks in enumerate(pairs):
        got = lax.ppermute(send, AXES, [(at, at ^ masks[at & 1]) for at in range(count * rows)])
        half = keep.shape[0] // 2
        if stage == len(pairs) - 1:
            return keep + got
        send = keep[half:] + got[half:]
        keep = keep[:half] + got[:half]


def matmul(a, b):
    return jnp.dot(a, b, preferred_element_type=jnp.float32)


def matmul_tn(a, b):
    return jnp.einsum("tn,tm->nm", a, b, preferred_element_type=jnp.float32)


def matmul_nt(a, b):
    return jnp.einsum("tn,mn->tm", a, b, preferred_element_type=jnp.float32)


def normalise(values, gain):
    scale = lax.rsqrt(jnp.mean(values * values, -1, keepdims=True) + EPS)
    return (values * scale * gain).astype(jnp.bfloat16)


def normalise_back(values, gain, grad):
    scale = lax.rsqrt(jnp.mean(values * values, -1, keepdims=True) + EPS)
    gain_grad = jnp.sum(grad * values * scale, 0)
    pulled = grad * gain
    return scale * pulled - values * (scale**3 * jnp.mean(pulled * values, -1, keepdims=True)), gain_grad


def padded(rows, width):
    table = jnp.stack([jnp.pad(row, (0, width - row.shape[0])) for row in rows])
    return jnp.pad(table, ((0, 8 - len(rows)), (0, 0)))


def local(
    inputs,
    lengths,
    norm_gain,
    in_weight,
    conv_weight,
    conv_bias,
    log_decay,
    dt_bias,
    skip,
    gate_gain,
    out_weight,
    cotangent,
):
    _, span, width = inputs.shape
    peers = lax.axis_size("seq")
    aux, auxr = token_marks(lengths[0], span)
    order = slab_order()
    hidden = inputs[0]
    saved = []
    for depth in range(LAYERS):
        conv = jnp.concatenate([conv_weight[depth].T, conv_bias[depth][None], jnp.zeros((3, CHANNELS), jnp.float32)])
        hp = padded([dt_bias[depth], -jnp.exp(log_decay[depth])], 128)
        ch = padded([jnp.repeat(skip[depth], HEAD_DIM), gate_gain[depth]], DI)
        gate_weight = in_weight[depth][:, :DI]
        mixed_weight = in_weight[depth][:, DI : DI + CHANNELS]
        rate_weight = jnp.pad(in_weight[depth][:, DI + CHANNELS :], ((0, 0), (0, 128 - HEADS)))
        before = shifted(hidden[span - HALO :], 1)
        normed = normalise(hidden, norm_gain[depth])
        normed_ext = jnp.concatenate([normalise(before, norm_gain[depth]), normed])
        mixed_ext = matmul(normed_ext, mixed_weight)
        rate = matmul(normed, rate_weight)
        gate = matmul(normed, gate_weight)
        values, bc, col, cumr, made, kx, pay = make_states(peers, mixed_ext, rate, aux, conv, hp)
        received = exchange(pay)
        yi = inner(bc, values, col, cumr, aux, auxr)
        keeps = received[:, -8:]
        state_in = exchange(scan_states(received, keeps, False)).reshape(DI // 128, STATE, 128)
        y, out_low = finish(yi, values, gate, bc, col, state_in, made, kx, ch)
        saved.append(
            (hidden, normed, mixed_ext, rate, gate, values, bc, col, cumr, made, kx, keeps, state_in, y, out_low)
            + (conv, hp, ch, gate_weight, mixed_weight, rate_weight)
        )
        hidden = hidden + matmul(out_low, out_weight[depth])
    gradient = cotangent[0]
    collected = [None] * LAYERS
    big_in = [None] * LAYERS
    big_out = [None] * LAYERS
    for depth in reversed(range(LAYERS)):
        entry, normed, mixed_ext, rate, gate, values, bc, col, cumr, made, kx, keeps, state_in, y, out_low = saved[depth][:15]
        conv, hp, ch, gate_weight, mixed_weight, rate_weight = saved[depth][15:]
        grad_low = gradient.astype(jnp.bfloat16)
        big_out[depth] = scattered(in_order(out_low, order), grad_low)
        dno = matmul_nt(grad_low, out_weight[depth])
        dy, dgate, gate_sums, d1, pay = gate_back(peers, dno, y, gate, values, bc, col, kx, ch)
        received = exchange(pay)
        xi, dbc, dcum = inner_back(bc, values, dy, col, cumr, aux, auxr)
        dso = exchange(scan_states(received, keeps, True)).reshape(DI // 128, STATE, 128)
        dconv, dconv_bc, drate, head_rows = states_back(
            xi, values, dy, mixed_ext, bc, col, dso, state_in, made, d1, kx, dbc, dcum, aux, conv, ch, hp, rate
        )
        following = shifted(jnp.concatenate([dconv[:HALO], dconv_bc[:HALO]], 1), -1)
        dmixed, conv_sums = conv_back(dconv, dconv_bc, following, mixed_ext, aux, conv)
        dprojected = jnp.concatenate([dgate, dmixed, drate[:, :HEADS]], 1)
        big_in[depth] = scattered(in_order(normed, order), dprojected)
        grad_normed = matmul_nt(dprojected, in_weight[depth])
        grad_hidden, gain_grad = normalise_back(entry, norm_gain[depth], grad_normed)
        gradient = gradient + grad_hidden
        collected[depth] = (
            gain_grad,
            conv_sums[:KW].T,
            conv_sums[KW],
            gate_sums[0],
            head_rows[1, :HEADS],
            head_rows[0, :HEADS],
            jnp.sum(gate_sums[1].reshape(HEADS, HEAD_DIM), 1),
        )
    devices = lax.axis_size(AXES)
    shares = [part.reshape(devices, -1) for sums in collected for part in sums[:4]]
    heads = jnp.concatenate([part for sums in collected for part in sums[4:]])
    table = jnp.concatenate(shares + [jnp.broadcast_to(heads, (devices,) + heads.shape)], 1)
    table = jnp.pad(table, ((0, 0), (0, -table.shape[1] % 128)))
    table = jnp.sum(lax.all_to_all(table, AXES, split_axis=0, concat_axis=0, tiled=True), 0)
    small = []
    at = 0
    for sums in collected:
        row = []
        for part in sums[:4]:
            size = part.size // devices
            row.append(table[at : at + size].reshape((part.shape[0] // devices,) + part.shape[1:]))
            at += size
        small.append(row)
    for row in small:
        for _ in range(3):
            row.append(table[at : at + HEADS])
            at += HEADS
    stacked = [jnp.stack([small[level][member] for level in range(LAYERS)]) for member in range(7)]
    norm_gain_grad, conv_w_grad, conv_b_grad, gain_grad, decay_grad, bias_grad, skip_grad = stacked
    return (
        hidden[None],
        gradient[None],
        norm_gain_grad,
        jnp.stack(big_in),
        conv_w_grad,
        conv_b_grad,
        decay_grad,
        bias_grad,
        skip_grad,
        gain_grad,
        jnp.stack(big_out),
    )


def solution(mesh):
    in_specs = (
        P("rows", "seq", None),
        P("rows", None),
        P(),
        P(),
        P(),
        P(),
        P(),
        P(),
        P(),
        P(),
        P(),
        P("rows", "seq", None),
    )
    out_specs = (
        P("rows", "seq", None),
        P("rows", "seq", None),
        P(None, ("seq", "rows")),
        P(None, ("seq", "rows"), None),
        P(None, ("seq", "rows"), None),
        P(None, ("seq", "rows")),
        P(),
        P(),
        P(),
        P(None, ("seq", "rows")),
        P(None, ("seq", "rows"), None),
    )
    return jax.shard_map(local, mesh=mesh, in_specs=in_specs, out_specs=out_specs, check_vma=False)
```

```python
from functools import partial

import jax
import jax.numpy as jnp
from jax import lax
from jax.experimental import pallas as pl
from jax.experimental.pallas import tpu as pltpu
from jax.sharding import PartitionSpec as P

DI = 2048
STATE = 128
HEAD_DIM = 64
HEADS = DI // HEAD_DIM
KW = 4
GROUP = 256
LAYERS = 2
CHANNELS = DI + 2 * STATE
TILE = 512
HEADS_AT = TILE // HEAD_DIM
MAPS = 2 * STATE
ROWS_STEP = 128
HALO = 8
HALF = 128
LOG2E = 1.4426950408889634
ROWS_AT = 64
VMEM_BYTES = 48 * 1024 * 1024

EPS = 1e-05
HIGHEST = lax.Precision.HIGHEST
AXES = ("seq", "rows")


def pcall(body, grid, in_specs, out_specs, out_shape, scratch, args, flops=0, nbytes=0, after=()):
    taken = len(args)

    def run(*refs):
        body(*refs[:taken], *refs[taken + len(after) :])

    return pl.pallas_call(
        run,
        grid=grid,
        in_specs=list(in_specs) + [pl.BlockSpec(memory_space=pltpu.HBM)] * len(after),
        out_specs=out_specs,
        out_shape=out_shape,
        scratch_shapes=scratch,
        compiler_params=pltpu.CompilerParams(vmem_limit_bytes=VMEM_BYTES),
        cost_estimate=pl.CostEstimate(flops=flops, bytes_accessed=nbytes, transcendentals=0),
    )(*args, *after)


def dot(a, b, dims=(((1,), (0,)), ((), ()))):
    return lax.dot_general(
        a.astype(jnp.bfloat16), b.astype(jnp.bfloat16), dims, preferred_element_type=jnp.float32
    )


def dot_nt(a, b):
    return dot(a, b, (((1,), (1,)), ((), ())))


def dot_exact(a, b):
    return jnp.dot(a, b, precision=HIGHEST, preferred_element_type=jnp.float32)


def sigmoid(v):
    return 0.5 * jnp.tanh(0.5 * v) + 0.5


def lane_iota(shape):
    return lax.broadcasted_iota(jnp.int32, shape, 1)


def low_half(rows):
    return lane_iota((rows, 128)) < HEAD_DIM


def to_heads(cols, first, pairs):
    rows = cols.shape[0]
    low = low_half(rows)
    parts = []
    for pair in range(pairs):
        at = first + 2 * pair
        parts.append(
            jnp.where(
                low,
                jnp.broadcast_to(cols[:, at : at + 1], (rows, 128)),
                jnp.broadcast_to(cols[:, at + 1 : at + 2], (rows, 128)),
            )
        )
    return jnp.concatenate(parts, 1) if pairs > 1 else parts[0]


def spread_heads(cols, pairs):
    pick = (
        lax.broadcasted_iota(jnp.int32, (128, 128 * pairs), 0) == lane_iota((128, 128 * pairs)) // HEAD_DIM
    ).astype(jnp.bfloat16)
    high = cols.astype(jnp.bfloat16)
    return dot(high, pick) + dot(cols - high.astype(jnp.float32), pick)


def head_pick(first, heads):
    shape = (128, HEAD_DIM * heads)
    return (lax.broadcasted_iota(jnp.int32, shape, 0) == first + lane_iota(shape) // HEAD_DIM).astype(jnp.bfloat16)


def picked_heads(cols, pick):
    high = cols.astype(jnp.bfloat16)
    return dot(high, pick) + dot(cols - high.astype(jnp.float32), pick)


def head_sums(first):
    channel = lax.broadcasted_iota(jnp.int32, (TILE, 128), 0)
    return (channel // HEAD_DIM + first == lane_iota((TILE, 128))).astype(jnp.bfloat16)


def keep_marks(marks_ref, aux_ref, lanes):
    for at, lane in enumerate(lanes):
        marks_ref[at] = jnp.broadcast_to(aux_ref[:, lane : lane + 1], marks_ref.shape[1:])


def conv_rows(x_ref, w_ref, marks_ref, first, count, lanes):
    total = w_ref[4:5, lanes] + w_ref[3:4, lanes] * x_ref[first + 8 : first + 8 + count, lanes]
    for tap in range(KW - 1):
        match = marks_ref[tap, first : first + count, :]
        total = total + w_ref[tap : tap + 1, lanes] * (x_ref[first + 5 + tap : first + 5 + tap + count, lanes] * match)
    return total


def chunks_of(rows, width):
    for pair in range(width // 128):
        for first in range(0, rows, ROWS_AT):
            yield first, slice(first, first + ROWS_AT), slice(pair * 128, (pair + 1) * 128)


def states_kernel(
    x_ref, xbc_ref, rate_ref, aux_ref, w_ref, wbc_ref, hp_ref,
    v_ref, bc_ref, col_ref, cumr_ref, made_ref, kx_ref, pay_ref,
    bt_ref, marks_ref,
):
    turn = pl.program_id(0)
    span = rate_ref.shape[0]
    count = span // GROUP

    @pl.when(turn == 0)
    def _():
        keep_marks(marks_ref, aux_ref, range(KW - 1))
        for first, rows, lanes in chunks_of(span, MAPS):
            conv = conv_rows(xbc_ref, wbc_ref, marks_ref, first, ROWS_AT, lanes)
            bc_ref[rows, lanes] = conv * sigmoid(conv)
        tri = (
            lax.broadcasted_iota(jnp.int32, (GROUP, GROUP), 0) >= lane_iota((GROUP, GROUP))
        ).astype(jnp.float32)
        for block in range(count):
            rows = slice(block * GROUP, (block + 1) * GROUP)
            bt_ref[block] = bc_ref[rows, :STATE].T.astype(jnp.bfloat16)
            raw = rate_ref[rows, :] + hp_ref[0:1, :]
            step = jnp.maximum(raw, 0.0) + jnp.log1p(jnp.exp(-jnp.abs(raw)))
            cum = dot_exact(tri, hp_ref[1:2, :] * step)
            last = cum[GROUP - 1 :, :]
            col_ref[0, rows, :] = cum
            col_ref[1, rows, :] = step
            col_ref[2, rows, :] = jnp.exp(cum) * aux_ref[rows, 3:4]
            col_ref[3, rows, :] = jnp.exp(last - cum) * aux_ref[rows, 4:5]
            cumr_ref[:, rows] = cum.T

    for first, rows, lanes in chunks_of(span, TILE):
        conv = conv_rows(x_ref, w_ref, marks_ref, first, ROWS_AT, lanes)
        v_ref[rows, lanes] = conv * sigmoid(conv)
    pick = head_pick(turn * HEADS_AT, HEADS_AT)
    made = []
    keep = []
    for block in range(count):
        rows = slice(block * GROUP, (block + 1) * GROUP)
        weight = picked_heads(col_ref[3, rows, :] * col_ref[1, rows, :], pick)
        made.append(dot(bt_ref[block], weight * v_ref[rows, :]))
        ends = col_ref[2, (block + 1) * GROUP - 8 : (block + 1) * GROUP, :]
        keep.append(picked_heads(ends, pick)[7:8, :])
    made_ref[...] = made[0]
    kx_ref[...] = jnp.concatenate([keep[0], keep[1], jnp.zeros((6, TILE), jnp.float32)], 0)
    final = keep[1] * made[0] + made[1]
    total = jnp.broadcast_to(keep[0] * keep[1], (8, TILE))
    pairs = TILE // 128
    chunks = pay_ref.shape[0] // pairs
    size = STATE // chunks
    for pair in range(pairs):
        lanes = slice(pair * 128, (pair + 1) * 128)
        for chunk in range(chunks):
            pay_ref[pair * chunks + chunk, :size, :] = final[chunk * size : (chunk + 1) * size, lanes]
            pay_ref[pair * chunks + chunk, size:, :] = total[:, lanes]


def inner_kernel(bc_ref, v_ref, col_ref, cumr_ref, aux_ref, auxr_ref, y_ref, g_ref):
    scores = dot_nt(bc_ref[:, STATE:], bc_ref[:, :STATE])
    allowed = (aux_ref[:, 5:6] == auxr_ref[0:1, :]) & (
        lax.broadcasted_iota(jnp.int32, (GROUP, GROUP), 0) >= lane_iota((GROUP, GROUP))
    )
    g_ref[...] = jnp.where(allowed, scores, 0.0)
    low = low_half(GROUP)
    cum = LOG2E * col_ref[0]
    cum_row = LOG2E * cumr_ref[:HEADS, :]
    steps = picked_heads(col_ref[1], head_pick(0, HEADS))
    for pair in range(HEADS // 2):
        lanes = slice(pair * 128, (pair + 1) * 128)
        scaled = steps[:, lanes] * v_ref[:, lanes]
        result = None
        for half in range(2):
            head = 2 * pair + half
            row = cum_row[head : head + 1, :]
            tops, bottoms = [], []
            for first in range(0, GROUP, 64):
                width = HALF if first < HALF else GROUP
                spread = cum[first : first + 64, head : head + 1] - row[:, :width]
                decay = jnp.exp2(jnp.minimum(spread, 0.0))
                mixing = (g_ref[first : first + 64, :width] * decay).astype(jnp.bfloat16)
                (tops if first < HALF else bottoms).append(mixing)
            picked = jnp.where(low if half == 0 else ~low, scaled, 0.0).astype(jnp.bfloat16)
            top = dot(jnp.concatenate(tops, 0), picked[:HALF])
            bottom = dot(jnp.concatenate(bottoms, 0), picked)
            result = (top, bottom) if result is None else (result[0] + top, result[1] + bottom)
        y_ref[:HALF, lanes] = result[0]
        y_ref[HALF:, lanes] = result[1]


def finish_kernel(
    yi_ref, v_ref, gate_ref, bc_ref, col_ref, sin_ref, made_ref, kx_ref, ch_ref,
    y_ref, out_ref,
    gated_ref,
):
    later = pl.program_id(0) * ROWS_STEP >= GROUP
    out_map = bc_ref[:, STATE:].astype(jnp.bfloat16)
    entering = picked_heads(col_ref[2], head_pick(0, HEADS))
    total = [jnp.zeros((ROWS_AT, 128), jnp.float32) for _ in range(ROWS_STEP // ROWS_AT)]
    for pair in range(HEADS // 2):
        lanes = slice(pair * 128, (pair + 1) * 128)
        state = sin_ref[pair]
        state = jnp.where(later, kx_ref[0:1, lanes] * state + made_ref[:, lanes], state)
        outer = entering[:, lanes] * dot(out_map, state)
        for at in range(ROWS_STEP // ROWS_AT):
            rows = slice(at * ROWS_AT, (at + 1) * ROWS_AT)
            result = yi_ref[rows, lanes] + outer[rows] + ch_ref[0:1, lanes] * v_ref[rows, lanes]
            y_ref[rows, lanes] = result
            gate = gate_ref[rows, lanes]
            gated = result * (gate * sigmoid(gate))
            gated_ref[rows, lanes] = gated
            total[at] = total[at] + gated * gated
    for at in range(ROWS_STEP // ROWS_AT):
        rows = slice(at * ROWS_AT, (at + 1) * ROWS_AT)
        scale = lax.rsqrt(jnp.sum(total[at], 1, keepdims=True) / DI + EPS)
        out_ref[rows, :] = (gated_ref[rows, :] * scale * ch_ref[1:2, :]).astype(jnp.bfloat16)


def gate_back_kernel(
    dno_ref, y_ref, gate_ref, v_ref, bc_ref, col_ref, kx_ref, ch_ref,
    dy_ref, dgate_ref, sum_ref, d1_ref, pay_ref,
    gated_ref, silu_ref,
):
    at_step = pl.program_id(0)
    later = at_step * ROWS_STEP >= GROUP
    parts = ROWS_STEP // ROWS_AT
    square = [jnp.zeros((ROWS_AT, 128), jnp.float32) for _ in range(parts)]
    cross = [jnp.zeros((ROWS_AT, 128), jnp.float32) for _ in range(parts)]
    for first, rows, lanes in chunks_of(ROWS_STEP, DI):
        gate = gate_ref[rows, lanes]
        sig = sigmoid(gate)
        silu = gate * sig
        y = y_ref[rows, lanes]
        gated = y * silu
        gated_ref[rows, lanes] = gated
        silu_ref[0, rows, lanes] = silu
        silu_ref[1, rows, lanes] = y * (sig * (1.0 + gate * (1.0 - sig)))
        at = first // ROWS_AT
        square[at] = square[at] + gated * gated
        cross[at] = cross[at] + gated * (dno_ref[rows, lanes] * ch_ref[1:2, lanes])
    scales = [lax.rsqrt(jnp.sum(part, 1, keepdims=True) / DI + EPS) for part in square]
    pulls = [scale * scale * scale * (jnp.sum(part, 1, keepdims=True) / DI) for scale, part in zip(scales, cross)]
    out_t = bc_ref[:, STATE:].T.astype(jnp.bfloat16)
    entering = picked_heads(col_ref[2], head_pick(0, HEADS))
    pairs = DI // 128
    chunks = pay_ref.shape[0] // pairs
    size = STATE // chunks

    @pl.when(at_step == 0)
    def _():
        sum_ref[...] = jnp.zeros_like(sum_ref)
        pay_ref[...] = jnp.zeros_like(pay_ref)

    @pl.when((at_step == 0) | (at_step * ROWS_STEP == GROUP))
    def _():
        d1_ref[...] = jnp.zeros_like(d1_ref)

    for pair in range(pairs):
        lanes = slice(pair * 128, (pair + 1) * 128)
        gain_sum = jnp.zeros((8, 128), jnp.float32)
        skip_sum = jnp.zeros((8, 128), jnp.float32)
        weighted = []
        for at in range(parts):
            rows = slice(at * ROWS_AT, (at + 1) * ROWS_AT)
            gated = gated_ref[rows, lanes]
            dno = dno_ref[rows, lanes] * scales[at]
            dgated = dno * ch_ref[1:2, lanes] - gated * pulls[at]
            dy = dgated * silu_ref[0, rows, lanes]
            dy_ref[rows, lanes] = dy
            dgate_ref[rows, lanes] = (dgated * silu_ref[1, rows, lanes]).astype(jnp.bfloat16)
            gain_sum = gain_sum + jnp.sum((dno * gated).reshape(-1, 8, 128), 0)
            skip_sum = skip_sum + jnp.sum((dy * v_ref[rows, lanes]).reshape(-1, 8, 128), 0)
            weighted.append((entering[rows, lanes] * dy).astype(jnp.bfloat16))
        sum_ref[0:1, lanes] += jnp.sum(gain_sum, 0, keepdims=True)
        sum_ref[1:2, lanes] += jnp.sum(skip_sum, 0, keepdims=True)
        fresh = dot(out_t, jnp.concatenate(weighted, 0))
        d1_ref[:, lanes] += fresh
        more = jnp.where(later, kx_ref[0:1, lanes], 1.0) * fresh
        for chunk in range(chunks):
            pay_ref[pair * chunks + chunk] += more[chunk * size : (chunk + 1) * size]


def inner_back_kernel(
    bc_ref, v_ref, dy_ref, col_ref, cumr_ref, aux_ref, auxr_ref,
    x_ref, dbc_ref,
    g_ref, dg_ref,
):
    allowed = (aux_ref[:, 5:6] == auxr_ref[0:1, :]) & (
        lax.broadcasted_iota(jnp.int32, (GROUP, GROUP), 0) <= lane_iota((GROUP, GROUP))
    )
    g_ref[...] = jnp.where(allowed, dot_nt(bc_ref[:, :STATE], bc_ref[:, STATE:]), 0.0)
    dg_ref[...] = jnp.zeros_like(dg_ref)
    low = low_half(GROUP)
    cum = LOG2E * col_ref[0]
    cum_row = LOG2E * cumr_ref[:HEADS, :]
    steps = picked_heads(col_ref[1], head_pick(0, HEADS))
    for pair in range(HEADS // 2):
        lanes = slice(pair * 128, (pair + 1) * 128)
        scaled = steps[:, lanes] * v_ref[:, lanes]
        dy = dy_ref[:, lanes]
        dy_low = dy.astype(jnp.bfloat16)
        result = None
        grads = {}
        for half in range(2):
            head = 2 * pair + half
            row = cum_row[head : head + 1, :]
            mine = low if half == 0 else ~low
            picked = jnp.where(mine, scaled, 0.0).astype(jnp.bfloat16)
            top_grad = dot_nt(picked[:HALF], dy_low)
            bottom_grad = dot_nt(picked[HALF:], dy_low[HALF:])
            tops, bottoms = [], []
            for first in range(0, GROUP, 64):
                rows = slice(first, first + 64)
                top = first < HALF
                across = slice(0 if top else HALF, GROUP)
                spread = row[:, across] - cum[rows, head : head + 1]
                decay = jnp.exp2(jnp.minimum(spread, 0.0))
                (tops if top else bottoms).append((g_ref[rows, across] * decay).astype(jnp.bfloat16))
                part = (top_grad[rows] if top else bottom_grad[first - HALF : first - HALF + 64]) * decay
                if half == 0:
                    grads[first] = part
                else:
                    dg_ref[rows, across] += grads[first] + part
            dy_mine = jnp.where(mine, dy, 0.0).astype(jnp.bfloat16)
            top = dot(jnp.concatenate(tops, 0), dy_mine)
            bottom = dot(jnp.concatenate(bottoms, 0), dy_mine[HALF:])
            result = (top, bottom) if result is None else (result[0] + top, result[1] + bottom)
        x_ref[:HALF, lanes] = result[0]
        x_ref[HALF:, lanes] = result[1]
    dg = jnp.where(allowed, dg_ref[...], 0.0)
    dbc_ref[:, :STATE] = dot(dg, bc_ref[:, STATE:])
    dbc_ref[:, STATE:] = dot(dg.T, bc_ref[:, :STATE])


def states_back_kernel(
    xi_ref, v_ref, dy_ref, yi_ref, x_ref, xbc_ref, bc_ref, col_ref, dso_ref, sin_ref, made_ref, d1_ref,
    kx_ref, dbc_ref, aux_ref, w_ref, wbc_ref, ch_ref, hp_ref, rate_ref,
    dconv_ref, dconv_bc_ref, drate_ref, sum_ref,
    ds_ref, dc_ref, z_ref, kd_ref, dmap_ref, marks_ref,
):
    turn = pl.program_id(0)
    span = v_ref.shape[0]
    count = span // GROUP

    @pl.when(turn == 0)
    def _():
        keep_marks(marks_ref, aux_ref, range(KW - 1))
        ds_ref[...] = jnp.zeros_like(ds_ref)
        dc_ref[...] = jnp.zeros_like(dc_ref)
        z_ref[...] = jnp.zeros_like(z_ref)
        kd_ref[...] = jnp.zeros_like(kd_ref)
        dmap_ref[...] = dbc_ref[...]

    sums = head_sums(turn * HEADS_AT)
    pick = head_pick(turn * HEADS_AT, HEADS_AT)
    end_grad = jnp.concatenate([dso_ref[pair] for pair in range(TILE // 128)], 1)
    state = jnp.concatenate([sin_ref[pair] for pair in range(TILE // 128)], 1)
    ends = [d1_ref[...] + kx_ref[1:2, :] * end_grad, end_grad]
    starts = [state, kx_ref[0:1, :] * state + made_ref[...]]
    for block in range(count):
        at = slice(block * GROUP, (block + 1) * GROUP)
        step = picked_heads(col_ref[1, at, :], pick)
        entering = picked_heads(col_ref[2, at, :], pick)
        tail = picked_heads(col_ref[3, at, :], pick)
        from_end = dot(bc_ref[at, :STATE], ends[block])
        outer = dot(bc_ref[at, STATE:], starts[block])
        kinds = {name: [] for name in ("ds", "z", "dc", "low", "values", "dy")}
        for first in range(0, GROUP, ROWS_AT):
            local = slice(first, first + ROWS_AT)
            rows = slice(block * GROUP + first, block * GROUP + first + ROWS_AT)
            pieces = {name: [] for name in kinds}
            for pair in range(TILE // 128):
                lanes = slice(pair * 128, (pair + 1) * 128)
                v = v_ref[rows, lanes]
                dy = dy_ref[rows, lanes]
                xi = xi_ref[rows, lanes]
                scaled = step[local, lanes] * v
                low = dy.astype(jnp.bfloat16).astype(jnp.float32)
                inside = low * yi_ref[rows, lanes] - scaled.astype(jnp.bfloat16).astype(jnp.float32) * xi
                ended = tail[local, lanes] * from_end[local, lanes]
                inside = inside + dy * (entering[local, lanes] * outer[local, lanes])
                pulled = xi + ended
                high = inside.astype(jnp.bfloat16)
                pieces["dc"].append(high)
                pieces["low"].append((inside - high.astype(jnp.float32)).astype(jnp.bfloat16))
                pieces["ds"].append((v * pulled).astype(jnp.bfloat16))
                pieces["z"].append((scaled * ended).astype(jnp.bfloat16))
                pieces["values"].append((tail[local, lanes] * scaled).astype(jnp.bfloat16))
                pieces["dy"].append((entering[local, lanes] * dy).astype(jnp.bfloat16))
                grad = step[local, lanes] * pulled + ch_ref[0:1, lanes] * dy
                conv = conv_rows(x_ref, w_ref, marks_ref, block * GROUP + first, ROWS_AT, lanes)
                sig = sigmoid(conv)
                dconv_ref[rows, lanes] = grad * (sig * (1.0 + conv * (1.0 - sig)))
            for name in kinds:
                kinds[name].append(jnp.concatenate(pieces[name], 1))
        whole = {name: jnp.concatenate(parts, 0) for name, parts in kinds.items()}
        ds_ref[at, :] += dot(whole["ds"], sums)
        z_ref[at, :] += dot(whole["z"], sums)
        dc_ref[at, :] += dot(whole["dc"], sums) + dot(whole["low"], sums)
        dmap_ref[at, :STATE] += dot_nt(whole["values"], ends[block])
        dmap_ref[at, STATE:] += dot_nt(whole["dy"], starts[block])
        kept = kx_ref[block : block + 1, :] * jnp.sum(ends[block] * starts[block], 0, keepdims=True)
        kd_ref[block] += dot_exact(jnp.broadcast_to(kept, (8, TILE)), sums.astype(jnp.float32))

    @pl.when(turn == pl.num_programs(0) - 1)
    def _():
        here = lax.broadcasted_iota(jnp.int32, (GROUP, GROUP), 0)
        after = (here <= lane_iota((GROUP, GROUP))).astype(jnp.float32)
        before = (here > lane_iota((GROUP, GROUP))).astype(jnp.float32)
        bias_sum = jnp.zeros((1, 128), jnp.float32)
        decay_sum = jnp.zeros((1, 128), jnp.float32)
        for first, rows, lanes in chunks_of(span, MAPS):
            conv = conv_rows(xbc_ref, wbc_ref, marks_ref, first, ROWS_AT, lanes)
            sig = sigmoid(conv)
            dconv_bc_ref[rows, lanes] = dmap_ref[rows, lanes] * (sig * (1.0 + conv * (1.0 - sig)))
        for block in range(count):
            rows = slice(block * GROUP, (block + 1) * GROUP)
            z = z_ref[rows, :]
            da = dot_exact(after, dc_ref[rows, :]) + kd_ref[block, 0:1, :]
            da = da + dot_exact(before, z)
            ds = ds_ref[rows, :] + hp_ref[1:2, :] * da
            drate = ds * sigmoid(rate_ref[rows, :] + hp_ref[0:1, :])
            drate_ref[rows, :] = drate.astype(jnp.bfloat16)
            bias_sum = bias_sum + jnp.sum(drate, 0, keepdims=True)
            decay_sum = decay_sum + jnp.sum(da * hp_ref[1:2, :] * col_ref[1, rows, :], 0, keepdims=True)
        sum_ref[...] = jnp.concatenate([bias_sum, decay_sum, jnp.zeros((6, 128), jnp.float32)], 0)


def conv_back_kernel(
    dconv_ref, dconv_bc_ref, next_ref, x_ref, aux_ref, w_ref, dx_ref, sum_ref, ext_ref, marks_ref
):
    turn = pl.program_id(0)
    last = pl.num_programs(0) - 1
    span = dconv_ref.shape[0]

    @pl.when(turn == 0)
    def _():
        keep_marks(marks_ref, aux_ref, (0, 1, 2, 6, 7, 8))

    @pl.when(turn < last)
    def _():
        ext_ref[:span, :] = dconv_ref[...]

    @pl.when(turn == last)
    def _():
        ext_ref[:span, :MAPS] = dconv_bc_ref[...]

    ext_ref[span:, :] = next_ref[...]
    for pair in range(TILE // 128):
        lanes = slice(pair * 128, (pair + 1) * 128)
        sums = [jnp.zeros((8, 128), jnp.float32) for _ in range(KW + 1)]
        for first in range(0, span, ROWS_AT):
            rows = slice(first, first + ROWS_AT)
            here = ext_ref[rows, lanes]
            grad = w_ref[3:4, lanes] * here
            for ahead in range(1, KW):
                shifted_grad = ext_ref[first + ahead : first + ahead + ROWS_AT, lanes]
                grad = grad + w_ref[3 - ahead : 4 - ahead, lanes] * (shifted_grad * marks_ref[2 + ahead, rows, :])
            dx_ref[rows, lanes] = grad.astype(jnp.bfloat16)
            for tap in range(KW):
                term = here * x_ref[first + 5 + tap : first + 5 + tap + ROWS_AT, lanes]
                if tap < KW - 1:
                    term = term * marks_ref[tap, rows, :]
                sums[tap] = sums[tap] + jnp.sum(term.reshape(-1, 8, 128), 0)
            sums[KW] = sums[KW] + jnp.sum(here.reshape(-1, 8, 128), 0)
        sums = [jnp.sum(part, 0, keepdims=True) for part in sums]
        sum_ref[:, lanes] = jnp.concatenate(sums + [jnp.zeros((3, 128), jnp.float32)], 0)


def scan_kernel(reverse, rows, in_ref, keep_ref, out_ref):
    peers = out_ref.shape[0]
    carried = jnp.zeros((rows, 128), jnp.float32)
    for at in range(peers):
        peer = peers - 1 - at if reverse else at
        out_ref[peer] = carried
        carried = keep_ref[peer, 0:1, :] * carried + in_ref[peer, :rows, :]


def total_kernel(in_ref, out_ref):
    out_ref[...] = jnp.sum(in_ref[...], 0)


def full(shape):
    return pl.BlockSpec(shape, lambda *at: (0,) * len(shape))


def shape_of(dims, dtype=jnp.float32):
    return jax.ShapeDtypeStruct(dims, dtype)


def vmem(dims, dtype=jnp.float32):
    return pltpu.VMEM(dims, dtype)


def make_states(peers, mixed_ext, rate, aux, conv, hp):
    span = rate.shape[0]
    groups = DI // TILE
    chunks = peers * 128 // DI
    tile = lambda rows: pl.BlockSpec((rows, TILE), lambda g: (0, g))
    maps = lambda rows: pl.BlockSpec((rows, MAPS), lambda g: (0, DI // MAPS))
    pay = (TILE // 128 * chunks, STATE // chunks + 8, 128)
    return pcall(
        states_kernel,
        (groups,),
        [tile(span + HALO), maps(span + HALO), full((span, 128)), full((span, 128)), tile(8), maps(8), full((8, 128))],
        [
            tile(span),
            full((span, MAPS)),
            full((4, span, 128)),
            full((128, span)),
            tile(STATE),
            tile(8),
            pl.BlockSpec(pay, lambda g: (g, 0, 0)),
        ],
        [
            shape_of((span, DI)),
            shape_of((span, MAPS)),
            shape_of((4, span, 128)),
            shape_of((128, span)),
            shape_of((STATE, DI)),
            shape_of((8, DI)),
            shape_of((peers,) + pay[1:]),
        ],
        [vmem((span // GROUP, STATE, GROUP), jnp.bfloat16), vmem((KW - 1, span, 128))],
        (mixed_ext, mixed_ext, rate, aux, conv, conv, hp),
        flops=2 * span * DI * STATE,
        nbytes=12 * span * DI,
    )


def block_rows(span):
    wide = pl.BlockSpec((GROUP, DI), lambda b: (b, 0))
    maps = pl.BlockSpec((GROUP, MAPS), lambda b: (b, 0))
    col = pl.BlockSpec((4, GROUP, 128), lambda b: (0, b, 0))
    row = pl.BlockSpec((128, GROUP), lambda b: (0, b))
    aux = pl.BlockSpec((GROUP, 128), lambda b: (b, 0))
    auxr = pl.BlockSpec((8, GROUP), lambda b: (0, b))
    return wide, maps, col, row, aux, auxr


def inner(bc, values, col, cumr, aux, auxr):
    span = values.shape[0]
    wide, maps, cols, row, auxs, auxrs = block_rows(span)
    return pcall(
        inner_kernel,
        (span // GROUP,),
        [maps, wide, cols, row, auxs, auxrs],
        wide,
        shape_of((span, DI)),
        [vmem((GROUP, GROUP))],
        (bc, values, col, cumr, aux, auxr),
        flops=2 * span * GROUP * DI * 4,
        nbytes=8 * span * DI,
    )


def finish(yi, values, gate, bc, col, state_in, made, kx, ch):
    span = values.shape[0]
    wide = pl.BlockSpec((ROWS_STEP, DI), lambda b: (b, 0))
    maps = pl.BlockSpec((ROWS_STEP, MAPS), lambda b: (b, 0))
    cols = pl.BlockSpec((4, ROWS_STEP, 128), lambda b: (0, b, 0))
    return pcall(
        finish_kernel,
        (span // ROWS_STEP,),
        [wide, wide, wide, maps, cols, full((DI // 128, STATE, 128)), full((STATE, DI)), full((8, DI)), full((8, DI))],
        [wide, wide],
        [shape_of((span, DI)), shape_of((span, DI), jnp.bfloat16)],
        [vmem((ROWS_STEP, DI))],
        (yi, values, gate, bc, col, state_in, made, kx, ch),
        flops=2 * span * DI * STATE,
        nbytes=18 * span * DI,
    )


def gate_back(peers, dno, y, gate, values, bc, col, kx, ch, after=()):
    span = values.shape[0]
    chunks = peers * 128 // DI
    wide = pl.BlockSpec((ROWS_STEP, DI), lambda b: (b, 0))
    maps = pl.BlockSpec((ROWS_STEP, MAPS), lambda b: (b, 0))
    cols = pl.BlockSpec((4, ROWS_STEP, 128), lambda b: (0, b, 0))
    pay = (peers, STATE // chunks, 128)
    return pcall(
        gate_back_kernel,
        (span // ROWS_STEP,),
        [wide, wide, wide, wide, maps, cols, full((8, DI)), full((8, DI))],
        [wide, wide, full((8, DI)), full((STATE, DI)), full(pay)],
        [
            shape_of((span, DI)),
            shape_of((span, DI), jnp.bfloat16),
            shape_of((8, DI)),
            shape_of((STATE, DI)),
            shape_of(pay),
        ],
        [vmem((ROWS_STEP, DI)), vmem((2, ROWS_STEP, DI))],
        (dno, y, gate, values, bc, col, kx, ch),
        flops=2 * span * DI * STATE,
        nbytes=22 * span * DI,
        after=after,
    )


def inner_back(bc, values, dy, col, cumr, aux, auxr, after=()):
    span = values.shape[0]
    wide, maps, cols, row, auxs, auxrs = block_rows(span)
    return pcall(
        inner_back_kernel,
        (span // GROUP,),
        [maps, wide, wide, cols, row, auxs, auxrs],
        [wide, maps],
        [shape_of((span, DI)), shape_of((span, MAPS))],
        [vmem((GROUP, GROUP)), vmem((GROUP, GROUP))],
        (bc, values, dy, col, cumr, aux, auxr),
        flops=2 * span * GROUP * DI * 8,
        nbytes=12 * span * DI,
        after=after,
    )


def states_back(xi, values, dy, yi, mixed_ext, bc, col, dso, state_in, made, d1, kx, dbc, aux, conv, ch, hp, rate, after=()):
    span = values.shape[0]
    groups = DI // TILE
    tile = lambda rows: pl.BlockSpec((rows, TILE), lambda g: (0, g))
    maps = lambda rows: pl.BlockSpec((rows, MAPS), lambda g: (0, DI // MAPS))
    state = pl.BlockSpec((TILE // 128, STATE, 128), lambda g: (g, 0, 0))
    small = full((span, 128))
    return pcall(
        states_back_kernel,
        (groups,),
        [
            tile(span), tile(span), tile(span), tile(span), tile(span + HALO), maps(span + HALO), full((span, MAPS)),
            full((4, span, 128)), state, state, tile(STATE), tile(STATE), tile(8), full((span, MAPS)),
            small, tile(8), maps(8), tile(8), full((8, 128)), small,
        ],
        [tile(span), full((span, MAPS)), small, full((8, 128))],
        [shape_of((span, DI)), shape_of((span, MAPS)), shape_of((span, 128), jnp.bfloat16), shape_of((8, 128))],
        [vmem((span, 128)), vmem((span, 128)), vmem((span, 128)), vmem((span // GROUP, 8, 128)), vmem((span, MAPS)), vmem((KW - 1, span, 128))],
        (xi, values, dy, yi, mixed_ext, mixed_ext, bc, col, dso, state_in, made, d1, kx, dbc, aux, conv, conv, ch, hp, rate),
        flops=8 * span * DI * STATE,
        nbytes=20 * span * DI,
        after=after,
    )


def conv_back(dconv, dconv_bc, following, mixed_ext, aux, conv, after=()):
    span = dconv.shape[0]
    groups = DI // TILE
    tile = lambda rows: pl.BlockSpec((rows, TILE), lambda g: (0, g))
    return pcall(
        conv_back_kernel,
        (groups + 1,),
        [
            pl.BlockSpec((span, TILE), lambda g: (0, jnp.minimum(g, groups - 1))),
            full((span, MAPS)), tile(HALO), tile(span + HALO), full((span, 128)), tile(8),
        ],
        [tile(span), tile(8)],
        [shape_of((span, CHANNELS), jnp.bfloat16), shape_of((8, CHANNELS))],
        [vmem((span + HALO, TILE)), vmem((2 * (KW - 1), span, 128))],
        (dconv, dconv_bc, following, mixed_ext, aux, conv),
        flops=8 * span * DI,
        nbytes=10 * span * DI,
        after=after,
    )


def scan_states(received, keeps, reverse, after=()):
    peers = received.shape[0]
    rows = STATE * DI // 128 // peers
    return pcall(
        partial(scan_kernel, reverse, rows),
        (1,),
        [full(received.shape), full(keeps.shape)],
        full((peers, rows, 128)),
        shape_of((peers, rows, 128)),
        [],
        (received, keeps),
        nbytes=8 * peers * rows * 128,
        after=after,
    )


def exchange(parts):
    return lax.all_to_all(parts, "seq", split_axis=0, concat_axis=0, tiled=True)


def shifted(value, steps):
    count = lax.axis_size("seq")
    first, last = max(0, -steps), min(count, count - steps)
    return lax.ppermute(value, "seq", [(source, source + steps) for source in range(first, last)])


def doc_table(lengths, first, count):
    starts = jnp.cumsum(lengths, -1) - lengths
    places = first + jnp.arange(count, dtype=jnp.int32)
    return jnp.sum((starts[None, :] <= places[:, None]).astype(jnp.int32), -1) - 1


def token_marks(lengths, span):
    docs_all = doc_table(lengths, lax.axis_index("seq") * span - HALO, span + 2 * HALO)
    docs = docs_all[HALO : HALO + span]
    ends = docs_all[HALO - 1 : HALO + span : GROUP]
    prior, final = jnp.repeat(ends[:-1], GROUP), jnp.repeat(ends[1:], GROUP)
    near = lambda step: docs_all[HALO + step : HALO + step + span] == docs
    marks = [near(-3), near(-2), near(-1), docs == prior, docs == final, docs, near(1), near(2), near(3)]
    marks = jnp.stack([mark.astype(jnp.float32) for mark in marks], 1)
    aux = jnp.pad(marks, ((0, 0), (0, 128 - marks.shape[1])))
    auxr = jnp.broadcast_to(docs.astype(jnp.float32)[None, :], (8, span))
    return aux, auxr


def halving(count, rows):
    def seq_masks(odd):
        masks = [rows << bit for bit in range(count.bit_length() - 1)]
        return masks[1::-1] + masks[2:] if odd else masks

    return [1 << bit for bit in range(rows.bit_length() - 1)], seq_masks(False), seq_masks(True)


def slab_order():
    count, rows = lax.axis_size("seq"), lax.axis_size("rows")
    row_masks, even, odd = halving(count, rows)
    stages = len(row_masks) + len(even)
    place = jnp.arange(count * rows, dtype=jnp.int32)
    bit = lambda stage: (place >> (stages - 1 - stage)) & 1
    slab = lax.axis_index("seq") * rows + lax.axis_index("rows") + 0 * place
    for stage, mask in enumerate(row_masks):
        slab = slab ^ (bit(stage) * mask)
    swapped = slab & 1
    for at, (one, two) in enumerate(zip(even, odd)):
        slab = slab ^ (bit(len(row_masks) + at) * jnp.where(swapped == 1, two, one))
    return slab


def in_order(values, order):
    width = values.shape[1]
    size = width // order.shape[0]
    source = (order[:, None] * size + jnp.arange(size, dtype=jnp.int32)[None, :]).reshape(-1)
    pick = (jnp.arange(width, dtype=jnp.int32)[:, None] == source[None, :]).astype(jnp.bfloat16)
    return jnp.dot(values, pick, preferred_element_type=jnp.float32).astype(jnp.bfloat16)


class Scatter:

    def __init__(self, left, right):
        half = left.shape[1] // 2
        self.send = matmul_tn(left[:, half:], right)
        self.keep = matmul_tn(left[:, :half], right)
        count, rows = lax.axis_size("seq"), lax.axis_size("rows")
        row_masks, even, odd = halving(count, rows)
        self.devices = count * rows
        self.stages = [(mask, mask) for mask in row_masks] + list(zip(even, odd))
        self.share()

    def share(self):
        masks = self.stages.pop(0)
        self.got = lax.ppermute(self.send, AXES, [(at, at ^ masks[at & 1]) for at in range(self.devices)])

    def step(self):
        if not self.stages:
            if self.got is not None:
                self.keep = self.keep + self.got
            self.got = None
            return (self.keep,)
        half = self.keep.shape[0] // 2
        self.send = self.keep[half:] + self.got[half:]
        self.keep = self.keep[:half] + self.got[:half]
        self.share()
        return (self.send, self.keep)

    def result(self):
        while self.got is not None:
            self.step()
        return self.keep


def steps(*scatters):
    return sum((scatter.step() for scatter in scatters), ())


def matmul(a, b):
    return jnp.dot(a, b, preferred_element_type=jnp.float32)


def matmul_tn(a, b):
    return jnp.einsum("tn,tm->nm", a, b, preferred_element_type=jnp.float32)


def matmul_nt(a, b):
    return jnp.einsum("tn,mn->tm", a, b, preferred_element_type=jnp.float32)


def normalise(values, gain):
    scale = lax.rsqrt(jnp.mean(values * values, -1, keepdims=True) + EPS)
    return (values * scale * gain).astype(jnp.bfloat16)


def normalise_back(values, gain, grad):
    scale = lax.rsqrt(jnp.mean(values * values, -1, keepdims=True) + EPS)
    gain_grad = jnp.sum(grad * values * scale, 0)
    pulled = grad * gain
    return scale * pulled - values * (scale**3 * jnp.mean(pulled * values, -1, keepdims=True)), gain_grad


def padded(rows, width):
    table = jnp.stack([jnp.pad(row, (0, width - row.shape[0])) for row in rows])
    return jnp.pad(table, ((0, 8 - len(rows)), (0, 0)))


def local(
    inputs,
    lengths,
    norm_gain,
    in_weight,
    conv_weight,
    conv_bias,
    log_decay,
    dt_bias,
    skip,
    gate_gain,
    out_weight,
    cotangent,
):
    _, span, width = inputs.shape
    peers = lax.axis_size("seq")
    aux, auxr = token_marks(lengths[0], span)
    order = slab_order()
    hidden = inputs[0]
    saved = []
    for depth in range(LAYERS):
        conv = jnp.concatenate([conv_weight[depth].T, conv_bias[depth][None], jnp.zeros((3, CHANNELS), jnp.float32)])
        hp = padded([dt_bias[depth], -jnp.exp(log_decay[depth])], 128)
        ch = padded([jnp.repeat(skip[depth], HEAD_DIM), gate_gain[depth]], DI)
        gate_weight = in_weight[depth][:, :DI]
        mixed_weight = in_weight[depth][:, DI : DI + CHANNELS]
        rate_weight = jnp.pad(in_weight[depth][:, DI + CHANNELS :], ((0, 0), (0, 128 - HEADS)))
        before = shifted(hidden[span - HALO :], 1)
        normed = normalise(hidden, norm_gain[depth])
        normed_ext = jnp.concatenate([normalise(before, norm_gain[depth]), normed])
        mixed_ext = matmul(normed_ext, mixed_weight)
        rate = matmul(normed, rate_weight)
        gate = matmul(normed, gate_weight)
        values, bc, col, cumr, made, kx, pay = make_states(peers, mixed_ext, rate, aux, conv, hp)
        received = exchange(pay)
        yi = inner(bc, values, col, cumr, aux, auxr)
        keeps = received[:, -8:]
        state_in = exchange(scan_states(received, keeps, False)).reshape(DI // 128, STATE, 128)
        y, out_low = finish(yi, values, gate, bc, col, state_in, made, kx, ch)
        saved.append(
            (hidden, normed, mixed_ext, rate, gate, values, bc, col, cumr, made, kx, keeps, state_in, y, out_low, yi)
            + (conv, hp, ch, gate_weight, mixed_weight, rate_weight)
        )
        hidden = hidden + matmul(out_low, out_weight[depth])
    gradient = cotangent[0]
    collected = [None] * LAYERS
    parts = [None] * LAYERS
    earlier = None
    for depth in reversed(range(LAYERS)):
        entry, normed, mixed_ext, rate, gate, values, bc, col, cumr, made, kx, keeps, state_in, y, out_low, yi = saved[depth][:16]
        conv, hp, ch, gate_weight, mixed_weight, rate_weight = saved[depth][16:]
        grad_low = gradient.astype(jnp.bfloat16)
        dno = matmul_nt(grad_low, out_weight[depth])
        waits = () if earlier is None else steps(*earlier[:2])
        dy, dgate, gate_sums, d1, pay = gate_back(peers, dno, y, gate, values, bc, col, kx, ch, after=waits)
        received = exchange(pay)
        normed_sorted = in_order(normed, order)
        if earlier is not None:
            parts[depth + 1] = earlier = earlier[:2] + (Scatter(normed_sorted_before, dmixed),)
        out_part = Scatter(in_order(out_low, order), grad_low)
        gate_part = Scatter(normed_sorted, dgate)
        waits = (out_part.send, out_part.keep, gate_part.send, gate_part.keep)
        if earlier is not None:
            waits += (earlier[2].send, earlier[2].keep) + steps(*earlier[:2])
        scanned = scan_states(received, keeps, True, after=waits)
        dso = exchange(scanned).reshape(DI // 128, STATE, 128)
        waits = steps(out_part, gate_part)
        if earlier is not None:
            waits += steps(earlier[2])
        xi, dbc = inner_back(bc, values, dy, col, cumr, aux, auxr, after=waits)
        waits = () if earlier is None else steps(*earlier)
        dconv, dconv_bc, drate, head_rows = states_back(
            xi, values, dy, yi, mixed_ext, bc, col, dso, state_in, made, d1, kx, dbc, aux, conv, ch, hp, rate,
            after=waits,
        )
        following = shifted(jnp.concatenate([dconv[:HALO], dconv_bc[:HALO]], 1), -1)
        waits = steps(out_part, gate_part) + (() if earlier is None else steps(earlier[2]))
        dmixed, conv_sums = conv_back(dconv, dconv_bc, following, mixed_ext, aux, conv, after=waits)
        dmixed = jnp.concatenate([dmixed, drate[:, :HEADS]], 1)
        normed_sorted_before = normed_sorted
        earlier = (out_part, gate_part)
        parts[depth] = earlier
        if depth == 0:
            parts[depth] = earlier + (Scatter(normed_sorted, dmixed),)
        grad_normed = matmul_nt(dgate, gate_weight) + matmul_nt(dmixed, in_weight[depth][:, DI:])
        grad_hidden, gain_grad = normalise_back(entry, norm_gain[depth], grad_normed)
        gradient = gradient + grad_hidden
        collected[depth] = (
            gain_grad,
            conv_sums[:KW].T,
            conv_sums[KW],
            gate_sums[0],
            head_rows[1, :HEADS],
            head_rows[0, :HEADS],
            jnp.sum(gate_sums[1].reshape(HEADS, HEAD_DIM), 1),
        )
    big_out = [trio[0].result() for trio in parts]
    big_in = [jnp.concatenate([trio[1].result(), trio[2].result()], 1) for trio in parts]
    devices = lax.axis_size(AXES)
    shares = [part.reshape(devices, -1) for sums in collected for part in sums[:4]]
    heads = jnp.concatenate([part for sums in collected for part in sums[4:]])
    table = jnp.concatenate(shares + [jnp.broadcast_to(heads, (devices,) + heads.shape)], 1)
    table = jnp.pad(table, ((0, 0), (0, -table.shape[1] % 128)))
    table = lax.all_to_all(table, AXES, split_axis=0, concat_axis=0, tiled=True).reshape(devices, -1, 128)
    table = pcall(
        total_kernel,
        (1,),
        [full(table.shape)],
        full(table.shape[1:]),
        shape_of(table.shape[1:]),
        [],
        (table,),
        after=tuple(big_in + big_out),
    ).reshape(-1)
    small = []
    at = 0
    for sums in collected:
        row = []
        for part in sums[:4]:
            size = part.size // devices
            row.append(table[at : at + size].reshape((part.shape[0] // devices,) + part.shape[1:]))
            at += size
        small.append(row)
    for row in small:
        for _ in range(3):
            row.append(table[at : at + HEADS])
            at += HEADS
    stacked = [jnp.stack([small[level][member] for level in range(LAYERS)]) for member in range(7)]
    norm_gain_grad, conv_w_grad, conv_b_grad, gain_grad, decay_grad, bias_grad, skip_grad = stacked
    return (
        hidden[None],
        gradient[None],
        norm_gain_grad,
        jnp.stack(big_in),
        conv_w_grad,
        conv_b_grad,
        decay_grad,
        bias_grad,
        skip_grad,
        gain_grad,
        jnp.stack(big_out),
    )


def solution(mesh):
    in_specs = (
        P("rows", "seq", None),
        P("rows", None),
        P(),
        P(),
        P(),
        P(),
        P(),
        P(),
        P(),
        P(),
        P(),
        P("rows", "seq", None),
    )
    out_specs = (
        P("rows", "seq", None),
        P("rows", "seq", None),
        P(None, ("seq", "rows")),
        P(None, ("seq", "rows"), None),
        P(None, ("seq", "rows"), None),
        P(None, ("seq", "rows")),
        P(),
        P(),
        P(),
        P(None, ("seq", "rows")),
        P(None, ("seq", "rows"), None),
    )
    return jax.shard_map(local, mesh=mesh, in_specs=in_specs, out_specs=out_specs, check_vma=False)
```

```python
from functools import partial

import jax
import jax.numpy as jnp
from jax import lax
from jax.experimental import pallas as pl
from jax.experimental.pallas import tpu as pltpu
from jax.sharding import PartitionSpec as P

DI = 2048
STATE = 128
HEAD_DIM = 64
HEADS = DI // HEAD_DIM
KW = 4
GROUP = 256
LAYERS = 2
CHANNELS = DI + 2 * STATE
TILE = 512
HEADS_AT = TILE // HEAD_DIM
MAPS = 2 * STATE
ROWS_STEP = 128
SUM_ROWS = 512
LAG = 2
AHEAD = 4
HALO = 8
HALF = 128
LOG2E = 1.4426950408889634
ROWS_AT = 64
VMEM_BYTES = 48 * 1024 * 1024

EPS = 1e-05
HIGHEST = lax.Precision.HIGHEST
AXES = ("seq", "rows")


def pcall(body, grid, in_specs, out_specs, out_shape, scratch, args, flops=0, nbytes=0, after=()):
    taken = len(args)

    def run(*refs):
        body(*refs[:taken], *refs[taken + len(after) :])

    return pl.pallas_call(
        run,
        grid=grid,
        in_specs=list(in_specs) + [pl.BlockSpec(memory_space=pltpu.HBM)] * len(after),
        out_specs=out_specs,
        out_shape=out_shape,
        scratch_shapes=scratch,
        compiler_params=pltpu.CompilerParams(vmem_limit_bytes=VMEM_BYTES),
        cost_estimate=pl.CostEstimate(flops=flops, bytes_accessed=nbytes, transcendentals=0),
    )(*args, *after)


def dot(a, b, dims=(((1,), (0,)), ((), ()))):
    return lax.dot_general(
        a.astype(jnp.bfloat16), b.astype(jnp.bfloat16), dims, preferred_element_type=jnp.float32
    )


def dot_nt(a, b):
    return dot(a, b, (((1,), (1,)), ((), ())))


def dot_exact(a, b):
    return jnp.dot(a, b, precision=HIGHEST, preferred_element_type=jnp.float32)


def sigmoid(v):
    return 0.5 * jnp.tanh(0.5 * v) + 0.5


def lane_iota(shape):
    return lax.broadcasted_iota(jnp.int32, shape, 1)


def low_half(rows):
    return lane_iota((rows, 128)) < HEAD_DIM


def to_heads(cols, first, pairs):
    rows = cols.shape[0]
    low = low_half(rows)
    parts = []
    for pair in range(pairs):
        at = first + 2 * pair
        parts.append(
            jnp.where(
                low,
                jnp.broadcast_to(cols[:, at : at + 1], (rows, 128)),
                jnp.broadcast_to(cols[:, at + 1 : at + 2], (rows, 128)),
            )
        )
    return jnp.concatenate(parts, 1) if pairs > 1 else parts[0]


def spread_heads(cols, pairs):
    pick = (
        lax.broadcasted_iota(jnp.int32, (128, 128 * pairs), 0) == lane_iota((128, 128 * pairs)) // HEAD_DIM
    ).astype(jnp.bfloat16)
    high = cols.astype(jnp.bfloat16)
    return dot(high, pick) + dot(cols - high.astype(jnp.float32), pick)


def head_pick(first, heads):
    shape = (128, HEAD_DIM * heads)
    return (lax.broadcasted_iota(jnp.int32, shape, 0) == first + lane_iota(shape) // HEAD_DIM).astype(jnp.bfloat16)


def picked_heads(cols, pick):
    high = cols.astype(jnp.bfloat16)
    return dot(high, pick) + dot(cols - high.astype(jnp.float32), pick)


def head_sums(first):
    channel = lax.broadcasted_iota(jnp.int32, (TILE, 128), 0)
    return (channel // HEAD_DIM + first == lane_iota((TILE, 128))).astype(jnp.bfloat16)


def keep_marks(marks_ref, aux_ref, lanes):
    for at, lane in enumerate(lanes):
        marks_ref[at] = jnp.broadcast_to(aux_ref[:, lane : lane + 1], marks_ref.shape[1:])


def conv_rows(x_ref, w_ref, marks_ref, first, count, lanes):
    total = w_ref[4:5, lanes] + w_ref[3:4, lanes] * x_ref[first + 8 : first + 8 + count, lanes]
    for tap in range(KW - 1):
        match = marks_ref[tap, first : first + count, :]
        total = total + w_ref[tap : tap + 1, lanes] * (x_ref[first + 5 + tap : first + 5 + tap + count, lanes] * match)
    return total


def chunks_of(rows, width):
    for pair in range(width // 128):
        for first in range(0, rows, ROWS_AT):
            yield first, slice(first, first + ROWS_AT), slice(pair * 128, (pair + 1) * 128)


def states_kernel(
    x_ref, xbc_ref, rate_ref, aux_ref, w_ref, wbc_ref, hp_ref,
    v_ref, bc_ref, col_ref, cumr_ref, made_ref, kx_ref, pay_ref,
    bt_ref, marks_ref,
):
    turn = pl.program_id(0)
    span = rate_ref.shape[0]
    count = span // GROUP

    @pl.when(turn == 0)
    def _():
        keep_marks(marks_ref, aux_ref, range(KW - 1))
        for first, rows, lanes in chunks_of(span, MAPS):
            conv = conv_rows(xbc_ref, wbc_ref, marks_ref, first, ROWS_AT, lanes)
            bc_ref[rows, lanes] = conv * sigmoid(conv)
        tri = (
            lax.broadcasted_iota(jnp.int32, (GROUP, GROUP), 0) >= lane_iota((GROUP, GROUP))
        ).astype(jnp.float32)
        for block in range(count):
            rows = slice(block * GROUP, (block + 1) * GROUP)
            bt_ref[block] = bc_ref[rows, :STATE].T.astype(jnp.bfloat16)
            raw = rate_ref[rows, :] + hp_ref[0:1, :]
            step = jnp.maximum(raw, 0.0) + jnp.log1p(jnp.exp(-jnp.abs(raw)))
            cum = dot_exact(tri, hp_ref[1:2, :] * step)
            last = cum[GROUP - 1 :, :]
            col_ref[0, rows, :] = cum
            col_ref[1, rows, :] = step
            col_ref[2, rows, :] = jnp.exp(cum) * aux_ref[rows, 3:4]
            col_ref[3, rows, :] = jnp.exp(last - cum) * aux_ref[rows, 4:5]
            cumr_ref[:, rows] = cum.T

    for first, rows, lanes in chunks_of(span, TILE):
        conv = conv_rows(x_ref, w_ref, marks_ref, first, ROWS_AT, lanes)
        v_ref[rows, lanes] = conv * sigmoid(conv)
    pick = head_pick(turn * HEADS_AT, HEADS_AT)
    made = []
    keep = []
    for block in range(count):
        rows = slice(block * GROUP, (block + 1) * GROUP)
        weight = picked_heads(col_ref[3, rows, :] * col_ref[1, rows, :], pick)
        made.append(dot(bt_ref[block], weight * v_ref[rows, :]))
        ends = col_ref[2, (block + 1) * GROUP - 8 : (block + 1) * GROUP, :]
        keep.append(picked_heads(ends, pick)[7:8, :])
    made_ref[...] = made[0]
    kx_ref[...] = jnp.concatenate([keep[0], keep[1], jnp.zeros((6, TILE), jnp.float32)], 0)
    final = keep[1] * made[0] + made[1]
    total = jnp.broadcast_to(keep[0] * keep[1], (8, TILE))
    pairs = TILE // 128
    chunks = pay_ref.shape[0] // pairs
    size = STATE // chunks
    for pair in range(pairs):
        lanes = slice(pair * 128, (pair + 1) * 128)
        for chunk in range(chunks):
            pay_ref[pair * chunks + chunk, :size, :] = final[chunk * size : (chunk + 1) * size, lanes]
            pay_ref[pair * chunks + chunk, size:, :] = total[:, lanes]


def inner_kernel(bc_ref, v_ref, col_ref, cumr_ref, aux_ref, auxr_ref, y_ref, g_ref):
    scores = dot_nt(bc_ref[:, STATE:], bc_ref[:, :STATE])
    allowed = (aux_ref[:, 5:6] == auxr_ref[0:1, :]) & (
        lax.broadcasted_iota(jnp.int32, (GROUP, GROUP), 0) >= lane_iota((GROUP, GROUP))
    )
    g_ref[...] = jnp.where(allowed, scores, 0.0)
    low = low_half(GROUP)
    cum = LOG2E * col_ref[0]
    cum_row = LOG2E * cumr_ref[:HEADS, :]
    steps = picked_heads(col_ref[1], head_pick(0, HEADS))
    for pair in range(HEADS // 2):
        lanes = slice(pair * 128, (pair + 1) * 128)
        scaled = steps[:, lanes] * v_ref[:, lanes]
        result = None
        for half in range(2):
            head = 2 * pair + half
            row = cum_row[head : head + 1, :]
            tops, bottoms = [], []
            for first in range(0, GROUP, 64):
                width = HALF if first < HALF else GROUP
                spread = cum[first : first + 64, head : head + 1] - row[:, :width]
                decay = jnp.exp2(jnp.minimum(spread, 0.0))
                mixing = (g_ref[first : first + 64, :width] * decay).astype(jnp.bfloat16)
                (tops if first < HALF else bottoms).append(mixing)
            picked = jnp.where(low if half == 0 else ~low, scaled, 0.0).astype(jnp.bfloat16)
            top = dot(jnp.concatenate(tops, 0), picked[:HALF])
            bottom = dot(jnp.concatenate(bottoms, 0), picked)
            result = (top, bottom) if result is None else (result[0] + top, result[1] + bottom)
        y_ref[:HALF, lanes] = result[0]
        y_ref[HALF:, lanes] = result[1]


def finish_kernel(
    yi_ref, v_ref, gate_ref, bc_ref, col_ref, sin_ref, made_ref, kx_ref, ch_ref,
    y_ref, out_ref,
    gated_ref,
):
    later = pl.program_id(0) * ROWS_STEP >= GROUP
    out_map = bc_ref[:, STATE:].astype(jnp.bfloat16)
    entering = picked_heads(col_ref[2], head_pick(0, HEADS))
    total = [jnp.zeros((ROWS_AT, 128), jnp.float32) for _ in range(ROWS_STEP // ROWS_AT)]
    for pair in range(HEADS // 2):
        lanes = slice(pair * 128, (pair + 1) * 128)
        state = sin_ref[pair]
        state = jnp.where(later, kx_ref[0:1, lanes] * state + made_ref[:, lanes], state)
        outer = entering[:, lanes] * dot(out_map, state)
        for at in range(ROWS_STEP // ROWS_AT):
            rows = slice(at * ROWS_AT, (at + 1) * ROWS_AT)
            result = yi_ref[rows, lanes] + outer[rows] + ch_ref[0:1, lanes] * v_ref[rows, lanes]
            y_ref[rows, lanes] = result
            gate = gate_ref[rows, lanes]
            gated = result * (gate * sigmoid(gate))
            gated_ref[rows, lanes] = gated
            total[at] = total[at] + gated * gated
    for at in range(ROWS_STEP // ROWS_AT):
        rows = slice(at * ROWS_AT, (at + 1) * ROWS_AT)
        scale = lax.rsqrt(jnp.sum(total[at], 1, keepdims=True) / DI + EPS)
        out_ref[rows, :] = (gated_ref[rows, :] * scale * ch_ref[1:2, :]).astype(jnp.bfloat16)


def gate_back_kernel(
    dno_ref, y_ref, gate_ref, v_ref, bc_ref, col_ref, kx_ref, ch_ref,
    dy_ref, dgate_ref, sum_ref, d1_ref, pay_ref,
    gated_ref, silu_ref,
):
    at_step = pl.program_id(0)
    later = at_step * ROWS_STEP >= GROUP
    parts = ROWS_STEP // ROWS_AT
    square = [jnp.zeros((ROWS_AT, 128), jnp.float32) for _ in range(parts)]
    cross = [jnp.zeros((ROWS_AT, 128), jnp.float32) for _ in range(parts)]
    for first, rows, lanes in chunks_of(ROWS_STEP, DI):
        gate = gate_ref[rows, lanes]
        sig = sigmoid(gate)
        silu = gate * sig
        y = y_ref[rows, lanes]
        gated = y * silu
        gated_ref[rows, lanes] = gated
        silu_ref[0, rows, lanes] = silu
        silu_ref[1, rows, lanes] = y * (sig * (1.0 + gate * (1.0 - sig)))
        at = first // ROWS_AT
        square[at] = square[at] + gated * gated
        cross[at] = cross[at] + gated * (dno_ref[rows, lanes] * ch_ref[1:2, lanes])
    scales = [lax.rsqrt(jnp.sum(part, 1, keepdims=True) / DI + EPS) for part in square]
    pulls = [scale * scale * scale * (jnp.sum(part, 1, keepdims=True) / DI) for scale, part in zip(scales, cross)]
    out_t = bc_ref[:, STATE:].T.astype(jnp.bfloat16)
    entering = picked_heads(col_ref[2], head_pick(0, HEADS))
    pairs = DI // 128
    chunks = pay_ref.shape[0] // pairs
    size = STATE // chunks

    @pl.when(at_step == 0)
    def _():
        sum_ref[...] = jnp.zeros_like(sum_ref)
        pay_ref[...] = jnp.zeros_like(pay_ref)

    @pl.when((at_step == 0) | (at_step * ROWS_STEP == GROUP))
    def _():
        d1_ref[...] = jnp.zeros_like(d1_ref)

    for pair in range(pairs):
        lanes = slice(pair * 128, (pair + 1) * 128)
        gain_sum = jnp.zeros((8, 128), jnp.float32)
        skip_sum = jnp.zeros((8, 128), jnp.float32)
        weighted = []
        for at in range(parts):
            rows = slice(at * ROWS_AT, (at + 1) * ROWS_AT)
            gated = gated_ref[rows, lanes]
            dno = dno_ref[rows, lanes] * scales[at]
            dgated = dno * ch_ref[1:2, lanes] - gated * pulls[at]
            dy = dgated * silu_ref[0, rows, lanes]
            dy_ref[rows, lanes] = dy
            dgate_ref[rows, lanes] = (dgated * silu_ref[1, rows, lanes]).astype(jnp.bfloat16)
            gain_sum = gain_sum + jnp.sum((dno * gated).reshape(-1, 8, 128), 0)
            skip_sum = skip_sum + jnp.sum((dy * v_ref[rows, lanes]).reshape(-1, 8, 128), 0)
            weighted.append((entering[rows, lanes] * dy).astype(jnp.bfloat16))
        sum_ref[0:1, lanes] += jnp.sum(gain_sum, 0, keepdims=True)
        sum_ref[1:2, lanes] += jnp.sum(skip_sum, 0, keepdims=True)
        fresh = dot(out_t, jnp.concatenate(weighted, 0))
        d1_ref[:, lanes] += fresh
        more = jnp.where(later, kx_ref[0:1, lanes], 1.0) * fresh
        for chunk in range(chunks):
            pay_ref[pair * chunks + chunk] += more[chunk * size : (chunk + 1) * size]


def inner_back_kernel(
    bc_ref, v_ref, dy_ref, col_ref, cumr_ref, aux_ref, auxr_ref,
    x_ref, dbc_ref,
    g_ref, dg_ref,
):
    allowed = (aux_ref[:, 5:6] == auxr_ref[0:1, :]) & (
        lax.broadcasted_iota(jnp.int32, (GROUP, GROUP), 0) <= lane_iota((GROUP, GROUP))
    )
    g_ref[...] = jnp.where(allowed, dot_nt(bc_ref[:, :STATE], bc_ref[:, STATE:]), 0.0)
    dg_ref[...] = jnp.zeros_like(dg_ref)
    low = low_half(GROUP)
    cum = LOG2E * col_ref[0]
    cum_row = LOG2E * cumr_ref[:HEADS, :]
    steps = picked_heads(col_ref[1], head_pick(0, HEADS))
    for pair in range(HEADS // 2):
        lanes = slice(pair * 128, (pair + 1) * 128)
        scaled = steps[:, lanes] * v_ref[:, lanes]
        dy = dy_ref[:, lanes]
        dy_low = dy.astype(jnp.bfloat16)
        result = None
        grads = {}
        for half in range(2):
            head = 2 * pair + half
            row = cum_row[head : head + 1, :]
            mine = low if half == 0 else ~low
            picked = jnp.where(mine, scaled, 0.0).astype(jnp.bfloat16)
            top_grad = dot_nt(picked[:HALF], dy_low)
            bottom_grad = dot_nt(picked[HALF:], dy_low[HALF:])
            tops, bottoms = [], []
            for first in range(0, GROUP, 64):
                rows = slice(first, first + 64)
                top = first < HALF
                across = slice(0 if top else HALF, GROUP)
                spread = row[:, across] - cum[rows, head : head + 1]
                decay = jnp.exp2(jnp.minimum(spread, 0.0))
                (tops if top else bottoms).append((g_ref[rows, across] * decay).astype(jnp.bfloat16))
                part = (top_grad[rows] if top else bottom_grad[first - HALF : first - HALF + 64]) * decay
                if half == 0:
                    grads[first] = part
                else:
                    dg_ref[rows, across] += grads[first] + part
            dy_mine = jnp.where(mine, dy, 0.0).astype(jnp.bfloat16)
            top = dot(jnp.concatenate(tops, 0), dy_mine)
            bottom = dot(jnp.concatenate(bottoms, 0), dy_mine[HALF:])
            result = (top, bottom) if result is None else (result[0] + top, result[1] + bottom)
        x_ref[:HALF, lanes] = result[0]
        x_ref[HALF:, lanes] = result[1]
    dg = jnp.where(allowed, dg_ref[...], 0.0)
    dbc_ref[:, :STATE] = dot(dg, bc_ref[:, STATE:])
    dbc_ref[:, STATE:] = dot(dg.T, bc_ref[:, :STATE])


def states_back_kernel(
    xi_ref, v_ref, dy_ref, yi_ref, x_ref, xbc_ref, bc_ref, col_ref, dso_ref, sin_ref, made_ref, d1_ref,
    kx_ref, dbc_ref, aux_ref, w_ref, wbc_ref, ch_ref, hp_ref, rate_ref,
    dconv_ref, dconv_bc_ref, drate_ref, sum_ref,
    ds_ref, dc_ref, z_ref, kd_ref, dmap_ref, marks_ref,
):
    turn = pl.program_id(0)
    span = v_ref.shape[0]
    count = span // GROUP

    @pl.when(turn == 0)
    def _():
        keep_marks(marks_ref, aux_ref, range(KW - 1))
        ds_ref[...] = jnp.zeros_like(ds_ref)
        dc_ref[...] = jnp.zeros_like(dc_ref)
        z_ref[...] = jnp.zeros_like(z_ref)
        kd_ref[...] = jnp.zeros_like(kd_ref)
        dmap_ref[...] = dbc_ref[...]

    sums = head_sums(turn * HEADS_AT)
    pick = head_pick(turn * HEADS_AT, HEADS_AT)
    end_grad = jnp.concatenate([dso_ref[pair] for pair in range(TILE // 128)], 1)
    state = jnp.concatenate([sin_ref[pair] for pair in range(TILE // 128)], 1)
    ends = [d1_ref[...] + kx_ref[1:2, :] * end_grad, end_grad]
    starts = [state, kx_ref[0:1, :] * state + made_ref[...]]
    for block in range(count):
        at = slice(block * GROUP, (block + 1) * GROUP)
        step = picked_heads(col_ref[1, at, :], pick)
        entering = picked_heads(col_ref[2, at, :], pick)
        tail = picked_heads(col_ref[3, at, :], pick)
        from_end = dot(bc_ref[at, :STATE], ends[block])
        outer = dot(bc_ref[at, STATE:], starts[block])
        kinds = {name: [] for name in ("ds", "z", "dc", "low", "values", "dy")}
        for first in range(0, GROUP, ROWS_AT):
            local = slice(first, first + ROWS_AT)
            rows = slice(block * GROUP + first, block * GROUP + first + ROWS_AT)
            pieces = {name: [] for name in kinds}
            for pair in range(TILE // 128):
                lanes = slice(pair * 128, (pair + 1) * 128)
                v = v_ref[rows, lanes]
                dy = dy_ref[rows, lanes]
                xi = xi_ref[rows, lanes]
                scaled = step[local, lanes] * v
                low = dy.astype(jnp.bfloat16).astype(jnp.float32)
                inside = low * yi_ref[rows, lanes] - scaled.astype(jnp.bfloat16).astype(jnp.float32) * xi
                ended = tail[local, lanes] * from_end[local, lanes]
                inside = inside + dy * (entering[local, lanes] * outer[local, lanes])
                pulled = xi + ended
                high = inside.astype(jnp.bfloat16)
                pieces["dc"].append(high)
                pieces["low"].append((inside - high.astype(jnp.float32)).astype(jnp.bfloat16))
                pieces["ds"].append((v * pulled).astype(jnp.bfloat16))
                pieces["z"].append((scaled * ended).astype(jnp.bfloat16))
                pieces["values"].append((tail[local, lanes] * scaled).astype(jnp.bfloat16))
                pieces["dy"].append((entering[local, lanes] * dy).astype(jnp.bfloat16))
                grad = step[local, lanes] * pulled + ch_ref[0:1, lanes] * dy
                conv = conv_rows(x_ref, w_ref, marks_ref, block * GROUP + first, ROWS_AT, lanes)
                sig = sigmoid(conv)
                dconv_ref[rows, lanes] = grad * (sig * (1.0 + conv * (1.0 - sig)))
            for name in kinds:
                kinds[name].append(jnp.concatenate(pieces[name], 1))
        whole = {name: jnp.concatenate(parts, 0) for name, parts in kinds.items()}
        ds_ref[at, :] += dot(whole["ds"], sums)
        z_ref[at, :] += dot(whole["z"], sums)
        dc_ref[at, :] += dot(whole["dc"], sums) + dot(whole["low"], sums)
        dmap_ref[at, :STATE] += dot_nt(whole["values"], ends[block])
        dmap_ref[at, STATE:] += dot_nt(whole["dy"], starts[block])
        kept = kx_ref[block : block + 1, :] * jnp.sum(ends[block] * starts[block], 0, keepdims=True)
        kd_ref[block] += dot_exact(jnp.broadcast_to(kept, (8, TILE)), sums.astype(jnp.float32))

    @pl.when(turn == pl.num_programs(0) - 1)
    def _():
        here = lax.broadcasted_iota(jnp.int32, (GROUP, GROUP), 0)
        after = (here <= lane_iota((GROUP, GROUP))).astype(jnp.float32)
        before = (here > lane_iota((GROUP, GROUP))).astype(jnp.float32)
        bias_sum = jnp.zeros((1, 128), jnp.float32)
        decay_sum = jnp.zeros((1, 128), jnp.float32)
        for first, rows, lanes in chunks_of(span, MAPS):
            conv = conv_rows(xbc_ref, wbc_ref, marks_ref, first, ROWS_AT, lanes)
            sig = sigmoid(conv)
            dconv_bc_ref[rows, lanes] = dmap_ref[rows, lanes] * (sig * (1.0 + conv * (1.0 - sig)))
        for block in range(count):
            rows = slice(block * GROUP, (block + 1) * GROUP)
            z = z_ref[rows, :]
            da = dot_exact(after, dc_ref[rows, :]) + kd_ref[block, 0:1, :]
            da = da + dot_exact(before, z)
            ds = ds_ref[rows, :] + hp_ref[1:2, :] * da
            drate = ds * sigmoid(rate_ref[rows, :] + hp_ref[0:1, :])
            drate_ref[rows, :] = drate.astype(jnp.bfloat16)
            bias_sum = bias_sum + jnp.sum(drate, 0, keepdims=True)
            decay_sum = decay_sum + jnp.sum(da * hp_ref[1:2, :] * col_ref[1, rows, :], 0, keepdims=True)
        sum_ref[...] = jnp.concatenate([bias_sum, decay_sum, jnp.zeros((6, 128), jnp.float32)], 0)


def conv_back_kernel(
    dconv_ref, dconv_bc_ref, drate_ref, next_ref, x_ref, aux_ref, w_ref, dx_ref, sum_ref, ext_ref, marks_ref
):
    turn = pl.program_id(0)
    last = pl.num_programs(0) - 1
    span = dconv_ref.shape[0]

    @pl.when(turn == 0)
    def _():
        keep_marks(marks_ref, aux_ref, (0, 1, 2, 6, 7, 8))

    @pl.when(turn < last)
    def _():
        ext_ref[:span, :] = dconv_ref[...]

    @pl.when(turn == last)
    def _():
        ext_ref[:span, :MAPS] = dconv_bc_ref[...]

    ext_ref[span:, :] = next_ref[...]
    for pair in range(TILE // 128):
        lanes = slice(pair * 128, (pair + 1) * 128)
        sums = [jnp.zeros((8, 128), jnp.float32) for _ in range(KW + 1)]
        for first in range(0, span, ROWS_AT):
            rows = slice(first, first + ROWS_AT)
            here = ext_ref[rows, lanes]
            grad = w_ref[3:4, lanes] * here
            for ahead in range(1, KW):
                shifted_grad = ext_ref[first + ahead : first + ahead + ROWS_AT, lanes]
                grad = grad + w_ref[3 - ahead : 4 - ahead, lanes] * (shifted_grad * marks_ref[2 + ahead, rows, :])
            dx_ref[rows, lanes] = grad.astype(jnp.bfloat16)
            for tap in range(KW):
                term = here * x_ref[first + 5 + tap : first + 5 + tap + ROWS_AT, lanes]
                if tap < KW - 1:
                    term = term * marks_ref[tap, rows, :]
                sums[tap] = sums[tap] + jnp.sum(term.reshape(-1, 8, 128), 0)
            sums[KW] = sums[KW] + jnp.sum(here.reshape(-1, 8, 128), 0)
        sums = [jnp.sum(part, 0, keepdims=True) for part in sums]
        sum_ref[:, lanes] = jnp.concatenate(sums + [jnp.zeros((3, 128), jnp.float32)], 0)

    @pl.when(turn == last)
    def _():
        dx_ref[:, MAPS : MAPS + 128] = drate_ref[...]
        dx_ref[:, MAPS + 128 :] = jnp.zeros_like(drate_ref)


def scan_kernel(reverse, rows, in_ref, keep_ref, out_ref):
    peers = out_ref.shape[0]
    carried = jnp.zeros((rows, 128), jnp.float32)
    for at in range(peers):
        peer = peers - 1 - at if reverse else at
        out_ref[peer] = carried
        carried = keep_ref[peer, 0:1, :] * carried + in_ref[peer, :rows, :]


def total_kernel(in_ref, out_ref):
    out_ref[...] = jnp.sum(in_ref[...], 0)


def weight_kernel(each, left_ref, right_ref, send_ref, keep_ref):
    slabs, size = send_ref.shape[0], SUM_ROWS
    total = dot(left_ref[...], right_ref[...])
    half = total.shape[0] // 2
    for out_ref, rows in ((keep_ref, total[:half]), (send_ref, total[half:])):
        if slabs == 1:
            out_ref[0] = rows
        else:
            split = rows.reshape(-1, slabs, each // slabs, rows.shape[1])
            for part in range(slabs):
                out_ref[part] = split[:, part].reshape(size, rows.shape[1])


def sums_kernel(counts, masks, *refs):
    pieces = len(counts)
    sends, keeps, out_ref, kept_ref = refs[:pieces], refs[pieces : 2 * pieces], refs[2 * pieces], refs[2 * pieces + 1]
    stages = len(masks)
    got = refs[2 * pieces + 2 : 2 * pieces + 2 + stages]
    load_sem, send_sem, recv_sem = refs[2 * pieces + 2 + stages :]
    chunks = sum(counts)
    seq, row = lax.axis_index("seq"), lax.axis_index("rows")
    odd = lax.rem(row, 2)

    def over(at, mask):
        return at + mask * (1 - 2 * lax.rem(at // mask, 2))

    partners = []
    for axis, even_mask, odd_mask in masks:
        if axis == "rows":
            partners.append({"seq": seq, "rows": over(row, even_mask)})
        else:
            one, two = over(seq, even_mask), over(seq, odd_mask)
            partners.append({"seq": one + odd * (two - one), "rows": row})

    barrier = pltpu.get_barrier_semaphore()
    for partner in partners:
        pl.semaphore_signal(barrier, inc=1, device_id=partner, device_id_type=pl.DeviceIdType.MESH)
    pl.semaphore_wait(barrier, stages)

    def copy(stage, chunk, source=None):
        size = SUM_ROWS >> stage
        if source is None:
            source = kept_ref.at[chunk] if stage == 0 else kept_ref.at[chunk, pl.ds(size, size)]
        return pltpu.make_async_remote_copy(
            src_ref=source,
            dst_ref=got[stage].at[chunk],
            send_sem=send_sem.at[stage, chunk],
            recv_sem=recv_sem.at[stage, chunk],
            device_id=partners[stage],
            device_id_type=pl.DeviceIdType.MESH,
        )

    def load(chunk, source):
        return pltpu.make_async_copy(source, kept_ref.at[chunk], load_sem.at[chunk])

    def begin(chunk):
        base = 0
        for count, send_ref, keep_ref in zip(counts, sends, keeps):

            @pl.when((chunk >= base) & (chunk < base + count))
            def _(base=base, send_ref=send_ref, keep_ref=keep_ref):
                copy(0, chunk, send_ref.at[chunk - base]).start()
                load(chunk, keep_ref.at[chunk - base]).start()

            base += count

    def first(chunk, _):
        begin(chunk)
        return 0

    lax.fori_loop(0, AHEAD, first, 0)

    def turn(at, _):
        begin(at + AHEAD)
        for stage in range(stages):
            chunk = at - LAG * stage

            @pl.when((chunk >= 0) & (chunk < chunks))
            def _():
                size = SUM_ROWS >> stage
                if stage == 0:
                    load(chunk, keeps[0].at[0]).wait()
                copy(stage, chunk, sends[0].at[0] if stage == 0 else None).wait_recv()
                total = kept_ref[chunk, :size] + got[stage][chunk]
                if stage + 1 < stages:
                    kept_ref[chunk, :size] = total
                    copy(stage + 1, chunk).start()
                else:
                    out_ref[chunk] = total

        return 0

    lax.fori_loop(0, chunks + LAG * (stages - 1), turn, 0)

    def ended(chunk, _):
        for stage in range(stages):
            copy(stage, chunk, sends[0].at[0] if stage == 0 else None).wait_send()
        return 0

    lax.fori_loop(0, chunks, ended, 0)


def full(shape):
    return pl.BlockSpec(shape, lambda *at: (0,) * len(shape))


def shape_of(dims, dtype=jnp.float32):
    return jax.ShapeDtypeStruct(dims, dtype)


def vmem(dims, dtype=jnp.float32):
    return pltpu.VMEM(dims, dtype)


def make_states(peers, mixed_ext, rate, aux, conv, hp):
    span = rate.shape[0]
    groups = DI // TILE
    chunks = peers * 128 // DI
    tile = lambda rows: pl.BlockSpec((rows, TILE), lambda g: (0, g))
    maps = lambda rows: pl.BlockSpec((rows, MAPS), lambda g: (0, DI // MAPS))
    pay = (TILE // 128 * chunks, STATE // chunks + 8, 128)
    return pcall(
        states_kernel,
        (groups,),
        [tile(span + HALO), maps(span + HALO), full((span, 128)), full((span, 128)), tile(8), maps(8), full((8, 128))],
        [
            tile(span),
            full((span, MAPS)),
            full((4, span, 128)),
            full((128, span)),
            tile(STATE),
            tile(8),
            pl.BlockSpec(pay, lambda g: (g, 0, 0)),
        ],
        [
            shape_of((span, DI)),
            shape_of((span, MAPS)),
            shape_of((4, span, 128)),
            shape_of((128, span)),
            shape_of((STATE, DI)),
            shape_of((8, DI)),
            shape_of((peers,) + pay[1:]),
        ],
        [vmem((span // GROUP, STATE, GROUP), jnp.bfloat16), vmem((KW - 1, span, 128))],
        (mixed_ext, mixed_ext, rate, aux, conv, conv, hp),
        flops=2 * span * DI * STATE,
        nbytes=12 * span * DI,
    )


def block_rows(span):
    wide = pl.BlockSpec((GROUP, DI), lambda b: (b, 0))
    maps = pl.BlockSpec((GROUP, MAPS), lambda b: (b, 0))
    col = pl.BlockSpec((4, GROUP, 128), lambda b: (0, b, 0))
    row = pl.BlockSpec((128, GROUP), lambda b: (0, b))
    aux = pl.BlockSpec((GROUP, 128), lambda b: (b, 0))
    auxr = pl.BlockSpec((8, GROUP), lambda b: (0, b))
    return wide, maps, col, row, aux, auxr


def inner(bc, values, col, cumr, aux, auxr):
    span = values.shape[0]
    wide, maps, cols, row, auxs, auxrs = block_rows(span)
    return pcall(
        inner_kernel,
        (span // GROUP,),
        [maps, wide, cols, row, auxs, auxrs],
        wide,
        shape_of((span, DI)),
        [vmem((GROUP, GROUP))],
        (bc, values, col, cumr, aux, auxr),
        flops=2 * span * GROUP * DI * 4,
        nbytes=8 * span * DI,
    )


def finish(yi, values, gate, bc, col, state_in, made, kx, ch):
    span = values.shape[0]
    wide = pl.BlockSpec((ROWS_STEP, DI), lambda b: (b, 0))
    maps = pl.BlockSpec((ROWS_STEP, MAPS), lambda b: (b, 0))
    cols = pl.BlockSpec((4, ROWS_STEP, 128), lambda b: (0, b, 0))
    return pcall(
        finish_kernel,
        (span // ROWS_STEP,),
        [wide, wide, wide, maps, cols, full((DI // 128, STATE, 128)), full((STATE, DI)), full((8, DI)), full((8, DI))],
        [wide, wide],
        [shape_of((span, DI)), shape_of((span, DI), jnp.bfloat16)],
        [vmem((ROWS_STEP, DI))],
        (yi, values, gate, bc, col, state_in, made, kx, ch),
        flops=2 * span * DI * STATE,
        nbytes=18 * span * DI,
    )


def gate_back(peers, dno, y, gate, values, bc, col, kx, ch, after=()):
    span = values.shape[0]
    chunks = peers * 128 // DI
    wide = pl.BlockSpec((ROWS_STEP, DI), lambda b: (b, 0))
    maps = pl.BlockSpec((ROWS_STEP, MAPS), lambda b: (b, 0))
    cols = pl.BlockSpec((4, ROWS_STEP, 128), lambda b: (0, b, 0))
    pay = (peers, STATE // chunks, 128)
    return pcall(
        gate_back_kernel,
        (span // ROWS_STEP,),
        [wide, wide, wide, wide, maps, cols, full((8, DI)), full((8, DI))],
        [wide, wide, full((8, DI)), full((STATE, DI)), full(pay)],
        [
            shape_of((span, DI)),
            shape_of((span, DI), jnp.bfloat16),
            shape_of((8, DI)),
            shape_of((STATE, DI)),
            shape_of(pay),
        ],
        [vmem((ROWS_STEP, DI)), vmem((2, ROWS_STEP, DI))],
        (dno, y, gate, values, bc, col, kx, ch),
        flops=2 * span * DI * STATE,
        nbytes=22 * span * DI,
        after=after,
    )


def inner_back(bc, values, dy, col, cumr, aux, auxr, after=()):
    span = values.shape[0]
    wide, maps, cols, row, auxs, auxrs = block_rows(span)
    return pcall(
        inner_back_kernel,
        (span // GROUP,),
        [maps, wide, wide, cols, row, auxs, auxrs],
        [wide, maps],
        [shape_of((span, DI)), shape_of((span, MAPS))],
        [vmem((GROUP, GROUP)), vmem((GROUP, GROUP))],
        (bc, values, dy, col, cumr, aux, auxr),
        flops=2 * span * GROUP * DI * 8,
        nbytes=12 * span * DI,
        after=after,
    )


def states_back(xi, values, dy, yi, mixed_ext, bc, col, dso, state_in, made, d1, kx, dbc, aux, conv, ch, hp, rate, after=()):
    span = values.shape[0]
    groups = DI // TILE
    tile = lambda rows: pl.BlockSpec((rows, TILE), lambda g: (0, g))
    maps = lambda rows: pl.BlockSpec((rows, MAPS), lambda g: (0, DI // MAPS))
    state = pl.BlockSpec((TILE // 128, STATE, 128), lambda g: (g, 0, 0))
    small = full((span, 128))
    return pcall(
        states_back_kernel,
        (groups,),
        [
            tile(span), tile(span), tile(span), tile(span), tile(span + HALO), maps(span + HALO), full((span, MAPS)),
            full((4, span, 128)), state, state, tile(STATE), tile(STATE), tile(8), full((span, MAPS)),
            small, tile(8), maps(8), tile(8), full((8, 128)), small,
        ],
        [tile(span), full((span, MAPS)), small, full((8, 128))],
        [shape_of((span, DI)), shape_of((span, MAPS)), shape_of((span, 128), jnp.bfloat16), shape_of((8, 128))],
        [vmem((span, 128)), vmem((span, 128)), vmem((span, 128)), vmem((span // GROUP, 8, 128)), vmem((span, MAPS)), vmem((KW - 1, span, 128))],
        (xi, values, dy, yi, mixed_ext, mixed_ext, bc, col, dso, state_in, made, d1, kx, dbc, aux, conv, conv, ch, hp, rate),
        flops=8 * span * DI * STATE,
        nbytes=20 * span * DI,
        after=after,
    )


def conv_back(dconv, dconv_bc, drate, following, mixed_ext, aux, conv, after=()):
    span = dconv.shape[0]
    groups = DI // TILE
    tile = lambda rows: pl.BlockSpec((rows, TILE), lambda g: (0, g))
    return pcall(
        conv_back_kernel,
        (groups + 1,),
        [
            pl.BlockSpec((span, TILE), lambda g: (0, jnp.minimum(g, groups - 1))),
            full((span, MAPS)), full((span, 128)), tile(HALO), tile(span + HALO), full((span, 128)), tile(8),
        ],
        [tile(span), tile(8)],
        [shape_of((span, DI + TILE), jnp.bfloat16), shape_of((8, CHANNELS))],
        [vmem((span + HALO, TILE)), vmem((2 * (KW - 1), span, 128))],
        (dconv, dconv_bc, drate, following, mixed_ext, aux, conv),
        flops=8 * span * DI,
        nbytes=10 * span * DI,
        after=after,
    )


def scan_states(received, keeps, reverse, after=()):
    peers = received.shape[0]
    rows = STATE * DI // 128 // peers
    return pcall(
        partial(scan_kernel, reverse, rows),
        (1,),
        [full(received.shape), full(keeps.shape)],
        full((peers, rows, 128)),
        shape_of((peers, rows, 128)),
        [],
        (received, keeps),
        nbytes=8 * peers * rows * 128,
        after=after,
    )


def exchange(parts):
    return lax.all_to_all(parts, "seq", split_axis=0, concat_axis=0, tiled=True)


def shifted(value, steps):
    count = lax.axis_size("seq")
    first, last = max(0, -steps), min(count, count - steps)
    return lax.ppermute(value, "seq", [(source, source + steps) for source in range(first, last)])


def doc_table(lengths, first, count):
    starts = jnp.cumsum(lengths, -1) - lengths
    places = first + jnp.arange(count, dtype=jnp.int32)
    return jnp.sum((starts[None, :] <= places[:, None]).astype(jnp.int32), -1) - 1


def token_marks(lengths, span):
    docs_all = doc_table(lengths, lax.axis_index("seq") * span - HALO, span + 2 * HALO)
    docs = docs_all[HALO : HALO + span]
    ends = docs_all[HALO - 1 : HALO + span : GROUP]
    prior, final = jnp.repeat(ends[:-1], GROUP), jnp.repeat(ends[1:], GROUP)
    near = lambda step: docs_all[HALO + step : HALO + step + span] == docs
    marks = [near(-3), near(-2), near(-1), docs == prior, docs == final, docs, near(1), near(2), near(3)]
    marks = jnp.stack([mark.astype(jnp.float32) for mark in marks], 1)
    aux = jnp.pad(marks, ((0, 0), (0, 128 - marks.shape[1])))
    auxr = jnp.broadcast_to(docs.astype(jnp.float32)[None, :], (8, span))
    return aux, auxr


def halving(count, rows):
    def seq_masks(odd):
        masks = [rows << bit for bit in range(count.bit_length() - 1)]
        return masks[1::-1] + masks[2:] if odd else masks

    return [1 << bit for bit in range(rows.bit_length() - 1)], seq_masks(False), seq_masks(True)


def slab_order():
    count, rows = lax.axis_size("seq"), lax.axis_size("rows")
    row_masks, even, odd = halving(count, rows)
    stages = len(row_masks) + len(even)
    place = jnp.arange(count * rows, dtype=jnp.int32)
    bit = lambda stage: (place >> (stages - 1 - stage)) & 1
    slab = lax.axis_index("seq") * rows + lax.axis_index("rows") + 0 * place
    for stage, mask in enumerate(row_masks):
        slab = slab ^ (bit(stage) * mask)
    swapped = slab & 1
    for at, (one, two) in enumerate(zip(even, odd)):
        slab = slab ^ (bit(len(row_masks) + at) * jnp.where(swapped == 1, two, one))
    return slab


def in_order(values, order):
    width = values.shape[1]
    size = width // order.shape[0]
    source = (order[:, None] * size + jnp.arange(size, dtype=jnp.int32)[None, :]).reshape(-1)
    pick = (jnp.arange(width, dtype=jnp.int32)[:, None] == source[None, :]).astype(jnp.bfloat16)
    return jnp.dot(values, pick, preferred_element_type=jnp.float32).astype(jnp.bfloat16)


def in_order_rows(values, order):
    width = values.shape[1]
    size = width // order.shape[0]
    source = (order[:, None] * size + jnp.arange(size, dtype=jnp.int32)[None, :]).reshape(-1)
    pick = (source[:, None] == jnp.arange(width, dtype=jnp.int32)[None, :]).astype(jnp.bfloat16)
    return jnp.einsum("ns,ts->nt", pick, values, preferred_element_type=jnp.float32).astype(jnp.bfloat16)


def weight_sums(devices, left, right, after=()):
    width, span = left.shape
    columns = right.shape[1]
    slabs = width // 2 // SUM_ROWS
    out = pl.BlockSpec((slabs, SUM_ROWS, 256), lambda g: (g, 0, 0))
    return pcall(
        partial(weight_kernel, width // devices),
        (columns // 256,),
        [full((width, span)), pl.BlockSpec((span, 256), lambda g: (0, g))],
        [out, out],
        [shape_of((columns // 256 * slabs, SUM_ROWS, 256))] * 2,
        [],
        (left, right),
        flops=2 * span * width * columns,
        nbytes=4 * width * columns,
        after=after,
    )


def summed(parts, after=()):
    count, rows = lax.axis_size("seq"), lax.axis_size("rows")
    row_masks, even, odd = halving(count, rows)
    masks = [("rows", mask, mask) for mask in row_masks] + [("seq", one, two) for one, two in zip(even, odd)]
    masks = [(axis, one // rows, two // rows) if axis == "seq" else (axis, one, two) for axis, one, two in masks]
    counts = [send.shape[0] for send, _ in parts]
    chunks, stages = sum(counts), len(masks)
    last = SUM_ROWS >> (stages - 1)
    anywhere = pl.BlockSpec(memory_space=pltpu.HBM)

    def run(*refs):
        taken = 2 * len(parts)
        sums_kernel(counts, masks, *refs[:taken], *refs[taken + len(after) :])

    return pl.pallas_call(
        run,
        in_specs=[anywhere] * (2 * len(parts) + len(after)),
        out_specs=pl.BlockSpec(memory_space=pltpu.VMEM),
        out_shape=shape_of((chunks, last, 256)),
        scratch_shapes=[vmem((chunks, SUM_ROWS, 256))]
        + [vmem((chunks, SUM_ROWS >> stage, 256)) for stage in range(stages)]
        + [
            pltpu.SemaphoreType.DMA((chunks,)),
            pltpu.SemaphoreType.DMA((stages, chunks)),
            pltpu.SemaphoreType.DMA((stages, chunks)),
        ],
        compiler_params=pltpu.CompilerParams(
            vmem_limit_bytes=56 * 1024 * 1024, collective_id=0, has_side_effects=True
        ),
        cost_estimate=pl.CostEstimate(flops=0, bytes_accessed=400 * 1024 * 1024, transcendentals=0),
    )(*[send for send, _ in parts], *[keep for _, keep in parts], *after)


class Scatter:

    def __init__(self, left, right):
        half = left.shape[1] // 2
        self.send = matmul_tn(left[:, half:], right)
        self.keep = matmul_tn(left[:, :half], right)
        count, rows = lax.axis_size("seq"), lax.axis_size("rows")
        row_masks, even, odd = halving(count, rows)
        self.devices = count * rows
        self.stages = [(mask, mask) for mask in row_masks] + list(zip(even, odd))
        self.share()

    def share(self):
        masks = self.stages.pop(0)
        self.got = lax.ppermute(self.send, AXES, [(at, at ^ masks[at & 1]) for at in range(self.devices)])

    def step(self):
        if not self.stages:
            if self.got is not None:
                self.keep = self.keep + self.got
            self.got = None
            return (self.keep,)
        half = self.keep.shape[0] // 2
        self.send = self.keep[half:] + self.got[half:]
        self.keep = self.keep[:half] + self.got[:half]
        self.share()
        return (self.send, self.keep)

    def result(self):
        while self.got is not None:
            self.step()
        return self.keep


def steps(*scatters):
    return sum((scatter.step() for scatter in scatters), ())


def matmul(a, b):
    return jnp.dot(a, b, preferred_element_type=jnp.float32)


def matmul_tn(a, b):
    return jnp.einsum("tn,tm->nm", a, b, preferred_element_type=jnp.float32)


def matmul_nt(a, b):
    return jnp.einsum("tn,mn->tm", a, b, preferred_element_type=jnp.float32)


def normalise(values, gain):
    scale = lax.rsqrt(jnp.mean(values * values, -1, keepdims=True) + EPS)
    return (values * scale * gain).astype(jnp.bfloat16)


def normalise_back(values, gain, grad):
    scale = lax.rsqrt(jnp.mean(values * values, -1, keepdims=True) + EPS)
    gain_grad = jnp.sum(grad * values * scale, 0)
    pulled = grad * gain
    return scale * pulled - values * (scale**3 * jnp.mean(pulled * values, -1, keepdims=True)), gain_grad


def padded(rows, width):
    table = jnp.stack([jnp.pad(row, (0, width - row.shape[0])) for row in rows])
    return jnp.pad(table, ((0, 8 - len(rows)), (0, 0)))


def local(
    inputs,
    lengths,
    norm_gain,
    in_weight,
    conv_weight,
    conv_bias,
    log_decay,
    dt_bias,
    skip,
    gate_gain,
    out_weight,
    cotangent,
):
    _, span, width = inputs.shape
    peers = lax.axis_size("seq")
    aux, auxr = token_marks(lengths[0], span)
    order = slab_order()
    hidden = inputs[0]
    saved = []
    for depth in range(LAYERS):
        conv = jnp.concatenate([conv_weight[depth].T, conv_bias[depth][None], jnp.zeros((3, CHANNELS), jnp.float32)])
        hp = padded([dt_bias[depth], -jnp.exp(log_decay[depth])], 128)
        ch = padded([jnp.repeat(skip[depth], HEAD_DIM), gate_gain[depth]], DI)
        gate_weight = in_weight[depth][:, :DI]
        mixed_weight = in_weight[depth][:, DI : DI + CHANNELS]
        rate_weight = jnp.pad(in_weight[depth][:, DI + CHANNELS :], ((0, 0), (0, 128 - HEADS)))
        before = shifted(hidden[span - HALO :], 1)
        normed = normalise(hidden, norm_gain[depth])
        normed_ext = jnp.concatenate([normalise(before, norm_gain[depth]), normed])
        mixed_ext = matmul(normed_ext, mixed_weight)
        rate = matmul(normed, rate_weight)
        gate = matmul(normed, gate_weight)
        values, bc, col, cumr, made, kx, pay = make_states(peers, mixed_ext, rate, aux, conv, hp)
        received = exchange(pay)
        yi = inner(bc, values, col, cumr, aux, auxr)
        keeps = received[:, -8:]
        state_in = exchange(scan_states(received, keeps, False)).reshape(DI // 128, STATE, 128)
        y, out_low = finish(yi, values, gate, bc, col, state_in, made, kx, ch)
        saved.append(
            (hidden, normed, mixed_ext, rate, gate, values, bc, col, cumr, made, kx, keeps, state_in, y, out_low, yi)
            + (conv, hp, ch, gate_weight, mixed_weight, rate_weight)
        )
        hidden = hidden + matmul(out_low, out_weight[depth])
    gradient = cotangent[0]
    devices = lax.axis_size(AXES)
    collected = [None] * LAYERS
    big_out = [None] * LAYERS
    big_in = [None] * LAYERS
    early, late = (), ()
    for depth in reversed(range(LAYERS)):
        entry, normed, mixed_ext, rate, gate, values, bc, col, cumr, made, kx, keeps, state_in, y, out_low, yi = saved[depth][:16]
        conv, hp, ch, gate_weight, mixed_weight, rate_weight = saved[depth][16:]
        normed_sorted = in_order(normed, order) if depth else in_order_rows(normed, order)
        out_sorted = in_order(out_low, order) if depth else in_order_rows(out_low, order)
        grad_low = gradient.astype(jnp.bfloat16)
        dno = matmul_nt(grad_low, out_weight[depth])
        waits = steps(*late)
        dy, dgate, gate_sums, d1, pay = gate_back(peers, dno, y, gate, values, bc, col, kx, ch, after=waits)
        received = exchange(pay)
        if depth:
            early_now = Scatter(out_sorted, grad_low), Scatter(normed_sorted, dgate)
            waits = sum(((part.send, part.keep) for part in early_now), ())
        else:
            out_chunks = weight_sums(devices, out_sorted, grad_low)
            gate_chunks = weight_sums(devices, normed_sorted, dgate, after=out_chunks[:1])
            waits = (gate_chunks[0],) + steps(*early)
        scanned = scan_states(received, keeps, True, after=waits)
        dso = exchange(scanned).reshape(DI // 128, STATE, 128)
        if depth:
            early = early_now
        waits = steps(*early) if depth else steps(*late)
        xi, dbc = inner_back(bc, values, dy, col, cumr, aux, auxr, after=waits)
        waits = () if depth else steps(*early, *late)
        dconv, dconv_bc, drate, head_rows = states_back(
            xi, values, dy, yi, mixed_ext, bc, col, dso, state_in, made, d1, kx, dbc, aux, conv, ch, hp, rate,
            after=waits,
        )
        following = shifted(jnp.concatenate([dconv[:HALO], dconv_bc[:HALO]], 1), -1)
        waits = steps(*early) if depth else steps(*late)
        dmixed, conv_sums = conv_back(dconv, dconv_bc, drate, following, mixed_ext, aux, conv, after=waits)
        if depth:
            late = (Scatter(normed_sorted, dmixed),)
        else:
            rest_chunks = weight_sums(devices, normed_sorted, dmixed)
        grad_normed = matmul_nt(dgate, gate_weight) + matmul_nt(
            dmixed[:, : CHANNELS + HEADS], in_weight[depth][:, DI:]
        )
        grad_hidden, gain_grad = normalise_back(entry, norm_gain[depth], grad_normed)
        gradient = gradient + grad_hidden
        collected[depth] = (
            gain_grad,
            conv_sums[:KW].T,
            conv_sums[KW],
            gate_sums[0],
            head_rows[1, :HEADS],
            head_rows[0, :HEADS],
            jnp.sum(gate_sums[1].reshape(HEADS, HEAD_DIM), 1),
        )
        if depth:
            trio = early + late
    big_out[1] = trio[0].result()
    big_in[1] = jnp.concatenate([trio[1].result(), trio[2].result()[:, : CHANNELS + HEADS]], 1)
    total = summed([out_chunks, gate_chunks, rest_chunks], after=(gradient, big_out[1], big_in[1]))
    wide = lambda part: jnp.moveaxis(part, 0, 1).reshape(part.shape[1], -1)
    n_out, n_gate = out_chunks[0].shape[0], gate_chunks[0].shape[0]
    slabs = n_out * 256 // out_weight.shape[2]
    big_out[0] = jnp.concatenate([wide(total[part:n_out:slabs]) for part in range(slabs)], 0)
    big_in[0] = wide(total[n_out:])[:, : DI + CHANNELS + HEADS]
    shares = [part.reshape(devices, -1) for sums in collected for part in sums[:4]]
    heads = jnp.concatenate([part for sums in collected for part in sums[4:]])
    table = jnp.concatenate(shares + [jnp.broadcast_to(heads, (devices,) + heads.shape)], 1)
    table = jnp.pad(table, ((0, 0), (0, -table.shape[1] % 128)))
    table = lax.all_to_all(table, AXES, split_axis=0, concat_axis=0, tiled=True).reshape(devices, -1, 128)
    table = pcall(
        total_kernel,
        (1,),
        [full(table.shape)],
        full(table.shape[1:]),
        shape_of(table.shape[1:]),
        [],
        (table,),
        after=(total,),
    ).reshape(-1)
    small = []
    at = 0
    for sums in collected:
        row = []
        for part in sums[:4]:
            size = part.size // devices
            row.append(table[at : at + size].reshape((part.shape[0] // devices,) + part.shape[1:]))
            at += size
        small.append(row)
    for row in small:
        for _ in range(3):
            row.append(table[at : at + HEADS])
            at += HEADS
    stacked = [jnp.stack([small[level][member] for level in range(LAYERS)]) for member in range(7)]
    norm_gain_grad, conv_w_grad, conv_b_grad, gain_grad, decay_grad, bias_grad, skip_grad = stacked
    return (
        hidden[None],
        gradient[None],
        norm_gain_grad,
        jnp.stack(big_in),
        conv_w_grad,
        conv_b_grad,
        decay_grad,
        bias_grad,
        skip_grad,
        gain_grad,
        jnp.stack(big_out),
    )


def solution(mesh):
    in_specs = (
        P("rows", "seq", None),
        P("rows", None),
        P(),
        P(),
        P(),
        P(),
        P(),
        P(),
        P(),
        P(),
        P(),
        P("rows", "seq", None),
    )
    out_specs = (
        P("rows", "seq", None),
        P("rows", "seq", None),
        P(None, ("seq", "rows")),
        P(None, ("seq", "rows"), None),
        P(None, ("seq", "rows"), None),
        P(None, ("seq", "rows")),
        P(),
        P(),
        P(),
        P(None, ("seq", "rows")),
        P(None, ("seq", "rows"), None),
    )
    return jax.shard_map(local, mesh=mesh, in_specs=in_specs, out_specs=out_specs, check_vma=False)
```

```python
from functools import partial

import jax
import jax.numpy as jnp
from jax import lax
from jax.experimental import pallas as pl
from jax.experimental.pallas import tpu as pltpu
from jax.sharding import PartitionSpec as P

DI = 2048
STATE = 128
HEAD_DIM = 64
HEADS = DI // HEAD_DIM
KW = 4
GROUP = 256
LAYERS = 2
CHANNELS = DI + 2 * STATE
TILE = 512
HEADS_AT = TILE // HEAD_DIM
MAPS = 2 * STATE
ROWS_STEP = 256
SUM_ROWS = 512
LAG = 3
AHEAD = 6
EVERY = 5
HALO = 8
HALF = 128
LOG2E = 1.4426950408889634
ROWS_AT = 64
ROWS_CONV = 64
VMEM_BYTES = 60 * 1024 * 1024

EPS = 1e-05
HIGHEST = lax.Precision.HIGHEST
AXES = ("seq", "rows")


def pcall(body, grid, in_specs, out_specs, out_shape, scratch, args, flops=0, nbytes=0, after=(), aliases={}):
    taken = len(args)

    def run(*refs):
        body(*refs[:taken], *refs[taken + len(after) :])

    return pl.pallas_call(
        run,
        grid=grid,
        in_specs=list(in_specs) + [pl.BlockSpec(memory_space=pltpu.HBM)] * len(after),
        out_specs=out_specs,
        out_shape=out_shape,
        scratch_shapes=scratch,
        input_output_aliases=aliases,
        compiler_params=pltpu.CompilerParams(vmem_limit_bytes=VMEM_BYTES),
        cost_estimate=pl.CostEstimate(flops=flops, bytes_accessed=nbytes, transcendentals=0),
    )(*args, *after)


def dot(a, b, dims=(((1,), (0,)), ((), ()))):
    return lax.dot_general(
        a.astype(jnp.bfloat16), b.astype(jnp.bfloat16), dims, preferred_element_type=jnp.float32
    )


def dot_nt(a, b):
    return dot(a, b, (((1,), (1,)), ((), ())))


def dot_exact(a, b):
    return jnp.dot(a, b, precision=HIGHEST, preferred_element_type=jnp.float32)


def sigmoid(v):
    return 0.5 * jnp.tanh(0.5 * v) + 0.5


def lane_iota(shape):
    return lax.broadcasted_iota(jnp.int32, shape, 1)


def low_half(rows):
    return lane_iota((rows, 128)) < HEAD_DIM


def to_heads(cols, first, pairs):
    rows = cols.shape[0]
    low = low_half(rows)
    parts = []
    for pair in range(pairs):
        at = first + 2 * pair
        parts.append(
            jnp.where(
                low,
                jnp.broadcast_to(cols[:, at : at + 1], (rows, 128)),
                jnp.broadcast_to(cols[:, at + 1 : at + 2], (rows, 128)),
            )
        )
    return jnp.concatenate(parts, 1) if pairs > 1 else parts[0]


def spread_heads(cols, pairs):
    pick = (
        lax.broadcasted_iota(jnp.int32, (128, 128 * pairs), 0) == lane_iota((128, 128 * pairs)) // HEAD_DIM
    ).astype(jnp.bfloat16)
    high = cols.astype(jnp.bfloat16)
    return dot(high, pick) + dot(cols - high.astype(jnp.float32), pick)


def head_pick(first, heads):
    shape = (128, HEAD_DIM * heads)
    return (lax.broadcasted_iota(jnp.int32, shape, 0) == first + lane_iota(shape) // HEAD_DIM).astype(jnp.bfloat16)


def picked_heads(cols, pick):
    high = cols.astype(jnp.bfloat16)
    return dot(high, pick) + dot(cols - high.astype(jnp.float32), pick)


def head_sums(first):
    channel = lax.broadcasted_iota(jnp.int32, (TILE, 128), 0)
    return (channel // HEAD_DIM + first == lane_iota((TILE, 128))).astype(jnp.bfloat16)


def keep_marks(marks_ref, aux_ref, lanes):
    for at, lane in enumerate(lanes):
        marks_ref[at] = jnp.broadcast_to(aux_ref[:, lane : lane + 1], marks_ref.shape[1:])


def conv_rows(x_ref, w_ref, marks_ref, first, count, lanes):
    total = w_ref[4:5, lanes] + w_ref[3:4, lanes] * x_ref[first + 8 : first + 8 + count, lanes]
    for tap in range(KW - 1):
        match = marks_ref[tap, first : first + count, :]
        total = total + w_ref[tap : tap + 1, lanes] * (x_ref[first + 5 + tap : first + 5 + tap + count, lanes] * match)
    return total


def chunks_of(rows, width):
    for pair in range(width // 128):
        for first in range(0, rows, ROWS_AT):
            yield first, slice(first, first + ROWS_AT), slice(pair * 128, (pair + 1) * 128)


def states_kernel(
    x_ref, xbc_ref, rate_ref, aux_ref, w_ref, wbc_ref, hp_ref,
    v_ref, bc_ref, col_ref, cumr_ref, made_ref, kx_ref, pay_ref, slope_ref, slope_bc_ref,
    bt_ref, marks_ref,
):
    turn = pl.program_id(0)
    span = v_ref.shape[0]
    count = span // GROUP

    @pl.when(turn == 0)
    def _():
        keep_marks(marks_ref, aux_ref, range(KW - 1))
        for first, rows, lanes in chunks_of(span, MAPS):
            conv = conv_rows(xbc_ref, wbc_ref, marks_ref, first, ROWS_AT, lanes)
            sig = sigmoid(conv)
            bc_ref[rows, lanes] = conv * sig
            slope_bc_ref[rows, lanes] = sig * (1.0 + conv * (1.0 - sig))
        tri = (
            lax.broadcasted_iota(jnp.int32, (GROUP, GROUP), 0) >= lane_iota((GROUP, GROUP))
        ).astype(jnp.float32)
        for block in range(count):
            rows = slice(block * GROUP, (block + 1) * GROUP)
            bt_ref[block] = bc_ref[rows, :STATE].T.astype(jnp.bfloat16)
            raw = rate_ref[HALO + block * GROUP : HALO + (block + 1) * GROUP, :] + hp_ref[0:1, :]
            step = jnp.maximum(raw, 0.0) + jnp.log1p(jnp.exp(-jnp.abs(raw)))
            cum = dot_exact(tri, hp_ref[1:2, :] * step)
            last = cum[GROUP - 1 :, :]
            col_ref[0, rows, :] = cum
            col_ref[1, rows, :] = step
            col_ref[2, rows, :] = jnp.exp(cum) * aux_ref[rows, 3:4]
            col_ref[3, rows, :] = jnp.exp(last - cum) * aux_ref[rows, 4:5]
            cumr_ref[:, rows] = cum.T

    for first, rows, lanes in chunks_of(span, TILE):
        conv = conv_rows(x_ref, w_ref, marks_ref, first, ROWS_AT, lanes)
        sig = sigmoid(conv)
        v_ref[rows, lanes] = conv * sig
        slope_ref[rows, lanes] = sig * (1.0 + conv * (1.0 - sig))
    pick = head_pick(turn * HEADS_AT, HEADS_AT)
    made = []
    keep = []
    for block in range(count):
        rows = slice(block * GROUP, (block + 1) * GROUP)
        weight = picked_heads(col_ref[3, rows, :] * col_ref[1, rows, :], pick)
        made.append(dot(bt_ref[block], weight * v_ref[rows, :]))
        ends = col_ref[2, (block + 1) * GROUP - 8 : (block + 1) * GROUP, :]
        keep.append(picked_heads(ends, pick)[7:8, :])
    made_ref[...] = made[0]
    kx_ref[...] = jnp.concatenate([keep[0], keep[1], jnp.zeros((6, TILE), jnp.float32)], 0)
    final = keep[1] * made[0] + made[1]
    total = jnp.broadcast_to(keep[0] * keep[1], (8, TILE))
    pairs = TILE // 128
    chunks = pay_ref.shape[0] // pairs
    size = STATE // chunks
    for pair in range(pairs):
        lanes = slice(pair * 128, (pair + 1) * 128)
        for chunk in range(chunks):
            pay_ref[pair * chunks + chunk, :size, :] = final[chunk * size : (chunk + 1) * size, lanes]
            pay_ref[pair * chunks + chunk, size:, :] = total[:, lanes]


def inner_kernel(bc_ref, v_ref, col_ref, cumr_ref, aux_ref, auxr_ref, y_ref, g_ref):
    scores = dot_nt(bc_ref[:, STATE:], bc_ref[:, :STATE])
    allowed = (aux_ref[:, 5:6] == auxr_ref[0:1, :]) & (
        lax.broadcasted_iota(jnp.int32, (GROUP, GROUP), 0) >= lane_iota((GROUP, GROUP))
    )
    g_ref[...] = jnp.where(allowed, scores, 0.0)
    low = low_half(GROUP)
    cum = LOG2E * col_ref[0]
    cum_row = LOG2E * cumr_ref[:HEADS, :]
    steps = picked_heads(col_ref[1], head_pick(0, HEADS))
    for pair in range(HEADS // 2):
        lanes = slice(pair * 128, (pair + 1) * 128)
        scaled = steps[:, lanes] * v_ref[:, lanes]
        result = None
        for half in range(2):
            head = 2 * pair + half
            row = cum_row[head : head + 1, :]
            tops, bottoms = [], []
            for first in range(0, GROUP, 64):
                width = HALF if first < HALF else GROUP
                spread = cum[first : first + 64, head : head + 1] - row[:, :width]
                decay = jnp.exp2(jnp.minimum(spread, 0.0))
                mixing = (g_ref[first : first + 64, :width] * decay).astype(jnp.bfloat16)
                (tops if first < HALF else bottoms).append(mixing)
            picked = jnp.where(low if half == 0 else ~low, scaled, 0.0).astype(jnp.bfloat16)
            top = dot(jnp.concatenate(tops, 0), picked[:HALF])
            bottom = dot(jnp.concatenate(bottoms, 0), picked)
            result = (top, bottom) if result is None else (result[0] + top, result[1] + bottom)
        y_ref[:HALF, lanes] = result[0]
        y_ref[HALF:, lanes] = result[1]


def finish_kernel(
    yi_ref, v_ref, gate_ref, bc_ref, col_ref, sin_ref, made_ref, kx_ref, ch_ref,
    y_ref, out_ref,
    gated_ref,
):
    later = pl.program_id(0) * ROWS_STEP >= GROUP
    out_map = bc_ref[:, STATE:].astype(jnp.bfloat16)
    entering = picked_heads(col_ref[2], head_pick(0, HEADS))
    total = [jnp.zeros((ROWS_AT, 128), jnp.float32) for _ in range(ROWS_STEP // ROWS_AT)]
    for pair in range(HEADS // 2):
        lanes = slice(pair * 128, (pair + 1) * 128)
        state = sin_ref[pair]
        state = jnp.where(later, kx_ref[0:1, lanes] * state + made_ref[:, lanes], state)
        outer = entering[:, lanes] * dot(out_map, state)
        for at in range(ROWS_STEP // ROWS_AT):
            rows = slice(at * ROWS_AT, (at + 1) * ROWS_AT)
            result = yi_ref[rows, lanes] + outer[rows] + ch_ref[0:1, lanes] * v_ref[rows, lanes]
            y_ref[rows, lanes] = result
            gate = gate_ref[rows, lanes]
            gated = result * (gate * sigmoid(gate))
            gated_ref[rows, lanes] = gated
            total[at] = total[at] + gated * gated
    for at in range(ROWS_STEP // ROWS_AT):
        rows = slice(at * ROWS_AT, (at + 1) * ROWS_AT)
        scale = lax.rsqrt(jnp.sum(total[at], 1, keepdims=True) / DI + EPS)
        out_ref[rows, :] = (gated_ref[rows, :] * scale * ch_ref[1:2, :]).astype(jnp.bfloat16)


def gate_back_kernel(
    dno_ref, y_ref, gate_ref, v_ref, bc_ref, col_ref, kx_ref, ch_ref,
    dy_ref, dgate_ref, sum_ref, d1_ref, pay_ref,
    gated_ref, silu_ref,
):
    at_step = pl.program_id(0)
    later = at_step * ROWS_STEP >= GROUP
    parts = ROWS_STEP // ROWS_AT
    square = [jnp.zeros((ROWS_AT, 128), jnp.float32) for _ in range(parts)]
    cross = [jnp.zeros((ROWS_AT, 128), jnp.float32) for _ in range(parts)]
    for first, rows, lanes in chunks_of(ROWS_STEP, DI):
        gate = gate_ref[rows, lanes]
        sig = sigmoid(gate)
        silu = gate * sig
        y = y_ref[rows, lanes]
        gated = y * silu
        gated_ref[rows, lanes] = gated
        silu_ref[0, rows, lanes] = silu
        silu_ref[1, rows, lanes] = y * (sig * (1.0 + gate * (1.0 - sig)))
        at = first // ROWS_AT
        square[at] = square[at] + gated * gated
        cross[at] = cross[at] + gated * (dno_ref[rows, lanes] * ch_ref[1:2, lanes])
    scales = [lax.rsqrt(jnp.sum(part, 1, keepdims=True) / DI + EPS) for part in square]
    pulls = [scale * scale * scale * (jnp.sum(part, 1, keepdims=True) / DI) for scale, part in zip(scales, cross)]
    out_t = bc_ref[:, STATE:].T.astype(jnp.bfloat16)
    entering = picked_heads(col_ref[2], head_pick(0, HEADS))
    pairs = DI // 128
    chunks = pay_ref.shape[0] // pairs
    size = STATE // chunks

    @pl.when(at_step == 0)
    def _():
        sum_ref[...] = jnp.zeros_like(sum_ref)
        pay_ref[...] = jnp.zeros_like(pay_ref)

    @pl.when((at_step == 0) | (at_step * ROWS_STEP == GROUP))
    def _():
        d1_ref[...] = jnp.zeros_like(d1_ref)

    for pair in range(pairs):
        lanes = slice(pair * 128, (pair + 1) * 128)
        gain_sum = jnp.zeros((8, 128), jnp.float32)
        skip_sum = jnp.zeros((8, 128), jnp.float32)
        weighted = []
        for at in range(parts):
            rows = slice(at * ROWS_AT, (at + 1) * ROWS_AT)
            gated = gated_ref[rows, lanes]
            dno = dno_ref[rows, lanes] * scales[at]
            dgated = dno * ch_ref[1:2, lanes] - gated * pulls[at]
            dy = dgated * silu_ref[0, rows, lanes]
            dy_ref[rows, lanes] = dy
            dgate_ref[rows, lanes] = (dgated * silu_ref[1, rows, lanes]).astype(jnp.bfloat16)
            gain_sum = gain_sum + jnp.sum((dno * gated).reshape(-1, 8, 128), 0)
            skip_sum = skip_sum + jnp.sum((dy * v_ref[rows, lanes]).reshape(-1, 8, 128), 0)
            weighted.append((entering[rows, lanes] * dy).astype(jnp.bfloat16))
        sum_ref[0:1, lanes] += jnp.sum(gain_sum, 0, keepdims=True)
        sum_ref[1:2, lanes] += jnp.sum(skip_sum, 0, keepdims=True)
        fresh = dot(out_t, jnp.concatenate(weighted, 0))
        d1_ref[:, lanes] += fresh
        more = jnp.where(later, kx_ref[0:1, lanes], 1.0) * fresh
        for chunk in range(chunks):
            pay_ref[pair * chunks + chunk] += more[chunk * size : (chunk + 1) * size]


def inner_back_kernel(
    bc_ref, v_ref, dy_ref, col_ref, cumr_ref, aux_ref, auxr_ref,
    x_ref, dbc_ref,
    g_ref, dg_ref,
):
    allowed = (aux_ref[:, 5:6] == auxr_ref[0:1, :]) & (
        lax.broadcasted_iota(jnp.int32, (GROUP, GROUP), 0) <= lane_iota((GROUP, GROUP))
    )
    g_ref[...] = jnp.where(allowed, dot_nt(bc_ref[:, :STATE], bc_ref[:, STATE:]), 0.0)
    dg_ref[...] = jnp.zeros_like(dg_ref)
    low = low_half(GROUP)
    cum = LOG2E * col_ref[0]
    cum_row = LOG2E * cumr_ref[:HEADS, :]
    steps = picked_heads(col_ref[1], head_pick(0, HEADS))
    for pair in range(HEADS // 2):
        lanes = slice(pair * 128, (pair + 1) * 128)
        scaled = steps[:, lanes] * v_ref[:, lanes]
        dy = dy_ref[:, lanes]
        dy_low = dy.astype(jnp.bfloat16)
        result = None
        grads = {}
        for half in range(2):
            head = 2 * pair + half
            row = cum_row[head : head + 1, :]
            mine = low if half == 0 else ~low
            picked = jnp.where(mine, scaled, 0.0).astype(jnp.bfloat16)
            top_grad = dot_nt(picked[:HALF], dy_low)
            bottom_grad = dot_nt(picked[HALF:], dy_low[HALF:])
            tops, bottoms = [], []
            for first in range(0, GROUP, 64):
                rows = slice(first, first + 64)
                top = first < HALF
                across = slice(0 if top else HALF, GROUP)
                spread = row[:, across] - cum[rows, head : head + 1]
                decay = jnp.exp2(jnp.minimum(spread, 0.0))
                (tops if top else bottoms).append((g_ref[rows, across] * decay).astype(jnp.bfloat16))
                part = (top_grad[rows] if top else bottom_grad[first - HALF : first - HALF + 64]) * decay
                if half == 0:
                    grads[first] = part
                else:
                    dg_ref[rows, across] += grads[first] + part
            dy_mine = jnp.where(mine, dy, 0.0).astype(jnp.bfloat16)
            top = dot(jnp.concatenate(tops, 0), dy_mine)
            bottom = dot(jnp.concatenate(bottoms, 0), dy_mine[HALF:])
            result = (top, bottom) if result is None else (result[0] + top, result[1] + bottom)
        x_ref[:HALF, lanes] = result[0]
        x_ref[HALF:, lanes] = result[1]
    dg = jnp.where(allowed, dg_ref[...], 0.0)
    dbc_ref[:, :STATE] = dot(dg, bc_ref[:, STATE:])
    dbc_ref[:, STATE:] = dot(dg.T, bc_ref[:, :STATE])


def states_pre_kernel(
    xi_ref, v_ref, dy_ref, yi_ref, bc_ref, col_ref, sin_ref, made_ref, kx_ref, dbc_ref, ch_ref,
    base_ref, ds_ref, dc_ref, dmap_ref,
):
    turn = pl.program_id(0)
    count = v_ref.shape[0] // GROUP

    @pl.when(turn == 0)
    def _():
        ds_ref[...] = jnp.zeros_like(ds_ref)
        dc_ref[...] = jnp.zeros_like(dc_ref)
        dmap_ref[...] = dbc_ref[...]

    sums = head_sums(turn * HEADS_AT)
    pick = head_pick(turn * HEADS_AT, HEADS_AT)
    state = jnp.concatenate([sin_ref[pair] for pair in range(TILE // 128)], 1)
    starts = [state, kx_ref[0:1, :] * state + made_ref[...]]
    for block in range(count):
        at = slice(block * GROUP, (block + 1) * GROUP)
        step = picked_heads(col_ref[1, at, :], pick)
        entering = picked_heads(col_ref[2, at, :], pick)
        outer = dot(bc_ref[at, STATE:], starts[block])
        kinds = {name: [] for name in ("ds", "dc", "low", "dy")}
        for first in range(0, GROUP, ROWS_AT):
            local = slice(first, first + ROWS_AT)
            rows = slice(block * GROUP + first, block * GROUP + first + ROWS_AT)
            pieces = {name: [] for name in kinds}
            for pair in range(TILE // 128):
                lanes = slice(pair * 128, (pair + 1) * 128)
                v = v_ref[rows, lanes]
                dy = dy_ref[rows, lanes]
                xi = xi_ref[rows, lanes]
                scaled = step[local, lanes] * v
                low = dy.astype(jnp.bfloat16).astype(jnp.float32)
                inside = low * yi_ref[rows, lanes] - scaled.astype(jnp.bfloat16).astype(jnp.float32) * xi
                inside = inside + dy * (entering[local, lanes] * outer[local, lanes])
                high = inside.astype(jnp.bfloat16)
                pieces["dc"].append(high)
                pieces["low"].append((inside - high.astype(jnp.float32)).astype(jnp.bfloat16))
                pieces["ds"].append((v * xi).astype(jnp.bfloat16))
                pieces["dy"].append((entering[local, lanes] * dy).astype(jnp.bfloat16))
                base_ref[rows, lanes] = step[local, lanes] * xi + ch_ref[0:1, lanes] * dy
            for name in kinds:
                kinds[name].append(jnp.concatenate(pieces[name], 1))
        whole = {name: jnp.concatenate(parts, 0) for name, parts in kinds.items()}
        ds_ref[at, :] += dot(whole["ds"], sums)
        dc_ref[at, :] += dot(whole["dc"], sums) + dot(whole["low"], sums)
        dmap_ref[at, STATE:] += dot_nt(whole["dy"], starts[block])


def states_back_kernel(
    base_ref, v_ref, slope_ref, slope_bc_ref, bc_ref, col_ref, dso_ref, sin_ref, made_ref, d1_ref,
    kx_ref, ds0_ref, dc_ref, dmap0_ref, hp_ref, rate_ref,
    dconv_ref, dconv_bc_ref, drate_ref, sum_ref,
    ds_ref, z_ref, kd_ref, dmap_ref,
):
    turn = pl.program_id(0)
    span = v_ref.shape[0]
    count = span // GROUP

    @pl.when(turn == 0)
    def _():
        ds_ref[...] = ds0_ref[...]
        z_ref[...] = jnp.zeros_like(z_ref)
        kd_ref[...] = jnp.zeros_like(kd_ref)
        dmap_ref[...] = dmap0_ref[...]

    sums = head_sums(turn * HEADS_AT)
    pick = head_pick(turn * HEADS_AT, HEADS_AT)
    end_grad = jnp.concatenate([dso_ref[pair] for pair in range(TILE // 128)], 1)
    state = jnp.concatenate([sin_ref[pair] for pair in range(TILE // 128)], 1)
    ends = [d1_ref[...] + kx_ref[1:2, :] * end_grad, end_grad]
    starts = [state, kx_ref[0:1, :] * state + made_ref[...]]
    for block in range(count):
        at = slice(block * GROUP, (block + 1) * GROUP)
        step = picked_heads(col_ref[1, at, :], pick)
        tail = picked_heads(col_ref[3, at, :], pick)
        from_end = dot(bc_ref[at, :STATE], ends[block])
        kinds = {name: [] for name in ("ds", "z", "values")}
        for first in range(0, GROUP, ROWS_AT):
            local = slice(first, first + ROWS_AT)
            rows = slice(block * GROUP + first, block * GROUP + first + ROWS_AT)
            pieces = {name: [] for name in kinds}
            for pair in range(TILE // 128):
                lanes = slice(pair * 128, (pair + 1) * 128)
                v = v_ref[rows, lanes]
                scaled = step[local, lanes] * v
                ended = tail[local, lanes] * from_end[local, lanes]
                pieces["ds"].append((v * ended).astype(jnp.bfloat16))
                pieces["z"].append((scaled * ended).astype(jnp.bfloat16))
                pieces["values"].append((tail[local, lanes] * scaled).astype(jnp.bfloat16))
                grad = base_ref[rows, lanes] + step[local, lanes] * ended
                dconv_ref[rows, lanes] = grad * slope_ref[rows, lanes]
            for name in kinds:
                kinds[name].append(jnp.concatenate(pieces[name], 1))
        whole = {name: jnp.concatenate(parts, 0) for name, parts in kinds.items()}
        ds_ref[at, :] += dot(whole["ds"], sums)
        z_ref[at, :] += dot(whole["z"], sums)
        dmap_ref[at, :STATE] += dot_nt(whole["values"], ends[block])
        kept = kx_ref[block : block + 1, :] * jnp.sum(ends[block] * starts[block], 0, keepdims=True)
        kd_ref[block] += dot_exact(jnp.broadcast_to(kept, (8, TILE)), sums.astype(jnp.float32))

    @pl.when(turn == pl.num_programs(0) - 1)
    def _():
        here = lax.broadcasted_iota(jnp.int32, (GROUP, GROUP), 0)
        after = (here <= lane_iota((GROUP, GROUP))).astype(jnp.float32)
        before = (here > lane_iota((GROUP, GROUP))).astype(jnp.float32)
        bias_sum = jnp.zeros((1, 128), jnp.float32)
        decay_sum = jnp.zeros((1, 128), jnp.float32)
        for first, rows, lanes in chunks_of(span, MAPS):
            dconv_bc_ref[rows, lanes] = dmap_ref[rows, lanes] * slope_bc_ref[rows, lanes]
        for block in range(count):
            rows = slice(block * GROUP, (block + 1) * GROUP)
            da = dot_exact(after, dc_ref[rows, :]) + kd_ref[block, 0:1, :]
            da = da + dot_exact(before, z_ref[rows, :])
            ds = ds_ref[rows, :] + hp_ref[1:2, :] * da
            drate = ds * sigmoid(rate_ref[HALO + block * GROUP : HALO + (block + 1) * GROUP, :] + hp_ref[0:1, :])
            drate_ref[rows, :] = drate.astype(jnp.bfloat16)
            bias_sum = bias_sum + jnp.sum(drate, 0, keepdims=True)
            decay_sum = decay_sum + jnp.sum(da * hp_ref[1:2, :] * col_ref[1, rows, :], 0, keepdims=True)
        sum_ref[...] = jnp.concatenate([bias_sum, decay_sum, jnp.zeros((6, 128), jnp.float32)], 0)


def conv_back_kernel(
    dconv_ref, dconv_bc_ref, drate_ref, next_ref, x_ref, aux_ref, w_ref, dx_ref, sum_ref, marks_ref
):
    turn = pl.program_id(0)
    last = pl.num_programs(0) - 1
    span = dconv_ref.shape[0]

    @pl.when(turn == 0)
    def _():
        keep_marks(marks_ref, aux_ref, (6, 7, 8))

    def tile(source_ref, width):
        for pair in range(width // 128):
            lanes = slice(pair * 128, (pair + 1) * 128)
            sums = [jnp.zeros((8, 128), jnp.float32) for _ in range(KW + 1)]
            weights = [jnp.broadcast_to(w_ref[tap : tap + 1, lanes], (8, 128)) for tap in range(KW)]
            for first in range(0, span, ROWS_CONV):
                rows = slice(first, first + ROWS_CONV)
                following = next_ref if first + ROWS_CONV == span else source_ref
                at = 0 if first + ROWS_CONV == span else first + ROWS_CONV
                here = source_ref[rows, lanes]
                whole = jnp.concatenate([here, following[at : at + 8, lanes]], 0)
                x = x_ref[HALO + first : HALO + first + ROWS_CONV, lanes]
                split = lambda v: v.reshape(ROWS_CONV // 8, 8, 128)
                x8, here8 = split(x), split(here)
                grad = weights[KW - 1] * here8
                sums[KW] = sums[KW] + jnp.sum(here8, 0)
                sums[KW - 1] = sums[KW - 1] + jnp.sum(here8 * x8, 0)
                for ahead in range(1, KW):
                    later = split(whole[ahead : ahead + ROWS_CONV] * marks_ref[ahead - 1, rows, :])
                    tap = KW - 1 - ahead
                    grad = grad + weights[tap] * later
                    sums[tap] = sums[tap] + jnp.sum(later * x8, 0)
                dx_ref[rows, lanes] = grad.reshape(ROWS_CONV, 128).astype(jnp.bfloat16)
            sums = [jnp.sum(part, 0, keepdims=True) for part in sums]
            sum_ref[:, lanes] = jnp.concatenate(sums + [jnp.zeros((3, 128), jnp.float32)], 0)

    @pl.when(turn < last)
    def _():
        tile(dconv_ref, TILE)

    @pl.when(turn == last)
    def _():
        tile(dconv_bc_ref, MAPS)
        sum_ref[:, MAPS:] = jnp.zeros_like(sum_ref[:, MAPS:])
        dx_ref[:, MAPS : MAPS + 128] = drate_ref[...]
        dx_ref[:, MAPS + 128 :] = jnp.zeros_like(drate_ref)


def scan_kernel(reverse, rows, in_ref, keep_ref, out_ref):
    peers = out_ref.shape[0]
    carried = jnp.zeros((rows, 128), jnp.float32)
    for at in range(peers):
        peer = peers - 1 - at if reverse else at
        out_ref[peer] = carried
        carried = keep_ref[peer, 0:1, :] * carried + in_ref[peer, :rows, :]


def total_kernel(in_ref, out_ref):
    out_ref[...] = jnp.sum(in_ref[...], 0)


def weight_kernel(each, left_ref, right_ref, send_ref, keep_ref):
    slabs, size = send_ref.shape[0], SUM_ROWS
    total = dot(left_ref[...], right_ref[...])
    half = total.shape[0] // 2
    for out_ref, rows in ((keep_ref, total[:half]), (send_ref, total[half:])):
        if slabs == 1:
            out_ref[0] = rows
        else:
            split = rows.reshape(-1, slabs, each // slabs, rows.shape[1])
            for part in range(slabs):
                out_ref[part] = split[:, part].reshape(size, rows.shape[1])


def sums_kernel(counts, orders, *refs):
    pieces = len(counts)
    sends, keeps, out_ref, kept_ref = refs[:pieces], refs[pieces : 2 * pieces], refs[2 * pieces], refs[2 * pieces + 1]
    stages = len(orders[0])
    got = refs[2 * pieces + 2 : 2 * pieces + 2 + stages]
    load_sem, send_sem, recv_sem = refs[2 * pieces + 2 + stages :]
    chunks = sum(counts)
    seq, row = lax.axis_index("seq"), lax.axis_index("rows")
    odd = lax.rem(row, 2)

    def over(at, mask):
        return at + mask * (1 - 2 * lax.rem(at // mask, 2))

    routes = []
    for masks in orders:
        partners = []
        for axis, even_mask, odd_mask in masks:
            if axis == "rows":
                partners.append((seq, over(row, even_mask)))
            else:
                one, two = over(seq, even_mask), over(seq, odd_mask)
                partners.append((one + odd * (two - one), row))
        routes.append(partners)

    barrier = pltpu.get_barrier_semaphore()
    for partner in routes[0]:
        pl.semaphore_signal(
            barrier,
            inc=1,
            device_id={"seq": partner[0], "rows": partner[1]},
            device_id_type=pl.DeviceIdType.MESH,
        )
    pl.semaphore_wait(barrier, stages)

    def second(chunk):
        return (EVERY - lax.rem(chunk, EVERY)) // EVERY

    def copy(stage, chunk, source=None):
        size = SUM_ROWS >> stage
        other = second(chunk)
        main, side = routes[0][stage], routes[1][stage]
        if source is None:
            source = kept_ref.at[chunk] if stage == 0 else kept_ref.at[chunk, pl.ds(size, size)]
        return pltpu.make_async_remote_copy(
            src_ref=source,
            dst_ref=got[stage].at[chunk],
            send_sem=send_sem.at[stage, chunk],
            recv_sem=recv_sem.at[stage, chunk],
            device_id={
                "seq": main[0] + other * (side[0] - main[0]),
                "rows": main[1] + other * (side[1] - main[1]),
            },
            device_id_type=pl.DeviceIdType.MESH,
        )

    def load(chunk, source):
        return pltpu.make_async_copy(source, kept_ref.at[chunk], load_sem.at[chunk])

    def begin(chunk):
        side = second(chunk)
        inner = chunk - chunk // EVERY - 1

        @pl.when((side == 1) & (chunk < chunks))
        def _():
            copy(0, chunk, sends[0].at[chunk // EVERY]).start()
            load(chunk, keeps[0].at[chunk // EVERY]).start()

        base = 0
        for count, send_ref, keep_ref in zip(counts[1:], sends[1:], keeps[1:]):

            @pl.when((side == 0) & (inner >= base) & (inner < base + count))
            def _(base=base, send_ref=send_ref, keep_ref=keep_ref):
                copy(0, chunk, send_ref.at[inner - base]).start()
                load(chunk, keep_ref.at[inner - base]).start()

            base += count

    def first(chunk, _):
        begin(chunk)
        return 0

    lax.fori_loop(0, AHEAD, first, 0)

    def turn(at, _):
        begin(at + AHEAD)
        for stage in range(stages):
            chunk = at - LAG * stage

            @pl.when((chunk >= 0) & (chunk < chunks))
            def _():
                size = SUM_ROWS >> stage
                if stage == 0:
                    load(chunk, keeps[0].at[0]).wait()
                copy(stage, chunk, sends[0].at[0] if stage == 0 else None).wait_recv()
                total = kept_ref[chunk, :size] + got[stage][chunk]
                if stage + 1 < stages:
                    kept_ref[chunk, :size] = total
                    copy(stage + 1, chunk).start()
                else:
                    out_ref[chunk] = total

        return 0

    lax.fori_loop(0, chunks + LAG * (stages - 1), turn, 0)

    def ended(chunk, _):
        for stage in range(stages):
            copy(stage, chunk, sends[0].at[0] if stage == 0 else None).wait_send()
        return 0

    lax.fori_loop(0, chunks, ended, 0)


def edge(weights, width, first):
    row = lax.broadcasted_iota(jnp.int32, weights.shape, 0)
    return jnp.where(first + row < width, weights, jnp.zeros_like(weights))


def project_kernel(width, first_block, x_ref, before_ref, gain_ref, w_ref, normed_ref, out_ref, ext_ref):
    turn = pl.program_id(0)
    last = pl.num_programs(0) - 1

    @pl.when(turn == 0)
    def _():
        def scaled(values):
            scale = lax.rsqrt(jnp.mean(values * values, 1, keepdims=True) + EPS)
            return (values * scale * gain_ref[...]).astype(jnp.bfloat16)

        for first in range(0, x_ref.shape[0], ROWS_AT):
            rows = slice(first, first + ROWS_AT)
            normed_ref[rows, :] = scaled(x_ref[rows, :])
        ext_ref[...] = jnp.concatenate([scaled(before_ref[...]), normed_ref[...]], 0)

    @pl.when(turn < last)
    def _():
        out_ref[...] = dot_nt(ext_ref[...], w_ref[0])

    @pl.when(turn == last)
    def _():
        out_ref[...] = dot_nt(ext_ref[...], edge(w_ref[0], width, (first_block + last) * TILE))


def gate_kernel(normed_ref, w_ref, out_ref):
    out_ref[...] = dot_nt(normed_ref[...], w_ref[0])


def project_back_gate_kernel(dgate_ref, w_ref, out_ref):
    @pl.when(pl.program_id(0) == 0)
    def _():
        out_ref[...] = dot(dgate_ref[...], w_ref[0])

    @pl.when(pl.program_id(0) > 0)
    def _():
        out_ref[...] += dot(dgate_ref[...], w_ref[0])


def project_back_kernel(
    width, first_block, part_ref, dmixed_ref, w_ref, x_ref, grad_ref, gain_ref,
    new_ref, low_ref, sum_ref,
    acc_ref,
):
    turn = pl.program_id(0)
    last = pl.num_programs(0) - 1

    @pl.when(turn == 0)
    def _():
        acc_ref[...] = part_ref[...] + dot(dmixed_ref[...], w_ref[0])

    @pl.when((turn > 0) & (turn < last))
    def _():
        acc_ref[...] += dot(dmixed_ref[...], w_ref[0])

    @pl.when(turn == last)
    def _():
        acc_ref[...] += dot(dmixed_ref[...], edge(w_ref[0], width, (first_block + last) * TILE))
        total = jnp.zeros((8, x_ref.shape[1]), jnp.float32)
        for first in range(0, x_ref.shape[0], 16):
            rows = slice(first, first + 16)
            x = x_ref[rows, :]
            grad = acc_ref[rows, :]
            scale = lax.rsqrt(jnp.mean(x * x, 1, keepdims=True) + EPS)
            pulled = grad * gain_ref[...]
            cross = jnp.mean(pulled * x, 1, keepdims=True)
            scaled = x * scale
            total = total + grad[:8] * scaled[:8] + grad[8:] * scaled[8:]
            new = grad_ref[rows, :] + (scale * pulled - x * (scale * scale * scale * cross))
            new_ref[rows, :] = new
            low_ref[rows, :] = new.astype(jnp.bfloat16)
        sum_ref[...] = total


def plain_weight_kernel(left_ref, right_ref, *refs):
    out_ref = refs[-1]
    out_ref[...] = dot(left_ref[...], right_ref[...], (((0,), (0,)), ((), ())))


def sort_kernel(source_ref, values_ref, out_ref):
    pick = (source_ref[...] == lane_iota((source_ref.shape[0], values_ref.shape[1]))).astype(jnp.bfloat16)
    out_ref[...] = dot_nt(pick, values_ref[...]).astype(jnp.bfloat16)


def assemble_kernel(outs, ins, total_ref, in_ref, all_out_ref, all_in_ref):
    rows = total_ref.shape[1]
    for level, parts in enumerate(outs):
        for part, places in enumerate(parts):
            for at, place in enumerate(places):
                lanes = slice(at * 256, (at + 1) * 256)
                all_out_ref[level, part * rows : (part + 1) * rows, lanes] = total_ref[place]
    columns = all_in_ref.shape[2]
    for at, place in enumerate(ins):
        size = min(256, columns - at * 256)
        all_in_ref[0, :, at * 256 : at * 256 + size] = total_ref[place, :, :size]
    all_in_ref[1] = in_ref[:, :columns]


def full(shape):
    return pl.BlockSpec(shape, lambda *at: (0,) * len(shape))


def shape_of(dims, dtype=jnp.float32):
    return jax.ShapeDtypeStruct(dims, dtype)


def vmem(dims, dtype=jnp.float32):
    return pltpu.VMEM(dims, dtype)


def make_states(peers, mixed_ext, aux, conv, hp):
    span = aux.shape[0]
    rate = pl.BlockSpec((span + HALO, 128), lambda g: (0, CHANNELS // 128))
    groups = DI // TILE
    chunks = peers * 128 // DI
    tile = lambda rows: pl.BlockSpec((rows, TILE), lambda g: (0, g))
    maps = lambda rows: pl.BlockSpec((rows, MAPS), lambda g: (0, DI // MAPS))
    pay = (TILE // 128 * chunks, STATE // chunks + 8, 128)
    return pcall(
        states_kernel,
        (groups,),
        [tile(span + HALO), maps(span + HALO), rate, full((span, 128)), tile(8), maps(8), full((8, 128))],
        [
            tile(span),
            full((span, MAPS)),
            full((4, span, 128)),
            full((128, span)),
            tile(STATE),
            tile(8),
            pl.BlockSpec(pay, lambda g: (g, 0, 0)),
            tile(span),
            full((span, MAPS)),
        ],
        [
            shape_of((span, DI)),
            shape_of((span, MAPS)),
            shape_of((4, span, 128)),
            shape_of((128, span)),
            shape_of((STATE, DI)),
            shape_of((8, DI)),
            shape_of((peers,) + pay[1:]),
            shape_of((span, DI)),
            shape_of((span, MAPS)),
        ],
        [vmem((span // GROUP, STATE, GROUP), jnp.bfloat16), vmem((KW - 1, span, 128))],
        (mixed_ext, mixed_ext, mixed_ext, aux, conv, conv, hp),
        flops=2 * span * DI * STATE,
        nbytes=12 * span * DI,
    )


def block_rows(span):
    wide = pl.BlockSpec((GROUP, DI), lambda b: (b, 0))
    maps = pl.BlockSpec((GROUP, MAPS), lambda b: (b, 0))
    col = pl.BlockSpec((4, GROUP, 128), lambda b: (0, b, 0))
    row = pl.BlockSpec((128, GROUP), lambda b: (0, b))
    aux = pl.BlockSpec((GROUP, 128), lambda b: (b, 0))
    auxr = pl.BlockSpec((8, GROUP), lambda b: (0, b))
    return wide, maps, col, row, aux, auxr


def inner(bc, values, col, cumr, aux, auxr):
    span = values.shape[0]
    wide, maps, cols, row, auxs, auxrs = block_rows(span)
    return pcall(
        inner_kernel,
        (span // GROUP,),
        [maps, wide, cols, row, auxs, auxrs],
        wide,
        shape_of((span, DI)),
        [vmem((GROUP, GROUP))],
        (bc, values, col, cumr, aux, auxr),
        flops=2 * span * GROUP * DI * 4,
        nbytes=8 * span * DI,
    )


def finish(yi, values, gate, bc, col, state_in, made, kx, ch):
    span = values.shape[0]
    wide = pl.BlockSpec((ROWS_STEP, DI), lambda b: (b, 0))
    maps = pl.BlockSpec((ROWS_STEP, MAPS), lambda b: (b, 0))
    cols = pl.BlockSpec((4, ROWS_STEP, 128), lambda b: (0, b, 0))
    return pcall(
        finish_kernel,
        (span // ROWS_STEP,),
        [wide, wide, wide, maps, cols, full((DI // 128, STATE, 128)), full((STATE, DI)), full((8, DI)), full((8, DI))],
        [wide, wide],
        [shape_of((span, DI)), shape_of((span, DI), jnp.bfloat16)],
        [vmem((ROWS_STEP, DI))],
        (yi, values, gate, bc, col, state_in, made, kx, ch),
        flops=2 * span * DI * STATE,
        nbytes=18 * span * DI,
    )


def gate_back(peers, dno, y, gate, values, bc, col, kx, ch, after=()):
    span = values.shape[0]
    chunks = peers * 128 // DI
    wide = pl.BlockSpec((ROWS_STEP, DI), lambda b: (b, 0))
    maps = pl.BlockSpec((ROWS_STEP, MAPS), lambda b: (b, 0))
    cols = pl.BlockSpec((4, ROWS_STEP, 128), lambda b: (0, b, 0))
    pay = (peers, STATE // chunks, 128)
    return pcall(
        gate_back_kernel,
        (span // ROWS_STEP,),
        [wide, wide, wide, wide, maps, cols, full((8, DI)), full((8, DI))],
        [wide, wide, full((8, DI)), full((STATE, DI)), full(pay)],
        [
            shape_of((span, DI)),
            shape_of((span, DI), jnp.bfloat16),
            shape_of((8, DI)),
            shape_of((STATE, DI)),
            shape_of(pay),
        ],
        [vmem((ROWS_STEP, DI)), vmem((2, ROWS_STEP, DI))],
        (dno, y, gate, values, bc, col, kx, ch),
        flops=2 * span * DI * STATE,
        nbytes=22 * span * DI,
        after=after,
    )


def inner_back(bc, values, dy, col, cumr, aux, auxr, after=()):
    span = values.shape[0]
    wide, maps, cols, row, auxs, auxrs = block_rows(span)
    return pcall(
        inner_back_kernel,
        (span // GROUP,),
        [maps, wide, wide, cols, row, auxs, auxrs],
        [wide, maps],
        [shape_of((span, DI)), shape_of((span, MAPS))],
        [vmem((GROUP, GROUP)), vmem((GROUP, GROUP))],
        (bc, values, dy, col, cumr, aux, auxr),
        flops=2 * span * GROUP * DI * 8,
        nbytes=12 * span * DI,
        after=after,
    )


def states_pre(xi, values, dy, yi, bc, col, state_in, made, kx, dbc, ch):
    span = values.shape[0]
    tile = lambda rows: pl.BlockSpec((rows, TILE), lambda g: (0, g))
    state = pl.BlockSpec((TILE // 128, STATE, 128), lambda g: (g, 0, 0))
    small, maps = full((span, 128)), full((span, MAPS))
    return pcall(
        states_pre_kernel,
        (DI // TILE,),
        [
            tile(span), tile(span), tile(span), tile(span), maps, full((4, span, 128)),
            state, tile(STATE), tile(8), maps, tile(8),
        ],
        [tile(span), small, small, maps],
        [shape_of((span, DI)), shape_of((span, 128)), shape_of((span, 128)), shape_of((span, MAPS))],
        [],
        (xi, values, dy, yi, bc, col, state_in, made, kx, dbc, ch),
        flops=4 * span * DI * STATE,
        nbytes=20 * span * DI,
    )


def states_back(base, values, slope, slope_bc, bc, col, dso, state_in, made, d1, kx, ds, dc, dmap, hp, mixed_ext):
    span = values.shape[0]
    tile = lambda rows: pl.BlockSpec((rows, TILE), lambda g: (0, g))
    state = pl.BlockSpec((TILE // 128, STATE, 128), lambda g: (g, 0, 0))
    small, maps = full((span, 128)), full((span, MAPS))
    rate = pl.BlockSpec((span + HALO, 128), lambda g: (0, CHANNELS // 128))
    return pcall(
        states_back_kernel,
        (DI // TILE,),
        [
            tile(span), tile(span), tile(span), maps, maps, full((4, span, 128)),
            state, state, tile(STATE), tile(STATE), tile(8), small, small, maps, full((8, 128)), rate,
        ],
        [tile(span), maps, small, full((8, 128))],
        [shape_of((span, DI)), shape_of((span, MAPS)), shape_of((span, 128), jnp.bfloat16), shape_of((8, 128))],
        [vmem((span, 128)), vmem((span, 128)), vmem((span // GROUP, 8, 128)), vmem((span, MAPS))],
        (base, values, slope, slope_bc, bc, col, dso, state_in, made, d1, kx, ds, dc, dmap, hp, mixed_ext),
        flops=4 * span * DI * STATE,
        nbytes=16 * span * DI,
    )


def conv_back(dconv, dconv_bc, drate, following, mixed_ext, aux, conv, after=()):
    span = dconv.shape[0]
    groups = DI // TILE
    tile = lambda rows: pl.BlockSpec((rows, TILE), lambda g: (0, g))
    return pcall(
        conv_back_kernel,
        (groups + 1,),
        [
            pl.BlockSpec((span, TILE), lambda g: (0, jnp.minimum(g, groups - 1))),
            full((span, MAPS)), full((span, 128)), tile(HALO), tile(span + HALO), full((span, 128)), tile(8),
        ],
        [tile(span), tile(8)],
        [shape_of((span, DI + TILE), jnp.bfloat16), shape_of((8, DI + TILE))],
        [vmem((KW - 1, span, 128))],
        (dconv, dconv_bc, drate, following, mixed_ext, aux, conv),
        flops=8 * span * DI,
        nbytes=10 * span * DI,
        after=after,
    )


def project(depth, hidden, before, gain, weight):
    span, width = hidden.shape
    columns = weight.shape[1]
    first, blocks = DI // TILE, pl.cdiv(columns - DI, TILE)
    return pcall(
        partial(project_kernel, columns, first),
        (blocks,),
        [
            full((span, width)), full((HALO, width)), full((1, width)),
            pl.BlockSpec((1, TILE, width), lambda g: (depth, first + g, 0)),
        ],
        [full((span, width)), pl.BlockSpec((span + HALO, TILE), lambda g: (0, g))],
        [shape_of((span, width), jnp.bfloat16), shape_of((span + HALO, blocks * TILE))],
        [vmem((span + HALO, width), jnp.bfloat16)],
        (hidden, before, gain[None], weight),
        flops=2 * span * width * blocks * TILE,
        nbytes=4 * span * blocks * TILE,
    )


def project_gate(depth, normed, weight):
    span, width = normed.shape
    return pcall(
        gate_kernel,
        (DI // TILE,),
        [full((span, width)), pl.BlockSpec((1, TILE, width), lambda g: (depth, g, 0))],
        pl.BlockSpec((span, TILE), lambda g: (0, g)),
        shape_of((span, DI)),
        [],
        (normed, weight),
        flops=2 * span * width * DI,
        nbytes=4 * span * DI,
    )


def project_back_gate(depth, dgate, weight, after=()):
    span, width = dgate.shape[0], weight.shape[2]
    return pcall(
        project_back_gate_kernel,
        (DI // TILE,),
        [pl.BlockSpec((span, TILE), lambda g: (0, g)), pl.BlockSpec((1, TILE, width), lambda g: (depth, g, 0))],
        full((span, width)),
        shape_of((span, width)),
        [],
        (dgate, weight),
        flops=2 * span * width * DI,
        nbytes=2 * width * DI,
        after=after,
    )


def project_back(depth, part, dmixed, weight, entry, gradient, gain, after=()):
    span, width = entry.shape
    columns = weight.shape[1]
    first, blocks = DI // TILE, pl.cdiv(columns - DI, TILE)
    return pcall(
        partial(project_back_kernel, columns, first),
        (blocks,),
        [
            full((span, width)),
            pl.BlockSpec((span, TILE), lambda g: (0, g)),
            pl.BlockSpec((1, TILE, width), lambda g: (depth, first + g, 0)),
            full((span, width)), full((span, width)), full((1, width)),
        ],
        [full((span, width)), full((span, width)), full((8, width))],
        [shape_of((span, width)), shape_of((span, width), jnp.bfloat16), shape_of((8, width))],
        [vmem((span, width))],
        (part, dmixed, weight, entry, gradient, gain[None]),
        flops=2 * span * width * (columns - DI),
        nbytes=4 * span * columns,
        after=after,
    )


def plain_weight(left, right, first, tiles, total=None, after=()):
    span, width = left.shape
    columns = right.shape[1]
    return pcall(
        plain_weight_kernel,
        (columns // 256,),
        [full((span, width)), pl.BlockSpec((span, 256), lambda g: (0, g))]
        + ([] if total is None else [pl.BlockSpec(memory_space=pltpu.HBM)]),
        pl.BlockSpec((width, 256), lambda g: (0, first + g)),
        shape_of((width, 256 * tiles)),
        [],
        (left, right) if total is None else (left, right, total),
        flops=2 * span * width * columns,
        nbytes=4 * width * columns,
        after=after,
        aliases={} if total is None else {2: 0},
    )


def scan_states(received, keeps, reverse, after=()):
    peers = received.shape[0]
    rows = STATE * DI // 128 // peers
    return pcall(
        partial(scan_kernel, reverse, rows),
        (1,),
        [full(received.shape), full(keeps.shape)],
        full((peers, rows, 128)),
        shape_of((peers, rows, 128)),
        [],
        (received, keeps),
        nbytes=8 * peers * rows * 128,
        after=after,
    )


def exchange(parts):
    return lax.all_to_all(parts, "seq", split_axis=0, concat_axis=0, tiled=True)


def shifted(value, steps):
    count = lax.axis_size("seq")
    first, last = max(0, -steps), min(count, count - steps)
    return lax.ppermute(value, "seq", [(source, source + steps) for source in range(first, last)])


def doc_table(lengths, first, count):
    starts = jnp.cumsum(lengths, -1) - lengths
    places = first + jnp.arange(count, dtype=jnp.int32)
    return jnp.sum((starts[None, :] <= places[:, None]).astype(jnp.int32), -1) - 1


def token_marks(lengths, span):
    docs_all = doc_table(lengths, lax.axis_index("seq") * span - HALO, span + 2 * HALO)
    docs = docs_all[HALO : HALO + span]
    ends = docs_all[HALO - 1 : HALO + span : GROUP]
    prior, final = jnp.repeat(ends[:-1], GROUP), jnp.repeat(ends[1:], GROUP)
    near = lambda step: docs_all[HALO + step : HALO + step + span] == docs
    marks = [near(-3), near(-2), near(-1), docs == prior, docs == final, docs, near(1), near(2), near(3)]
    marks = jnp.stack([mark.astype(jnp.float32) for mark in marks], 1)
    aux = jnp.pad(marks, ((0, 0), (0, 128 - marks.shape[1])))
    auxr = jnp.broadcast_to(docs.astype(jnp.float32)[None, :], (8, span))
    return aux, auxr


def halving(count, rows, turned=False):
    masks = [rows << bit for bit in range(count.bit_length() - 1)]
    near, far = masks[:2], masks[2:]
    pick = lambda pair: far + pair if turned else pair + far
    return [1 << bit for bit in range(rows.bit_length() - 1)], pick(near), pick(near[::-1])


def slab_order(turned=False):
    count, rows = lax.axis_size("seq"), lax.axis_size("rows")
    row_masks, even, odd = halving(count, rows, turned)
    stages = len(row_masks) + len(even)
    place = jnp.arange(count * rows, dtype=jnp.int32)
    bit = lambda stage: (place >> (stages - 1 - stage)) & 1
    slab = lax.axis_index("seq") * rows + lax.axis_index("rows") + 0 * place
    for stage, mask in enumerate(row_masks):
        slab = slab ^ (bit(stage) * mask)
    swapped = slab & 1
    for at, (one, two) in enumerate(zip(even, odd)):
        slab = slab ^ (bit(len(row_masks) + at) * jnp.where(swapped == 1, two, one))
    return slab


def in_order(values, order, after=()):
    span, width = values.shape
    size = width // order.shape[0]
    source = (order[:, None] * size + jnp.arange(size, dtype=jnp.int32)[None, :]).reshape(-1, 1)
    return pcall(
        sort_kernel,
        (width // 256,),
        [pl.BlockSpec((256, 1), lambda g: (g, 0)), full((span, width))],
        pl.BlockSpec((256, span), lambda g: (g, 0)),
        shape_of((width, span), jnp.bfloat16),
        [],
        (source, values),
        flops=2 * span * width * width,
        nbytes=4 * span * width,
        after=after,
    )


def weight_sums(devices, left, right, first=0, tiles=None, after=()):
    width, span = left.shape
    columns = right.shape[1] if tiles is None else 256 * tiles
    slabs = width // 2 // SUM_ROWS
    out = pl.BlockSpec((slabs, SUM_ROWS, 256), lambda g: (g, 0, 0))
    return pcall(
        partial(weight_kernel, width // devices),
        (columns // 256,),
        [full((width, span)), pl.BlockSpec((span, 256), lambda g: (0, first + g))],
        [out, out],
        [shape_of((columns // 256 * slabs, SUM_ROWS, 256))] * 2,
        [],
        (left, right),
        flops=2 * span * width * columns,
        nbytes=4 * width * columns,
        after=after,
    )


def summed(parts, after=()):
    count, rows = lax.axis_size("seq"), lax.axis_size("rows")
    orders = []
    for turned in (False, True):
        row_masks, even, odd = halving(count, rows, turned)
        masks = [("rows", mask, mask) for mask in row_masks]
        orders.append(masks + [("seq", one // rows, two // rows) for one, two in zip(even, odd)])
    counts = [send.shape[0] for send, _ in parts]
    chunks, stages = sum(counts), len(orders[0])
    last = SUM_ROWS >> (stages - 1)
    anywhere = pl.BlockSpec(memory_space=pltpu.HBM)

    def run(*refs):
        taken = 2 * len(parts)
        sums_kernel(counts, orders, *refs[:taken], *refs[taken + len(after) :])

    return pl.pallas_call(
        run,
        in_specs=[anywhere] * (2 * len(parts) + len(after)),
        out_specs=pl.BlockSpec(memory_space=pltpu.VMEM),
        out_shape=shape_of((chunks, last, 256)),
        scratch_shapes=[vmem((chunks, SUM_ROWS, 256))]
        + [vmem((chunks, SUM_ROWS >> stage, 256)) for stage in range(stages)]
        + [
            pltpu.SemaphoreType.DMA((chunks,)),
            pltpu.SemaphoreType.DMA((stages, chunks)),
            pltpu.SemaphoreType.DMA((stages, chunks)),
        ],
        compiler_params=pltpu.CompilerParams(
            vmem_limit_bytes=VMEM_BYTES, collective_id=0, has_side_effects=True
        ),
        cost_estimate=pl.CostEstimate(flops=0, bytes_accessed=400 * 1024 * 1024, transcendentals=0),
    )(*[send for send, _ in parts], *[keep for _, keep in parts], *after)


def scattered(total):
    return lax.psum_scatter(total, AXES, scatter_dimension=0, tiled=True)


def matmul(a, b):
    return jnp.dot(a, b, preferred_element_type=jnp.float32)


def matmul_tn(a, b):
    return jnp.einsum("tn,tm->nm", a, b, preferred_element_type=jnp.float32)


def matmul_nt(a, b):
    return jnp.einsum("tn,mn->tm", a, b, preferred_element_type=jnp.float32)


def padded(rows, width):
    table = jnp.stack([jnp.pad(row, (0, width - row.shape[0])) for row in rows])
    return jnp.pad(table, ((0, 8 - len(rows)), (0, 0)))


def local(
    inputs,
    lengths,
    norm_gain,
    in_weight,
    conv_weight,
    conv_bias,
    log_decay,
    dt_bias,
    skip,
    gate_gain,
    out_weight,
    cotangent,
):
    _, span, width = inputs.shape
    peers = lax.axis_size("seq")
    aux, auxr = token_marks(lengths[0], span)
    order = slab_order()
    in_weight = jnp.swapaxes(in_weight, 1, 2)
    hidden = inputs[0]
    saved = []
    for depth in range(LAYERS):
        conv = jnp.concatenate([conv_weight[depth].T, conv_bias[depth][None], jnp.zeros((3, CHANNELS), jnp.float32)])
        conv = jnp.pad(conv, ((0, 0), (0, DI + TILE - CHANNELS)))
        hp = padded([dt_bias[depth], -jnp.exp(log_decay[depth])], 128)
        ch = padded([jnp.repeat(skip[depth], HEAD_DIM), gate_gain[depth]], DI)
        before = shifted(hidden[span - HALO :], 1)
        normed, mixed_ext = project(depth, hidden, before, norm_gain[depth], in_weight)
        values, bc, col, cumr, made, kx, pay, slope, slope_bc = make_states(peers, mixed_ext, aux, conv, hp)
        received = exchange(pay)
        gate = project_gate(depth, normed, in_weight)
        keeps = received[:, -8:]
        waits = (gate,)
        if depth:
            ready = [in_order(values, by, after=(pay,)) for values, by in sorting]
            waits += tuple(ready)
        scanned = scan_states(received, keeps, False, after=waits)
        state_in = exchange(scanned).reshape(DI // 128, STATE, 128)
        yi = inner(bc, values, col, cumr, aux, auxr)
        y, out_low = finish(yi, values, gate, bc, col, state_in, made, kx, ch)
        saved.append(
            (hidden, normed, mixed_ext, gate, values, bc, col, cumr, made, kx, keeps, state_in, y, out_low, yi)
            + (slope, slope_bc, conv, hp, ch)
        )
        sorting = [(out_low, order), (normed, order), (normed, slab_order(True))]
        hidden = hidden + matmul(out_low, out_weight[depth])
    gradient = cotangent[0]
    grad_low = gradient.astype(jnp.bfloat16)
    devices = lax.axis_size(AXES)
    collected = [None] * LAYERS
    for depth in reversed(range(LAYERS)):
        entry, normed, mixed_ext, gate, values, bc, col, cumr, made, kx, keeps, state_in, y, out_low, yi = saved[depth][:15]
        slope, slope_bc, conv, hp, ch = saved[depth][15:]
        dno = matmul_nt(grad_low, out_weight[depth])
        dy, dgate, gate_sums, d1, pay = gate_back(peers, dno, y, gate, values, bc, col, kx, ch)
        received = exchange(pay)
        if depth:
            out_sorted = in_order(out_low, order, after=(pay,))
            high_chunks = weight_sums(devices, out_sorted, grad_low)
            waits = high_chunks[:1]
        else:
            out_sorted, normed_sorted, turned_sorted = ready
            out_chunks = weight_sums(devices, out_sorted, grad_low, after=(pay,))
            gate_chunks = weight_sums(devices, normed_sorted, dgate, after=out_chunks[:1])
            waits = (gate_chunks[0],)
        scanned = scan_states(received, keeps, True, after=waits)
        dso = exchange(scanned).reshape(DI // 128, STATE, 128)
        tiles = (DI + DI + TILE) // 256
        in_total = plain_weight(normed, dgate, 0, tiles, after=(scanned,)) if depth else None
        xi, dbc = inner_back(bc, values, dy, col, cumr, aux, auxr, after=(in_total,) if depth else ())
        base, ds, dc, dmap = states_pre(xi, values, dy, yi, bc, col, state_in, made, kx, dbc, ch)
        dconv, dconv_bc, drate, head_rows = states_back(
            base, values, slope, slope_bc, bc, col, dso, state_in, made, d1, kx, ds, dc, dmap, hp, mixed_ext
        )
        following = shifted(jnp.concatenate([dconv[:HALO], dconv_bc[:HALO]], 1), -1)
        part = project_back_gate(depth, dgate, in_weight, after=(head_rows,))
        dmixed, conv_sums = conv_back(dconv, dconv_bc, drate, following, mixed_ext, aux, conv, after=(part,))
        if depth:
            in_total = plain_weight(normed, dmixed, DI // 256, tiles, in_total)
            high_in = scattered(in_total)
            waits = (in_total,)
        else:
            others = [high_chunks, out_chunks, gate_chunks]
            count = sum(part[0].shape[0] for part in others) + dmixed.shape[1] // 256
            turned_tiles = pl.cdiv(count, EVERY)
            waits = ()
        gradient, grad_low, gain_sums = project_back(
            depth, part, dmixed, in_weight, entry, gradient, norm_gain[depth], after=waits
        )
        if depth == 0:
            turned_chunks = weight_sums(devices, turned_sorted, dmixed, 0, turned_tiles, after=(gain_sums,))
            rest_tiles = dmixed.shape[1] // 256 - turned_tiles
            rest_chunks = weight_sums(
                devices, normed_sorted, dmixed, turned_tiles, rest_tiles, after=turned_chunks[:1]
            )
        gain_grad = jnp.sum(gain_sums, 0)
        collected[depth] = (
            gain_grad,
            conv_sums[:KW, :CHANNELS].T,
            conv_sums[KW, :CHANNELS],
            gate_sums[0],
            head_rows[1, :HEADS],
            head_rows[0, :HEADS],
            jnp.sum(gate_sums[1].reshape(HEADS, HEAD_DIM), 1),
        )
    total = summed([turned_chunks, high_chunks, out_chunks, gate_chunks, rest_chunks], after=(gradient,))
    places = list(range(total.shape[0]))
    between = [place for place in places if place % EVERY]
    n_out = out_chunks[0].shape[0]
    n_gate = 2 * n_out + gate_chunks[0].shape[0]
    slabs = n_out * 256 // out_weight.shape[2]
    columns = between[2 * n_out : n_gate] + places[::EVERY] + between[n_gate:]
    columns = columns[: pl.cdiv(in_weight.shape[1], 256)]
    outs = [[between[first + part : first + n_out : slabs] for part in range(slabs)] for first in (n_out, 0)]
    shapes = [(LAYERS, slabs * total.shape[1], out_weight.shape[2]), (LAYERS, high_in.shape[0], in_weight.shape[1])]
    all_out, all_in = pcall(
        partial(assemble_kernel, outs, columns),
        (1,),
        [full(total.shape), full(high_in.shape)],
        [full(shape) for shape in shapes],
        [shape_of(shape) for shape in shapes],
        [],
        (total, high_in),
        nbytes=4 * 1024 * 1024,
    )
    shares = [part.reshape(devices, -1) for sums in collected for part in sums[:4]]
    heads = jnp.concatenate([part for sums in collected for part in sums[4:]])
    table = jnp.concatenate(shares + [jnp.broadcast_to(heads, (devices,) + heads.shape)], 1)
    table = jnp.pad(table, ((0, 0), (0, -table.shape[1] % 128)))
    table = lax.all_to_all(table, AXES, split_axis=0, concat_axis=0, tiled=True).reshape(devices, -1, 128)
    table = pcall(
        total_kernel,
        (1,),
        [full(table.shape)],
        full(table.shape[1:]),
        shape_of(table.shape[1:]),
        [],
        (table,),
    ).reshape(-1)
    small = []
    at = 0
    for sums in collected:
        row = []
        for part in sums[:4]:
            size = part.size // devices
            row.append(table[at : at + size].reshape((part.shape[0] // devices,) + part.shape[1:]))
            at += size
        small.append(row)
    for row in small:
        for _ in range(3):
            row.append(table[at : at + HEADS])
            at += HEADS
    stacked = [jnp.stack([small[level][member] for level in range(LAYERS)]) for member in range(7)]
    norm_gain_grad, conv_w_grad, conv_b_grad, gain_grad, decay_grad, bias_grad, skip_grad = stacked
    return (
        hidden[None],
        gradient[None],
        norm_gain_grad,
        all_in,
        conv_w_grad,
        conv_b_grad,
        decay_grad,
        bias_grad,
        skip_grad,
        gain_grad,
        all_out,
    )


def solution(mesh):
    in_specs = (
        P("rows", "seq", None),
        P("rows", None),
        P(),
        P(),
        P(),
        P(),
        P(),
        P(),
        P(),
        P(),
        P(),
        P("rows", "seq", None),
    )
    out_specs = (
        P("rows", "seq", None),
        P("rows", "seq", None),
        P(None, ("seq", "rows")),
        P(None, ("seq", "rows"), None),
        P(None, ("seq", "rows"), None),
        P(None, ("seq", "rows")),
        P(),
        P(),
        P(),
        P(None, ("seq", "rows")),
        P(None, ("seq", "rows"), None),
    )
    return jax.shard_map(local, mesh=mesh, in_specs=in_specs, out_specs=out_specs, check_vma=False)
```

```python
from functools import partial

import jax
import jax.numpy as jnp
from jax import lax
from jax.experimental import pallas as pl
from jax.experimental.pallas import tpu as pltpu
from jax.sharding import PartitionSpec as P

DI = 2048
STATE = 128
HEAD_DIM = 64
HEADS = DI // HEAD_DIM
KW = 4
SMALL_ROWS = 6 + KW
GROUP = 256
LAYERS = 2
CHANNELS = DI + 2 * STATE
TILE = 512
HEADS_AT = TILE // HEAD_DIM
MAPS = 2 * STATE
ROWS_STEP = 256
SUM_ROWS = 512
LAG = 3
AHEAD = 6
EVERY = 5
HALO = 8
HALF = 128
LOG2E = 1.4426950408889634
ROWS_AT = 64
ROWS_CONV = 64
VMEM_BYTES = 60 * 1024 * 1024

EPS = 1e-05
HIGHEST = lax.Precision.HIGHEST
AXES = ("seq", "rows")


def pcall(body, grid, in_specs, out_specs, out_shape, scratch, args, flops=0, nbytes=0, after=(), aliases={}):
    taken = len(args)

    def run(*refs):
        body(*refs[:taken], *refs[taken + len(after) :])

    return pl.pallas_call(
        run,
        grid=grid,
        in_specs=list(in_specs) + [pl.BlockSpec(memory_space=pltpu.HBM)] * len(after),
        out_specs=out_specs,
        out_shape=out_shape,
        scratch_shapes=scratch,
        input_output_aliases=aliases,
        compiler_params=pltpu.CompilerParams(vmem_limit_bytes=VMEM_BYTES),
        cost_estimate=pl.CostEstimate(flops=flops, bytes_accessed=nbytes, transcendentals=0),
    )(*args, *after)


def dot(a, b, dims=(((1,), (0,)), ((), ()))):
    return lax.dot_general(
        a.astype(jnp.bfloat16), b.astype(jnp.bfloat16), dims, preferred_element_type=jnp.float32
    )


def dot_nt(a, b):
    return dot(a, b, (((1,), (1,)), ((), ())))


def dot_exact(a, b):
    return jnp.dot(a, b, precision=HIGHEST, preferred_element_type=jnp.float32)


def sigmoid(v):
    return 0.5 * jnp.tanh(0.5 * v) + 0.5


def lane_iota(shape):
    return lax.broadcasted_iota(jnp.int32, shape, 1)


def low_half(rows):
    return lane_iota((rows, 128)) < HEAD_DIM


def to_heads(cols, first, pairs):
    rows = cols.shape[0]
    low = low_half(rows)
    parts = []
    for pair in range(pairs):
        at = first + 2 * pair
        parts.append(
            jnp.where(
                low,
                jnp.broadcast_to(cols[:, at : at + 1], (rows, 128)),
                jnp.broadcast_to(cols[:, at + 1 : at + 2], (rows, 128)),
            )
        )
    return jnp.concatenate(parts, 1) if pairs > 1 else parts[0]


def spread_heads(cols, pairs):
    pick = (
        lax.broadcasted_iota(jnp.int32, (128, 128 * pairs), 0) == lane_iota((128, 128 * pairs)) // HEAD_DIM
    ).astype(jnp.bfloat16)
    high = cols.astype(jnp.bfloat16)
    return dot(high, pick) + dot(cols - high.astype(jnp.float32), pick)


def head_pick(first, heads):
    shape = (128, HEAD_DIM * heads)
    return (lax.broadcasted_iota(jnp.int32, shape, 0) == first + lane_iota(shape) // HEAD_DIM).astype(jnp.bfloat16)


def picked_heads(cols, pick):
    high = cols.astype(jnp.bfloat16)
    return dot(high, pick) + dot(cols - high.astype(jnp.float32), pick)


def head_sums(first):
    channel = lax.broadcasted_iota(jnp.int32, (TILE, 128), 0)
    return (channel // HEAD_DIM + first == lane_iota((TILE, 128))).astype(jnp.bfloat16)


def keep_marks(marks_ref, aux_ref, lanes):
    for at, lane in enumerate(lanes):
        marks_ref[at] = jnp.broadcast_to(aux_ref[:, lane : lane + 1], marks_ref.shape[1:])


def conv_rows(x_ref, w_ref, marks_ref, first, count, lanes):
    total = w_ref[4:5, lanes] + w_ref[3:4, lanes] * x_ref[first + 8 : first + 8 + count, lanes]
    for tap in range(KW - 1):
        match = marks_ref[tap, first : first + count, :]
        total = total + w_ref[tap : tap + 1, lanes] * (x_ref[first + 5 + tap : first + 5 + tap + count, lanes] * match)
    return total


def chunks_of(rows, width):
    for pair in range(width // 128):
        for first in range(0, rows, ROWS_AT):
            yield first, slice(first, first + ROWS_AT), slice(pair * 128, (pair + 1) * 128)


def states_kernel(
    x_ref, xbc_ref, rate_ref, aux_ref, w_ref, wbc_ref, hp_ref,
    v_ref, bc_ref, col_ref, cumr_ref, made_ref, kx_ref, pay_ref, slope_ref, slope_bc_ref,
    bt_ref, marks_ref,
):
    turn = pl.program_id(0)
    span = v_ref.shape[0]
    count = span // GROUP

    @pl.when(turn == 0)
    def _():
        keep_marks(marks_ref, aux_ref, range(KW - 1))
        for first, rows, lanes in chunks_of(span, MAPS):
            conv = conv_rows(xbc_ref, wbc_ref, marks_ref, first, ROWS_AT, lanes)
            sig = sigmoid(conv)
            bc_ref[rows, lanes] = conv * sig
            slope_bc_ref[rows, lanes] = sig * (1.0 + conv * (1.0 - sig))
        tri = (
            lax.broadcasted_iota(jnp.int32, (GROUP, GROUP), 0) >= lane_iota((GROUP, GROUP))
        ).astype(jnp.float32)
        for block in range(count):
            rows = slice(block * GROUP, (block + 1) * GROUP)
            bt_ref[block] = bc_ref[rows, :STATE].T.astype(jnp.bfloat16)
            raw = rate_ref[HALO + block * GROUP : HALO + (block + 1) * GROUP, :] + hp_ref[0:1, :]
            step = jnp.maximum(raw, 0.0) + jnp.log1p(jnp.exp(-jnp.abs(raw)))
            cum = dot_exact(tri, hp_ref[1:2, :] * step)
            last = cum[GROUP - 1 :, :]
            col_ref[0, rows, :] = cum
            col_ref[1, rows, :] = step
            col_ref[2, rows, :] = jnp.exp(cum) * aux_ref[rows, 3:4]
            col_ref[3, rows, :] = jnp.exp(last - cum) * aux_ref[rows, 4:5]
            cumr_ref[:, rows] = cum.T

    for first, rows, lanes in chunks_of(span, TILE):
        conv = conv_rows(x_ref, w_ref, marks_ref, first, ROWS_AT, lanes)
        sig = sigmoid(conv)
        v_ref[rows, lanes] = conv * sig
        slope_ref[rows, lanes] = sig * (1.0 + conv * (1.0 - sig))
    pick = head_pick(turn * HEADS_AT, HEADS_AT)
    made = []
    keep = []
    for block in range(count):
        rows = slice(block * GROUP, (block + 1) * GROUP)
        weight = picked_heads(col_ref[3, rows, :] * col_ref[1, rows, :], pick)
        made.append(dot(bt_ref[block], weight * v_ref[rows, :]))
        ends = col_ref[2, (block + 1) * GROUP - 8 : (block + 1) * GROUP, :]
        keep.append(picked_heads(ends, pick)[7:8, :])
    made_ref[...] = made[0]
    kx_ref[...] = jnp.concatenate([keep[0], keep[1], jnp.zeros((6, TILE), jnp.float32)], 0)
    final = keep[1] * made[0] + made[1]
    total = jnp.broadcast_to(keep[0] * keep[1], (8, TILE))
    pairs = TILE // 128
    chunks = pay_ref.shape[0] // pairs
    size = STATE // chunks
    for pair in range(pairs):
        lanes = slice(pair * 128, (pair + 1) * 128)
        for chunk in range(chunks):
            pay_ref[pair * chunks + chunk, :size, :] = final[chunk * size : (chunk + 1) * size, lanes]
            pay_ref[pair * chunks + chunk, size:, :] = total[:, lanes]


def inner_kernel(bc_ref, v_ref, col_ref, cumr_ref, aux_ref, auxr_ref, y_ref, g_ref):
    scores = dot_nt(bc_ref[:, STATE:], bc_ref[:, :STATE])
    allowed = (aux_ref[:, 5:6] == auxr_ref[0:1, :]) & (
        lax.broadcasted_iota(jnp.int32, (GROUP, GROUP), 0) >= lane_iota((GROUP, GROUP))
    )
    g_ref[...] = jnp.where(allowed, scores, 0.0)
    low = low_half(GROUP)
    cum = LOG2E * col_ref[0]
    cum_row = LOG2E * cumr_ref[:HEADS, :]
    steps = picked_heads(col_ref[1], head_pick(0, HEADS))
    for pair in range(HEADS // 2):
        lanes = slice(pair * 128, (pair + 1) * 128)
        scaled = steps[:, lanes] * v_ref[:, lanes]
        result = None
        for half in range(2):
            head = 2 * pair + half
            row = cum_row[head : head + 1, :]
            tops, bottoms = [], []
            for first in range(0, GROUP, 64):
                width = HALF if first < HALF else GROUP
                spread = cum[first : first + 64, head : head + 1] - row[:, :width]
                decay = jnp.exp2(jnp.minimum(spread, 0.0))
                mixing = (g_ref[first : first + 64, :width] * decay).astype(jnp.bfloat16)
                (tops if first < HALF else bottoms).append(mixing)
            picked = jnp.where(low if half == 0 else ~low, scaled, 0.0).astype(jnp.bfloat16)
            top = dot(jnp.concatenate(tops, 0), picked[:HALF])
            bottom = dot(jnp.concatenate(bottoms, 0), picked)
            result = (top, bottom) if result is None else (result[0] + top, result[1] + bottom)
        y_ref[:HALF, lanes] = result[0]
        y_ref[HALF:, lanes] = result[1]


def finish_kernel(
    yi_ref, v_ref, gate_ref, bc_ref, col_ref, sin_ref, made_ref, kx_ref, ch_ref,
    y_ref, out_ref,
    gated_ref,
):
    later = pl.program_id(0) * ROWS_STEP >= GROUP
    out_map = bc_ref[:, STATE:].astype(jnp.bfloat16)
    entering = picked_heads(col_ref[2], head_pick(0, HEADS))
    total = [jnp.zeros((ROWS_AT, 128), jnp.float32) for _ in range(ROWS_STEP // ROWS_AT)]
    for pair in range(HEADS // 2):
        lanes = slice(pair * 128, (pair + 1) * 128)
        state = sin_ref[pair]
        state = jnp.where(later, kx_ref[0:1, lanes] * state + made_ref[:, lanes], state)
        outer = entering[:, lanes] * dot(out_map, state)
        for at in range(ROWS_STEP // ROWS_AT):
            rows = slice(at * ROWS_AT, (at + 1) * ROWS_AT)
            result = yi_ref[rows, lanes] + outer[rows] + ch_ref[0:1, lanes] * v_ref[rows, lanes]
            y_ref[rows, lanes] = result
            gate = gate_ref[rows, lanes]
            gated = result * (gate * sigmoid(gate))
            gated_ref[rows, lanes] = gated
            total[at] = total[at] + gated * gated
    for at in range(ROWS_STEP // ROWS_AT):
        rows = slice(at * ROWS_AT, (at + 1) * ROWS_AT)
        scale = lax.rsqrt(jnp.sum(total[at], 1, keepdims=True) / DI + EPS)
        out_ref[rows, :] = (gated_ref[rows, :] * scale * ch_ref[1:2, :]).astype(jnp.bfloat16)


def gate_back_kernel(
    dno_ref, y_ref, gate_ref, v_ref, bc_ref, col_ref, kx_ref, ch_ref,
    dy_ref, dgate_ref, sum_ref, d1_ref, pay_ref,
    gated_ref, silu_ref,
):
    at_step = pl.program_id(0)
    later = at_step * ROWS_STEP >= GROUP
    parts = ROWS_STEP // ROWS_AT
    square = [jnp.zeros((ROWS_AT, 128), jnp.float32) for _ in range(parts)]
    cross = [jnp.zeros((ROWS_AT, 128), jnp.float32) for _ in range(parts)]
    for first, rows, lanes in chunks_of(ROWS_STEP, DI):
        gate = gate_ref[rows, lanes]
        sig = sigmoid(gate)
        silu = gate * sig
        y = y_ref[rows, lanes]
        gated = y * silu
        gated_ref[rows, lanes] = gated
        silu_ref[0, rows, lanes] = silu
        silu_ref[1, rows, lanes] = y * (sig * (1.0 + gate * (1.0 - sig)))
        at = first // ROWS_AT
        square[at] = square[at] + gated * gated
        cross[at] = cross[at] + gated * (dno_ref[rows, lanes] * ch_ref[1:2, lanes])
    scales = [lax.rsqrt(jnp.sum(part, 1, keepdims=True) / DI + EPS) for part in square]
    pulls = [scale * scale * scale * (jnp.sum(part, 1, keepdims=True) / DI) for scale, part in zip(scales, cross)]
    out_t = bc_ref[:, STATE:].T.astype(jnp.bfloat16)
    entering = picked_heads(col_ref[2], head_pick(0, HEADS))
    pairs = DI // 128
    chunks = pay_ref.shape[0] // pairs
    size = STATE // chunks

    @pl.when(at_step == 0)
    def _():
        sum_ref[...] = jnp.zeros_like(sum_ref)
        pay_ref[...] = jnp.zeros_like(pay_ref)

    @pl.when((at_step == 0) | (at_step * ROWS_STEP == GROUP))
    def _():
        d1_ref[...] = jnp.zeros_like(d1_ref)

    for pair in range(pairs):
        lanes = slice(pair * 128, (pair + 1) * 128)
        gain_sum = jnp.zeros((8, 128), jnp.float32)
        skip_sum = jnp.zeros((8, 128), jnp.float32)
        weighted = []
        for at in range(parts):
            rows = slice(at * ROWS_AT, (at + 1) * ROWS_AT)
            gated = gated_ref[rows, lanes]
            dno = dno_ref[rows, lanes] * scales[at]
            dgated = dno * ch_ref[1:2, lanes] - gated * pulls[at]
            dy = dgated * silu_ref[0, rows, lanes]
            dy_ref[rows, lanes] = dy
            dgate_ref[rows, lanes] = (dgated * silu_ref[1, rows, lanes]).astype(jnp.bfloat16)
            gain_sum = gain_sum + jnp.sum((dno * gated).reshape(-1, 8, 128), 0)
            skip_sum = skip_sum + jnp.sum((dy * v_ref[rows, lanes]).reshape(-1, 8, 128), 0)
            weighted.append((entering[rows, lanes] * dy).astype(jnp.bfloat16))
        sum_ref[0:1, lanes] += jnp.sum(gain_sum, 0, keepdims=True)
        sum_ref[1:2, lanes] += jnp.sum(skip_sum, 0, keepdims=True)
        fresh = dot(out_t, jnp.concatenate(weighted, 0))
        d1_ref[:, lanes] += fresh
        more = jnp.where(later, kx_ref[0:1, lanes], 1.0) * fresh
        for chunk in range(chunks):
            pay_ref[pair * chunks + chunk] += more[chunk * size : (chunk + 1) * size]


def inner_back_kernel(
    bc_ref, v_ref, dy_ref, col_ref, cumr_ref, aux_ref, auxr_ref,
    x_ref, dbc_ref,
    g_ref, dg_ref,
):
    allowed = (aux_ref[:, 5:6] == auxr_ref[0:1, :]) & (
        lax.broadcasted_iota(jnp.int32, (GROUP, GROUP), 0) <= lane_iota((GROUP, GROUP))
    )
    g_ref[...] = jnp.where(allowed, dot_nt(bc_ref[:, :STATE], bc_ref[:, STATE:]), 0.0)
    dg_ref[...] = jnp.zeros_like(dg_ref)
    low = low_half(GROUP)
    cum = LOG2E * col_ref[0]
    cum_row = LOG2E * cumr_ref[:HEADS, :]
    steps = picked_heads(col_ref[1], head_pick(0, HEADS))
    for pair in range(HEADS // 2):
        lanes = slice(pair * 128, (pair + 1) * 128)
        scaled = steps[:, lanes] * v_ref[:, lanes]
        dy = dy_ref[:, lanes]
        dy_low = dy.astype(jnp.bfloat16)
        result = None
        grads = {}
        for half in range(2):
            head = 2 * pair + half
            row = cum_row[head : head + 1, :]
            mine = low if half == 0 else ~low
            picked = jnp.where(mine, scaled, 0.0).astype(jnp.bfloat16)
            top_grad = dot_nt(picked[:HALF], dy_low)
            bottom_grad = dot_nt(picked[HALF:], dy_low[HALF:])
            tops, bottoms = [], []
            for first in range(0, GROUP, 64):
                rows = slice(first, first + 64)
                top = first < HALF
                across = slice(0 if top else HALF, GROUP)
                spread = row[:, across] - cum[rows, head : head + 1]
                decay = jnp.exp2(jnp.minimum(spread, 0.0))
                (tops if top else bottoms).append((g_ref[rows, across] * decay).astype(jnp.bfloat16))
                part = (top_grad[rows] if top else bottom_grad[first - HALF : first - HALF + 64]) * decay
                if half == 0:
                    grads[first] = part
                else:
                    dg_ref[rows, across] += grads[first] + part
            dy_mine = jnp.where(mine, dy, 0.0).astype(jnp.bfloat16)
            top = dot(jnp.concatenate(tops, 0), dy_mine)
            bottom = dot(jnp.concatenate(bottoms, 0), dy_mine[HALF:])
            result = (top, bottom) if result is None else (result[0] + top, result[1] + bottom)
        x_ref[:HALF, lanes] = result[0]
        x_ref[HALF:, lanes] = result[1]
    dg = jnp.where(allowed, dg_ref[...], 0.0)
    dbc_ref[:, :STATE] = dot(dg, bc_ref[:, STATE:])
    dbc_ref[:, STATE:] = dot(dg.T, bc_ref[:, :STATE])


def states_pre_kernel(
    xi_ref, v_ref, dy_ref, yi_ref, bc_ref, col_ref, sin_ref, made_ref, kx_ref, dbc_ref, ch_ref,
    base_ref, ds_ref, dc_ref, dmap_ref,
):
    turn = pl.program_id(0)
    count = v_ref.shape[0] // GROUP

    @pl.when(turn == 0)
    def _():
        ds_ref[...] = jnp.zeros_like(ds_ref)
        dc_ref[...] = jnp.zeros_like(dc_ref)
        dmap_ref[...] = dbc_ref[...]

    sums = head_sums(turn * HEADS_AT)
    pick = head_pick(turn * HEADS_AT, HEADS_AT)
    state = jnp.concatenate([sin_ref[pair] for pair in range(TILE // 128)], 1)
    starts = [state, kx_ref[0:1, :] * state + made_ref[...]]
    for block in range(count):
        at = slice(block * GROUP, (block + 1) * GROUP)
        step = picked_heads(col_ref[1, at, :], pick)
        entering = picked_heads(col_ref[2, at, :], pick)
        outer = dot(bc_ref[at, STATE:], starts[block])
        kinds = {name: [] for name in ("ds", "dc", "low", "dy")}
        for first in range(0, GROUP, ROWS_AT):
            local = slice(first, first + ROWS_AT)
            rows = slice(block * GROUP + first, block * GROUP + first + ROWS_AT)
            pieces = {name: [] for name in kinds}
            for pair in range(TILE // 128):
                lanes = slice(pair * 128, (pair + 1) * 128)
                v = v_ref[rows, lanes]
                dy = dy_ref[rows, lanes]
                xi = xi_ref[rows, lanes]
                scaled = step[local, lanes] * v
                low = dy.astype(jnp.bfloat16).astype(jnp.float32)
                inside = low * yi_ref[rows, lanes] - scaled.astype(jnp.bfloat16).astype(jnp.float32) * xi
                inside = inside + dy * (entering[local, lanes] * outer[local, lanes])
                high = inside.astype(jnp.bfloat16)
                pieces["dc"].append(high)
                pieces["low"].append((inside - high.astype(jnp.float32)).astype(jnp.bfloat16))
                pieces["ds"].append((v * xi).astype(jnp.bfloat16))
                pieces["dy"].append((entering[local, lanes] * dy).astype(jnp.bfloat16))
                base_ref[rows, lanes] = step[local, lanes] * xi + ch_ref[0:1, lanes] * dy
            for name in kinds:
                kinds[name].append(jnp.concatenate(pieces[name], 1))
        whole = {name: jnp.concatenate(parts, 0) for name, parts in kinds.items()}
        ds_ref[at, :] += dot(whole["ds"], sums)
        dc_ref[at, :] += dot(whole["dc"], sums) + dot(whole["low"], sums)
        dmap_ref[at, STATE:] += dot_nt(whole["dy"], starts[block])


def states_back_kernel(
    base_ref, v_ref, slope_ref, slope_bc_ref, bc_ref, col_ref, dso_ref, sin_ref, made_ref, d1_ref,
    kx_ref, ds0_ref, dc_ref, dmap0_ref, hp_ref, rate_ref,
    dconv_ref, dconv_bc_ref, drate_ref, sum_ref,
    ds_ref, z_ref, kd_ref, dmap_ref,
):
    turn = pl.program_id(0)
    span = v_ref.shape[0]
    count = span // GROUP

    @pl.when(turn == 0)
    def _():
        ds_ref[...] = ds0_ref[...]
        z_ref[...] = jnp.zeros_like(z_ref)
        kd_ref[...] = jnp.zeros_like(kd_ref)
        dmap_ref[...] = dmap0_ref[...]

    sums = head_sums(turn * HEADS_AT)
    pick = head_pick(turn * HEADS_AT, HEADS_AT)
    end_grad = jnp.concatenate([dso_ref[pair] for pair in range(TILE // 128)], 1)
    state = jnp.concatenate([sin_ref[pair] for pair in range(TILE // 128)], 1)
    ends = [d1_ref[...] + kx_ref[1:2, :] * end_grad, end_grad]
    starts = [state, kx_ref[0:1, :] * state + made_ref[...]]
    for block in range(count):
        at = slice(block * GROUP, (block + 1) * GROUP)
        step = picked_heads(col_ref[1, at, :], pick)
        tail = picked_heads(col_ref[3, at, :], pick)
        from_end = dot(bc_ref[at, :STATE], ends[block])
        kinds = {name: [] for name in ("ds", "z", "values")}
        for first in range(0, GROUP, ROWS_AT):
            local = slice(first, first + ROWS_AT)
            rows = slice(block * GROUP + first, block * GROUP + first + ROWS_AT)
            pieces = {name: [] for name in kinds}
            for pair in range(TILE // 128):
                lanes = slice(pair * 128, (pair + 1) * 128)
                v = v_ref[rows, lanes]
                scaled = step[local, lanes] * v
                ended = tail[local, lanes] * from_end[local, lanes]
                pieces["ds"].append((v * ended).astype(jnp.bfloat16))
                pieces["z"].append((scaled * ended).astype(jnp.bfloat16))
                pieces["values"].append((tail[local, lanes] * scaled).astype(jnp.bfloat16))
                grad = base_ref[rows, lanes] + step[local, lanes] * ended
                dconv_ref[rows, lanes] = grad * slope_ref[rows, lanes]
            for name in kinds:
                kinds[name].append(jnp.concatenate(pieces[name], 1))
        whole = {name: jnp.concatenate(parts, 0) for name, parts in kinds.items()}
        ds_ref[at, :] += dot(whole["ds"], sums)
        z_ref[at, :] += dot(whole["z"], sums)
        dmap_ref[at, :STATE] += dot_nt(whole["values"], ends[block])
        kept = kx_ref[block : block + 1, :] * jnp.sum(ends[block] * starts[block], 0, keepdims=True)
        kd_ref[block] += dot_exact(jnp.broadcast_to(kept, (8, TILE)), sums.astype(jnp.float32))

    @pl.when(turn == pl.num_programs(0) - 1)
    def _():
        here = lax.broadcasted_iota(jnp.int32, (GROUP, GROUP), 0)
        after = (here <= lane_iota((GROUP, GROUP))).astype(jnp.float32)
        before = (here > lane_iota((GROUP, GROUP))).astype(jnp.float32)
        bias_sum = jnp.zeros((1, 128), jnp.float32)
        decay_sum = jnp.zeros((1, 128), jnp.float32)
        for first, rows, lanes in chunks_of(span, MAPS):
            dconv_bc_ref[rows, lanes] = dmap_ref[rows, lanes] * slope_bc_ref[rows, lanes]
        for block in range(count):
            rows = slice(block * GROUP, (block + 1) * GROUP)
            da = dot_exact(after, dc_ref[rows, :]) + kd_ref[block, 0:1, :]
            da = da + dot_exact(before, z_ref[rows, :])
            ds = ds_ref[rows, :] + hp_ref[1:2, :] * da
            drate = ds * sigmoid(rate_ref[HALO + block * GROUP : HALO + (block + 1) * GROUP, :] + hp_ref[0:1, :])
            drate_ref[rows, :] = drate.astype(jnp.bfloat16)
            bias_sum = bias_sum + jnp.sum(drate, 0, keepdims=True)
            decay_sum = decay_sum + jnp.sum(da * hp_ref[1:2, :] * col_ref[1, rows, :], 0, keepdims=True)
        sum_ref[...] = jnp.concatenate([bias_sum, decay_sum, jnp.zeros((6, 128), jnp.float32)], 0)


def conv_back_kernel(
    dconv_ref, dconv_bc_ref, drate_ref, next_ref, x_ref, aux_ref, w_ref, dx_ref, sum_ref, marks_ref
):
    turn = pl.program_id(0)
    last = pl.num_programs(0) - 1
    span = dconv_ref.shape[0]

    @pl.when(turn == 0)
    def _():
        keep_marks(marks_ref, aux_ref, (6, 7, 8))

    def tile(source_ref, width):
        for pair in range(width // 128):
            lanes = slice(pair * 128, (pair + 1) * 128)
            sums = [jnp.zeros((8, 128), jnp.float32) for _ in range(KW + 1)]
            weights = [jnp.broadcast_to(w_ref[tap : tap + 1, lanes], (8, 128)) for tap in range(KW)]
            for first in range(0, span, ROWS_CONV):
                rows = slice(first, first + ROWS_CONV)
                following = next_ref if first + ROWS_CONV == span else source_ref
                at = 0 if first + ROWS_CONV == span else first + ROWS_CONV
                here = source_ref[rows, lanes]
                whole = jnp.concatenate([here, following[at : at + 8, lanes]], 0)
                x = x_ref[HALO + first : HALO + first + ROWS_CONV, lanes]
                split = lambda v: v.reshape(ROWS_CONV // 8, 8, 128)
                x8, here8 = split(x), split(here)
                grad = weights[KW - 1] * here8
                sums[KW] = sums[KW] + jnp.sum(here8, 0)
                sums[KW - 1] = sums[KW - 1] + jnp.sum(here8 * x8, 0)
                for ahead in range(1, KW):
                    later = split(whole[ahead : ahead + ROWS_CONV] * marks_ref[ahead - 1, rows, :])
                    tap = KW - 1 - ahead
                    grad = grad + weights[tap] * later
                    sums[tap] = sums[tap] + jnp.sum(later * x8, 0)
                dx_ref[rows, lanes] = grad.reshape(ROWS_CONV, 128).astype(jnp.bfloat16)
            sums = [jnp.sum(part, 0, keepdims=True) for part in sums]
            sum_ref[:, lanes] = jnp.concatenate(sums + [jnp.zeros((3, 128), jnp.float32)], 0)

    @pl.when(turn < last)
    def _():
        tile(dconv_ref, TILE)

    @pl.when(turn == last)
    def _():
        tile(dconv_bc_ref, MAPS)
        sum_ref[:, MAPS:] = jnp.zeros_like(sum_ref[:, MAPS:])
        dx_ref[:, MAPS : MAPS + 128] = drate_ref[...]
        dx_ref[:, MAPS + 128 :] = jnp.zeros_like(drate_ref)


def scan_kernel(reverse, rows, in_ref, keep_ref, out_ref):
    peers = out_ref.shape[0]
    carried = jnp.zeros((rows, 128), jnp.float32)
    for at in range(peers):
        peer = peers - 1 - at if reverse else at
        out_ref[peer] = carried
        carried = keep_ref[peer, 0:1, :] * carried + in_ref[peer, :rows, :]


def weight_kernel(each, left_ref, right_ref, send_ref, keep_ref):
    slabs, size = send_ref.shape[0], SUM_ROWS
    total = dot(left_ref[...], right_ref[...])
    half = total.shape[0] // 2
    for out_ref, rows in ((keep_ref, total[:half]), (send_ref, total[half:])):
        if slabs == 1:
            out_ref[0] = rows
        else:
            split = rows.reshape(-1, slabs, each // slabs, rows.shape[1])
            for part in range(slabs):
                out_ref[part] = split[:, part].reshape(size, rows.shape[1])


def sums_kernel(counts, orders, *refs):
    pieces = len(counts)
    sends, keeps, out_ref, kept_ref = refs[:pieces], refs[pieces : 2 * pieces], refs[2 * pieces], refs[2 * pieces + 1]
    stages = len(orders[0])
    got = refs[2 * pieces + 2 : 2 * pieces + 2 + stages]
    load_sem, send_sem, recv_sem = refs[2 * pieces + 2 + stages :]
    chunks = sum(counts)
    seq, row = lax.axis_index("seq"), lax.axis_index("rows")
    odd = lax.rem(row, 2)

    def over(at, mask):
        return at + mask * (1 - 2 * lax.rem(at // mask, 2))

    routes = []
    for masks in orders:
        partners = []
        for axis, even_mask, odd_mask in masks:
            if axis == "rows":
                partners.append((seq, over(row, even_mask)))
            else:
                one, two = over(seq, even_mask), over(seq, odd_mask)
                partners.append((one + odd * (two - one), row))
        routes.append(partners)

    barrier = pltpu.get_barrier_semaphore()
    for partner in routes[0]:
        pl.semaphore_signal(
            barrier,
            inc=1,
            device_id={"seq": partner[0], "rows": partner[1]},
            device_id_type=pl.DeviceIdType.MESH,
        )
    pl.semaphore_wait(barrier, stages)

    def second(chunk):
        return (EVERY - lax.rem(chunk, EVERY)) // EVERY

    def copy(stage, chunk, source=None):
        size = SUM_ROWS >> stage
        other = second(chunk)
        main, side = routes[0][stage], routes[1][stage]
        if source is None:
            source = kept_ref.at[chunk] if stage == 0 else kept_ref.at[chunk, pl.ds(size, size)]
        return pltpu.make_async_remote_copy(
            src_ref=source,
            dst_ref=got[stage].at[chunk],
            send_sem=send_sem.at[stage, chunk],
            recv_sem=recv_sem.at[stage, chunk],
            device_id={
                "seq": main[0] + other * (side[0] - main[0]),
                "rows": main[1] + other * (side[1] - main[1]),
            },
            device_id_type=pl.DeviceIdType.MESH,
        )

    def load(chunk, source):
        return pltpu.make_async_copy(source, kept_ref.at[chunk], load_sem.at[chunk])

    def begin(chunk):
        side = second(chunk)
        inner = chunk - chunk // EVERY - 1

        @pl.when((side == 1) & (chunk < chunks))
        def _():
            copy(0, chunk, sends[0].at[chunk // EVERY]).start()
            load(chunk, keeps[0].at[chunk // EVERY]).start()

        base = 0
        for count, send_ref, keep_ref in zip(counts[1:], sends[1:], keeps[1:]):

            @pl.when((side == 0) & (inner >= base) & (inner < base + count))
            def _(base=base, send_ref=send_ref, keep_ref=keep_ref):
                copy(0, chunk, send_ref.at[inner - base]).start()
                load(chunk, keep_ref.at[inner - base]).start()

            base += count

    def first(chunk, _):
        begin(chunk)
        return 0

    lax.fori_loop(0, AHEAD, first, 0)

    def turn(at, _):
        begin(at + AHEAD)
        for stage in range(stages):
            chunk = at - LAG * stage

            @pl.when((chunk >= 0) & (chunk < chunks))
            def _():
                size = SUM_ROWS >> stage
                if stage == 0:
                    load(chunk, keeps[0].at[0]).wait()
                copy(stage, chunk, sends[0].at[0] if stage == 0 else None).wait_recv()
                total = kept_ref[chunk, :size] + got[stage][chunk]
                if stage + 1 < stages:
                    kept_ref[chunk, :size] = total
                    copy(stage + 1, chunk).start()
                else:
                    out_ref[chunk] = total

        return 0

    lax.fori_loop(0, chunks + LAG * (stages - 1), turn, 0)

    def ended(chunk, _):
        for stage in range(stages):
            copy(stage, chunk, sends[0].at[0] if stage == 0 else None).wait_send()
        return 0

    lax.fori_loop(0, chunks, ended, 0)


def edge(weights, width, first):
    row = lax.broadcasted_iota(jnp.int32, weights.shape, 0)
    return jnp.where(first + row < width, weights, jnp.zeros_like(weights))


def project_kernel(width, first_block, x_ref, before_ref, gain_ref, w_ref, normed_ref, out_ref, ext_ref):
    turn = pl.program_id(0)
    last = pl.num_programs(0) - 1

    @pl.when(turn == 0)
    def _():
        def scaled(values):
            scale = lax.rsqrt(jnp.mean(values * values, 1, keepdims=True) + EPS)
            return (values * scale * gain_ref[...]).astype(jnp.bfloat16)

        for first in range(0, x_ref.shape[0], ROWS_AT):
            rows = slice(first, first + ROWS_AT)
            normed_ref[rows, :] = scaled(x_ref[rows, :])
        ext_ref[...] = jnp.concatenate([scaled(before_ref[...]), normed_ref[...]], 0)

    @pl.when(turn < last)
    def _():
        out_ref[...] = dot_nt(ext_ref[...], w_ref[0])

    @pl.when(turn == last)
    def _():
        out_ref[...] = dot_nt(ext_ref[...], edge(w_ref[0], width, (first_block + last) * TILE))


def gate_kernel(normed_ref, w_ref, out_ref):
    out_ref[...] = dot_nt(normed_ref[...], w_ref[0])


def project_back_gate_kernel(dgate_ref, w_ref, out_ref):
    @pl.when(pl.program_id(0) == 0)
    def _():
        out_ref[...] = dot(dgate_ref[...], w_ref[0])

    @pl.when(pl.program_id(0) > 0)
    def _():
        out_ref[...] += dot(dgate_ref[...], w_ref[0])


def project_back_kernel(
    width, first_block, part_ref, dmixed_ref, w_ref, x_ref, grad_ref, gain_ref,
    new_ref, low_ref, sum_ref,
    acc_ref,
):
    turn = pl.program_id(0)
    last = pl.num_programs(0) - 1

    @pl.when(turn == 0)
    def _():
        acc_ref[...] = part_ref[...] + dot(dmixed_ref[...], w_ref[0])

    @pl.when((turn > 0) & (turn < last))
    def _():
        acc_ref[...] += dot(dmixed_ref[...], w_ref[0])

    @pl.when(turn == last)
    def _():
        acc_ref[...] += dot(dmixed_ref[...], edge(w_ref[0], width, (first_block + last) * TILE))
        total = jnp.zeros((8, x_ref.shape[1]), jnp.float32)
        for first in range(0, x_ref.shape[0], 16):
            rows = slice(first, first + 16)
            x = x_ref[rows, :]
            grad = acc_ref[rows, :]
            scale = lax.rsqrt(jnp.mean(x * x, 1, keepdims=True) + EPS)
            pulled = grad * gain_ref[...]
            cross = jnp.mean(pulled * x, 1, keepdims=True)
            scaled = x * scale
            total = total + grad[:8] * scaled[:8] + grad[8:] * scaled[8:]
            new = grad_ref[rows, :] + (scale * pulled - x * (scale * scale * scale * cross))
            new_ref[rows, :] = new
            low_ref[rows, :] = new.astype(jnp.bfloat16)
        sum_ref[...] = total


def plain_weight_kernel(left_ref, right_ref, *refs):
    out_ref = refs[-1]
    out_ref[...] = dot(left_ref[...], right_ref[...], (((0,), (0,)), ((), ())))


def sort_kernel(source_ref, values_ref, out_ref):
    pick = (source_ref[...] == lane_iota((source_ref.shape[0], values_ref.shape[1]))).astype(jnp.bfloat16)
    out_ref[...] = dot_nt(pick, values_ref[...]).astype(jnp.bfloat16)


def assemble_kernel(outs, ins, total_ref, in_ref, all_out_ref, all_in_ref):
    rows = total_ref.shape[1]
    for level, parts in enumerate(outs):
        for part, places in enumerate(parts):
            for at, place in enumerate(places):
                lanes = slice(at * 256, (at + 1) * 256)
                all_out_ref[level, part * rows : (part + 1) * rows, lanes] = total_ref[place]
    columns = all_in_ref.shape[2]
    for at, place in enumerate(ins):
        size = min(256, columns - at * 256)
        all_in_ref[0, :, at * 256 : at * 256 + size] = total_ref[place, :, :size]
    all_in_ref[1] = in_ref[:, :columns]


def small_kernel(in_ref, gain_ref, conv_ref, bias_ref, decay_ref, dt_ref, skip_ref, gate_ref):
    total = jnp.sum(in_ref[...], 0)
    for level in range(LAYERS):
        at = SMALL_ROWS * level
        row = lambda place, ref: total[at + place : at + place + 1, : ref.shape[1]]
        here = slice(level, level + 1)
        gain_ref[here, :] = row(0, gain_ref)
        taps = jnp.concatenate([total[at + 1 : at + 1 + KW], jnp.zeros((128 - KW, 128), jnp.float32)], 0)
        conv_ref[level] = taps.T[: conv_ref.shape[1], :KW]
        bias_ref[here, :] = row(1 + KW, bias_ref)
        gate_ref[here, :] = row(2 + KW, gate_ref)
        decay_ref[here, :] = row(3 + KW, decay_ref)
        dt_ref[here, :] = row(4 + KW, dt_ref)
        skip_ref[here, :] = row(5 + KW, skip_ref)


def full(shape):
    return pl.BlockSpec(shape, lambda *at: (0,) * len(shape))


def shape_of(dims, dtype=jnp.float32):
    return jax.ShapeDtypeStruct(dims, dtype)


def vmem(dims, dtype=jnp.float32):
    return pltpu.VMEM(dims, dtype)


def make_states(peers, mixed_ext, aux, conv, hp):
    span = aux.shape[0]
    rate = pl.BlockSpec((span + HALO, 128), lambda g: (0, CHANNELS // 128))
    groups = DI // TILE
    chunks = peers * 128 // DI
    tile = lambda rows: pl.BlockSpec((rows, TILE), lambda g: (0, g))
    maps = lambda rows: pl.BlockSpec((rows, MAPS), lambda g: (0, DI // MAPS))
    pay = (TILE // 128 * chunks, STATE // chunks + 8, 128)
    return pcall(
        states_kernel,
        (groups,),
        [tile(span + HALO), maps(span + HALO), rate, full((span, 128)), tile(8), maps(8), full((8, 128))],
        [
            tile(span),
            full((span, MAPS)),
            full((4, span, 128)),
            full((128, span)),
            tile(STATE),
            tile(8),
            pl.BlockSpec(pay, lambda g: (g, 0, 0)),
            tile(span),
            full((span, MAPS)),
        ],
        [
            shape_of((span, DI)),
            shape_of((span, MAPS)),
            shape_of((4, span, 128)),
            shape_of((128, span)),
            shape_of((STATE, DI)),
            shape_of((8, DI)),
            shape_of((peers,) + pay[1:]),
            shape_of((span, DI)),
            shape_of((span, MAPS)),
        ],
        [vmem((span // GROUP, STATE, GROUP), jnp.bfloat16), vmem((KW - 1, span, 128))],
        (mixed_ext, mixed_ext, mixed_ext, aux, conv, conv, hp),
        flops=2 * span * DI * STATE,
        nbytes=12 * span * DI,
    )


def block_rows(span):
    wide = pl.BlockSpec((GROUP, DI), lambda b: (b, 0))
    maps = pl.BlockSpec((GROUP, MAPS), lambda b: (b, 0))
    col = pl.BlockSpec((4, GROUP, 128), lambda b: (0, b, 0))
    row = pl.BlockSpec((128, GROUP), lambda b: (0, b))
    aux = pl.BlockSpec((GROUP, 128), lambda b: (b, 0))
    auxr = pl.BlockSpec((8, GROUP), lambda b: (0, b))
    return wide, maps, col, row, aux, auxr


def inner(bc, values, col, cumr, aux, auxr):
    span = values.shape[0]
    wide, maps, cols, row, auxs, auxrs = block_rows(span)
    return pcall(
        inner_kernel,
        (span // GROUP,),
        [maps, wide, cols, row, auxs, auxrs],
        wide,
        shape_of((span, DI)),
        [vmem((GROUP, GROUP))],
        (bc, values, col, cumr, aux, auxr),
        flops=2 * span * GROUP * DI * 4,
        nbytes=8 * span * DI,
    )


def finish(yi, values, gate, bc, col, state_in, made, kx, ch):
    span = values.shape[0]
    wide = pl.BlockSpec((ROWS_STEP, DI), lambda b: (b, 0))
    maps = pl.BlockSpec((ROWS_STEP, MAPS), lambda b: (b, 0))
    cols = pl.BlockSpec((4, ROWS_STEP, 128), lambda b: (0, b, 0))
    return pcall(
        finish_kernel,
        (span // ROWS_STEP,),
        [wide, wide, wide, maps, cols, full((DI // 128, STATE, 128)), full((STATE, DI)), full((8, DI)), full((8, DI))],
        [wide, wide],
        [shape_of((span, DI)), shape_of((span, DI), jnp.bfloat16)],
        [vmem((ROWS_STEP, DI))],
        (yi, values, gate, bc, col, state_in, made, kx, ch),
        flops=2 * span * DI * STATE,
        nbytes=18 * span * DI,
    )


def gate_back(peers, dno, y, gate, values, bc, col, kx, ch, after=()):
    span = values.shape[0]
    chunks = peers * 128 // DI
    wide = pl.BlockSpec((ROWS_STEP, DI), lambda b: (b, 0))
    maps = pl.BlockSpec((ROWS_STEP, MAPS), lambda b: (b, 0))
    cols = pl.BlockSpec((4, ROWS_STEP, 128), lambda b: (0, b, 0))
    pay = (peers, STATE // chunks, 128)
    return pcall(
        gate_back_kernel,
        (span // ROWS_STEP,),
        [wide, wide, wide, wide, maps, cols, full((8, DI)), full((8, DI))],
        [wide, wide, full((8, DI)), full((STATE, DI)), full(pay)],
        [
            shape_of((span, DI)),
            shape_of((span, DI), jnp.bfloat16),
            shape_of((8, DI)),
            shape_of((STATE, DI)),
            shape_of(pay),
        ],
        [vmem((ROWS_STEP, DI)), vmem((2, ROWS_STEP, DI))],
        (dno, y, gate, values, bc, col, kx, ch),
        flops=2 * span * DI * STATE,
        nbytes=22 * span * DI,
        after=after,
    )


def inner_back(bc, values, dy, col, cumr, aux, auxr, after=()):
    span = values.shape[0]
    wide, maps, cols, row, auxs, auxrs = block_rows(span)
    return pcall(
        inner_back_kernel,
        (span // GROUP,),
        [maps, wide, wide, cols, row, auxs, auxrs],
        [wide, maps],
        [shape_of((span, DI)), shape_of((span, MAPS))],
        [vmem((GROUP, GROUP)), vmem((GROUP, GROUP))],
        (bc, values, dy, col, cumr, aux, auxr),
        flops=2 * span * GROUP * DI * 8,
        nbytes=12 * span * DI,
        after=after,
    )


def states_pre(xi, values, dy, yi, bc, col, state_in, made, kx, dbc, ch):
    span = values.shape[0]
    tile = lambda rows: pl.BlockSpec((rows, TILE), lambda g: (0, g))
    state = pl.BlockSpec((TILE // 128, STATE, 128), lambda g: (g, 0, 0))
    small, maps = full((span, 128)), full((span, MAPS))
    return pcall(
        states_pre_kernel,
        (DI // TILE,),
        [
            tile(span), tile(span), tile(span), tile(span), maps, full((4, span, 128)),
            state, tile(STATE), tile(8), maps, tile(8),
        ],
        [tile(span), small, small, maps],
        [shape_of((span, DI)), shape_of((span, 128)), shape_of((span, 128)), shape_of((span, MAPS))],
        [],
        (xi, values, dy, yi, bc, col, state_in, made, kx, dbc, ch),
        flops=4 * span * DI * STATE,
        nbytes=20 * span * DI,
    )


def states_back(base, values, slope, slope_bc, bc, col, dso, state_in, made, d1, kx, ds, dc, dmap, hp, mixed_ext):
    span = values.shape[0]
    tile = lambda rows: pl.BlockSpec((rows, TILE), lambda g: (0, g))
    state = pl.BlockSpec((TILE // 128, STATE, 128), lambda g: (g, 0, 0))
    small, maps = full((span, 128)), full((span, MAPS))
    rate = pl.BlockSpec((span + HALO, 128), lambda g: (0, CHANNELS // 128))
    return pcall(
        states_back_kernel,
        (DI // TILE,),
        [
            tile(span), tile(span), tile(span), maps, maps, full((4, span, 128)),
            state, state, tile(STATE), tile(STATE), tile(8), small, small, maps, full((8, 128)), rate,
        ],
        [tile(span), maps, small, full((8, 128))],
        [shape_of((span, DI)), shape_of((span, MAPS)), shape_of((span, 128), jnp.bfloat16), shape_of((8, 128))],
        [vmem((span, 128)), vmem((span, 128)), vmem((span // GROUP, 8, 128)), vmem((span, MAPS))],
        (base, values, slope, slope_bc, bc, col, dso, state_in, made, d1, kx, ds, dc, dmap, hp, mixed_ext),
        flops=4 * span * DI * STATE,
        nbytes=16 * span * DI,
    )


def conv_back(dconv, dconv_bc, drate, following, mixed_ext, aux, conv, after=()):
    span = dconv.shape[0]
    groups = DI // TILE
    tile = lambda rows: pl.BlockSpec((rows, TILE), lambda g: (0, g))
    return pcall(
        conv_back_kernel,
        (groups + 1,),
        [
            pl.BlockSpec((span, TILE), lambda g: (0, jnp.minimum(g, groups - 1))),
            full((span, MAPS)), full((span, 128)), tile(HALO), tile(span + HALO), full((span, 128)), tile(8),
        ],
        [tile(span), tile(8)],
        [shape_of((span, DI + TILE), jnp.bfloat16), shape_of((8, DI + TILE))],
        [vmem((KW - 1, span, 128))],
        (dconv, dconv_bc, drate, following, mixed_ext, aux, conv),
        flops=8 * span * DI,
        nbytes=10 * span * DI,
        after=after,
    )


def project(depth, hidden, before, gain, weight):
    span, width = hidden.shape
    columns = weight.shape[1]
    first, blocks = DI // TILE, pl.cdiv(columns - DI, TILE)
    return pcall(
        partial(project_kernel, columns, first),
        (blocks,),
        [
            full((span, width)), full((HALO, width)), full((1, width)),
            pl.BlockSpec((1, TILE, width), lambda g: (depth, first + g, 0)),
        ],
        [full((span, width)), pl.BlockSpec((span + HALO, TILE), lambda g: (0, g))],
        [shape_of((span, width), jnp.bfloat16), shape_of((span + HALO, blocks * TILE))],
        [vmem((span + HALO, width), jnp.bfloat16)],
        (hidden, before, gain[None], weight),
        flops=2 * span * width * blocks * TILE,
        nbytes=4 * span * blocks * TILE,
    )


def project_gate(depth, normed, weight):
    span, width = normed.shape
    return pcall(
        gate_kernel,
        (DI // TILE,),
        [full((span, width)), pl.BlockSpec((1, TILE, width), lambda g: (depth, g, 0))],
        pl.BlockSpec((span, TILE), lambda g: (0, g)),
        shape_of((span, DI)),
        [],
        (normed, weight),
        flops=2 * span * width * DI,
        nbytes=4 * span * DI,
    )


def project_back_gate(depth, dgate, weight, after=()):
    span, width = dgate.shape[0], weight.shape[2]
    return pcall(
        project_back_gate_kernel,
        (DI // TILE,),
        [pl.BlockSpec((span, TILE), lambda g: (0, g)), pl.BlockSpec((1, TILE, width), lambda g: (depth, g, 0))],
        full((span, width)),
        shape_of((span, width)),
        [],
        (dgate, weight),
        flops=2 * span * width * DI,
        nbytes=2 * width * DI,
        after=after,
    )


def project_back(depth, part, dmixed, weight, entry, gradient, gain, after=()):
    span, width = entry.shape
    columns = weight.shape[1]
    first, blocks = DI // TILE, pl.cdiv(columns - DI, TILE)
    return pcall(
        partial(project_back_kernel, columns, first),
        (blocks,),
        [
            full((span, width)),
            pl.BlockSpec((span, TILE), lambda g: (0, g)),
            pl.BlockSpec((1, TILE, width), lambda g: (depth, first + g, 0)),
            full((span, width)), full((span, width)), full((1, width)),
        ],
        [full((span, width)), full((span, width)), full((8, width))],
        [shape_of((span, width)), shape_of((span, width), jnp.bfloat16), shape_of((8, width))],
        [vmem((span, width))],
        (part, dmixed, weight, entry, gradient, gain[None]),
        flops=2 * span * width * (columns - DI),
        nbytes=4 * span * columns,
        after=after,
    )


def plain_weight(left, right, first, tiles, total=None, after=()):
    span, width = left.shape
    columns = right.shape[1]
    return pcall(
        plain_weight_kernel,
        (columns // 256,),
        [full((span, width)), pl.BlockSpec((span, 256), lambda g: (0, g))]
        + ([] if total is None else [pl.BlockSpec(memory_space=pltpu.HBM)]),
        pl.BlockSpec((width, 256), lambda g: (0, first + g)),
        shape_of((width, 256 * tiles)),
        [],
        (left, right) if total is None else (left, right, total),
        flops=2 * span * width * columns,
        nbytes=4 * width * columns,
        after=after,
        aliases={} if total is None else {2: 0},
    )


def scan_states(received, keeps, reverse, after=()):
    peers = received.shape[0]
    rows = STATE * DI // 128 // peers
    return pcall(
        partial(scan_kernel, reverse, rows),
        (1,),
        [full(received.shape), full(keeps.shape)],
        full((peers, rows, 128)),
        shape_of((peers, rows, 128)),
        [],
        (received, keeps),
        nbytes=8 * peers * rows * 128,
        after=after,
    )


def exchange(parts):
    return lax.all_to_all(parts, "seq", split_axis=0, concat_axis=0, tiled=True)


def shifted(value, steps):
    count = lax.axis_size("seq")
    first, last = max(0, -steps), min(count, count - steps)
    return lax.ppermute(value, "seq", [(source, source + steps) for source in range(first, last)])


def doc_table(lengths, first, count):
    starts = jnp.cumsum(lengths, -1) - lengths
    places = first + jnp.arange(count, dtype=jnp.int32)
    return jnp.sum((starts[None, :] <= places[:, None]).astype(jnp.int32), -1) - 1


def token_marks(lengths, span):
    docs_all = doc_table(lengths, lax.axis_index("seq") * span - HALO, span + 2 * HALO)
    docs = docs_all[HALO : HALO + span]
    ends = docs_all[HALO - 1 : HALO + span : GROUP]
    prior, final = jnp.repeat(ends[:-1], GROUP), jnp.repeat(ends[1:], GROUP)
    near = lambda step: docs_all[HALO + step : HALO + step + span] == docs
    marks = [near(-3), near(-2), near(-1), docs == prior, docs == final, docs, near(1), near(2), near(3)]
    marks = jnp.stack([mark.astype(jnp.float32) for mark in marks], 1)
    aux = jnp.pad(marks, ((0, 0), (0, 128 - marks.shape[1])))
    auxr = jnp.broadcast_to(docs.astype(jnp.float32)[None, :], (8, span))
    return aux, auxr


def halving(count, rows, turned=False):
    masks = [rows << bit for bit in range(count.bit_length() - 1)]
    near, far = masks[:2], masks[2:]
    pick = lambda pair: far + pair if turned else pair + far
    return [1 << bit for bit in range(rows.bit_length() - 1)], pick(near), pick(near[::-1])


def slab_order(turned=False):
    count, rows = lax.axis_size("seq"), lax.axis_size("rows")
    row_masks, even, odd = halving(count, rows, turned)
    stages = len(row_masks) + len(even)
    place = jnp.arange(count * rows, dtype=jnp.int32)
    bit = lambda stage: (place >> (stages - 1 - stage)) & 1
    slab = lax.axis_index("seq") * rows + lax.axis_index("rows") + 0 * place
    for stage, mask in enumerate(row_masks):
        slab = slab ^ (bit(stage) * mask)
    swapped = slab & 1
    for at, (one, two) in enumerate(zip(even, odd)):
        slab = slab ^ (bit(len(row_masks) + at) * jnp.where(swapped == 1, two, one))
    return slab


def in_order(values, order, after=()):
    span, width = values.shape
    size = width // order.shape[0]
    source = (order[:, None] * size + jnp.arange(size, dtype=jnp.int32)[None, :]).reshape(-1, 1)
    return pcall(
        sort_kernel,
        (width // 256,),
        [pl.BlockSpec((256, 1), lambda g: (g, 0)), full((span, width))],
        pl.BlockSpec((256, span), lambda g: (g, 0)),
        shape_of((width, span), jnp.bfloat16),
        [],
        (source, values),
        flops=2 * span * width * width,
        nbytes=4 * span * width,
        after=after,
    )


def weight_sums(devices, left, right, first=0, tiles=None, after=()):
    width, span = left.shape
    columns = right.shape[1] if tiles is None else 256 * tiles
    slabs = width // 2 // SUM_ROWS
    out = pl.BlockSpec((slabs, SUM_ROWS, 256), lambda g: (g, 0, 0))
    return pcall(
        partial(weight_kernel, width // devices),
        (columns // 256,),
        [full((width, span)), pl.BlockSpec((span, 256), lambda g: (0, first + g))],
        [out, out],
        [shape_of((columns // 256 * slabs, SUM_ROWS, 256))] * 2,
        [],
        (left, right),
        flops=2 * span * width * columns,
        nbytes=4 * width * columns,
        after=after,
    )


def summed(parts, after=()):
    count, rows = lax.axis_size("seq"), lax.axis_size("rows")
    orders = []
    for turned in (False, True):
        row_masks, even, odd = halving(count, rows, turned)
        masks = [("rows", mask, mask) for mask in row_masks]
        orders.append(masks + [("seq", one // rows, two // rows) for one, two in zip(even, odd)])
    counts = [send.shape[0] for send, _ in parts]
    chunks, stages = sum(counts), len(orders[0])
    last = SUM_ROWS >> (stages - 1)
    anywhere = pl.BlockSpec(memory_space=pltpu.HBM)

    def run(*refs):
        taken = 2 * len(parts)
        sums_kernel(counts, orders, *refs[:taken], *refs[taken + len(after) :])

    return pl.pallas_call(
        run,
        in_specs=[anywhere] * (2 * len(parts) + len(after)),
        out_specs=pl.BlockSpec(memory_space=pltpu.VMEM),
        out_shape=shape_of((chunks, last, 256)),
        scratch_shapes=[vmem((chunks, SUM_ROWS, 256))]
        + [vmem((chunks, SUM_ROWS >> stage, 256)) for stage in range(stages)]
        + [
            pltpu.SemaphoreType.DMA((chunks,)),
            pltpu.SemaphoreType.DMA((stages, chunks)),
            pltpu.SemaphoreType.DMA((stages, chunks)),
        ],
        compiler_params=pltpu.CompilerParams(
            vmem_limit_bytes=VMEM_BYTES, collective_id=0, has_side_effects=True
        ),
        cost_estimate=pl.CostEstimate(flops=0, bytes_accessed=400 * 1024 * 1024, transcendentals=0),
    )(*[send for send, _ in parts], *[keep for _, keep in parts], *after)


def scattered(total):
    return lax.psum_scatter(total, AXES, scatter_dimension=0, tiled=True)


def matmul(a, b):
    return jnp.dot(a, b, preferred_element_type=jnp.float32)


def matmul_tn(a, b):
    return jnp.einsum("tn,tm->nm", a, b, preferred_element_type=jnp.float32)


def matmul_nt(a, b):
    return jnp.einsum("tn,mn->tm", a, b, preferred_element_type=jnp.float32)


def padded(rows, width):
    table = jnp.stack([jnp.pad(row, (0, width - row.shape[0])) for row in rows])
    return jnp.pad(table, ((0, 8 - len(rows)), (0, 0)))


def local(
    inputs,
    lengths,
    norm_gain,
    in_weight,
    conv_weight,
    conv_bias,
    log_decay,
    dt_bias,
    skip,
    gate_gain,
    out_weight,
    cotangent,
):
    _, span, width = inputs.shape
    peers = lax.axis_size("seq")
    aux, auxr = token_marks(lengths[0], span)
    order = slab_order()
    in_weight = jnp.swapaxes(in_weight, 1, 2)
    hidden = inputs[0]
    saved = []
    for depth in range(LAYERS):
        conv = jnp.concatenate([conv_weight[depth].T, conv_bias[depth][None], jnp.zeros((3, CHANNELS), jnp.float32)])
        conv = jnp.pad(conv, ((0, 0), (0, DI + TILE - CHANNELS)))
        hp = padded([dt_bias[depth], -jnp.exp(log_decay[depth])], 128)
        ch = padded([jnp.repeat(skip[depth], HEAD_DIM), gate_gain[depth]], DI)
        before = shifted(hidden[span - HALO :], 1)
        normed, mixed_ext = project(depth, hidden, before, norm_gain[depth], in_weight)
        values, bc, col, cumr, made, kx, pay, slope, slope_bc = make_states(peers, mixed_ext, aux, conv, hp)
        received = exchange(pay)
        gate = project_gate(depth, normed, in_weight)
        keeps = received[:, -8:]
        waits = (gate,)
        if depth:
            ready = [in_order(values, by, after=(pay,)) for values, by in sorting]
            waits += tuple(ready)
        scanned = scan_states(received, keeps, False, after=waits)
        state_in = exchange(scanned).reshape(DI // 128, STATE, 128)
        yi = inner(bc, values, col, cumr, aux, auxr)
        y, out_low = finish(yi, values, gate, bc, col, state_in, made, kx, ch)
        saved.append(
            (hidden, normed, mixed_ext, gate, values, bc, col, cumr, made, kx, keeps, state_in, y, out_low, yi)
            + (slope, slope_bc, conv, hp, ch)
        )
        sorting = [(out_low, order), (normed, order), (normed, slab_order(True))]
        hidden = hidden + matmul(out_low, out_weight[depth])
    gradient = cotangent[0]
    grad_low = gradient.astype(jnp.bfloat16)
    devices = lax.axis_size(AXES)
    collected = [None] * LAYERS
    for depth in reversed(range(LAYERS)):
        entry, normed, mixed_ext, gate, values, bc, col, cumr, made, kx, keeps, state_in, y, out_low, yi = saved[depth][:15]
        slope, slope_bc, conv, hp, ch = saved[depth][15:]
        dno = matmul_nt(grad_low, out_weight[depth])
        dy, dgate, gate_sums, d1, pay = gate_back(peers, dno, y, gate, values, bc, col, kx, ch)
        received = exchange(pay)
        if depth:
            out_sorted = in_order(out_low, order, after=(pay,))
            high_chunks = weight_sums(devices, out_sorted, grad_low)
            waits = high_chunks[:1]
        else:
            out_sorted, normed_sorted, turned_sorted = ready
            out_chunks = weight_sums(devices, out_sorted, grad_low, after=(pay,))
            gate_chunks = weight_sums(devices, normed_sorted, dgate, after=out_chunks[:1])
            waits = (gate_chunks[0],)
        scanned = scan_states(received, keeps, True, after=waits)
        dso = exchange(scanned).reshape(DI // 128, STATE, 128)
        tiles = (DI + DI + TILE) // 256
        in_total = plain_weight(normed, dgate, 0, tiles, after=(scanned,)) if depth else None
        xi, dbc = inner_back(bc, values, dy, col, cumr, aux, auxr, after=(in_total,) if depth else ())
        base, ds, dc, dmap = states_pre(xi, values, dy, yi, bc, col, state_in, made, kx, dbc, ch)
        dconv, dconv_bc, drate, head_rows = states_back(
            base, values, slope, slope_bc, bc, col, dso, state_in, made, d1, kx, ds, dc, dmap, hp, mixed_ext
        )
        following = shifted(jnp.concatenate([dconv[:HALO], dconv_bc[:HALO]], 1), -1)
        part = project_back_gate(depth, dgate, in_weight, after=(head_rows,))
        dmixed, conv_sums = conv_back(dconv, dconv_bc, drate, following, mixed_ext, aux, conv, after=(part,))
        if depth:
            in_total = plain_weight(normed, dmixed, DI // 256, tiles, in_total)
            high_in = scattered(in_total)
            waits = (in_total,)
        else:
            others = [high_chunks, out_chunks, gate_chunks]
            count = sum(part[0].shape[0] for part in others) + dmixed.shape[1] // 256
            turned_tiles = pl.cdiv(count, EVERY)
            waits = ()
        gradient, grad_low, gain_sums = project_back(
            depth, part, dmixed, in_weight, entry, gradient, norm_gain[depth], after=waits
        )
        if depth == 0:
            turned_chunks = weight_sums(devices, turned_sorted, dmixed, 0, turned_tiles, after=(gain_sums,))
            rest_tiles = dmixed.shape[1] // 256 - turned_tiles
            rest_chunks = weight_sums(
                devices, normed_sorted, dmixed, turned_tiles, rest_tiles, after=turned_chunks[:1]
            )
        gain_grad = jnp.sum(gain_sums, 0)
        spread = lambda part: jnp.moveaxis(part.reshape(part.shape[0], devices, -1), 0, 1)
        widened = lambda part: jnp.pad(part, ((0, 0), (0, 0), (0, 128 - part.shape[2])))
        skip_sums = jnp.sum(gate_sums[1].reshape(HEADS, HEAD_DIM), 1)
        heads = jnp.stack([head_rows[1], head_rows[0], jnp.pad(skip_sums, (0, 128 - HEADS))])
        collected[depth] = jnp.concatenate(
            [
                widened(spread(gain_grad[None])),
                widened(spread(conv_sums[: KW + 1, :CHANNELS])),
                widened(spread(gate_sums[:1])),
                jnp.broadcast_to(heads, (devices,) + heads.shape),
            ],
            1,
        )
    total = summed([turned_chunks, high_chunks, out_chunks, gate_chunks, rest_chunks], after=(gradient,))
    places = list(range(total.shape[0]))
    between = [place for place in places if place % EVERY]
    n_out = out_chunks[0].shape[0]
    n_gate = 2 * n_out + gate_chunks[0].shape[0]
    slabs = n_out * 256 // out_weight.shape[2]
    columns = between[2 * n_out : n_gate] + places[::EVERY] + between[n_gate:]
    columns = columns[: pl.cdiv(in_weight.shape[1], 256)]
    outs = [[between[first + part : first + n_out : slabs] for part in range(slabs)] for first in (n_out, 0)]
    shapes = [(LAYERS, slabs * total.shape[1], out_weight.shape[2]), (LAYERS, high_in.shape[0], in_weight.shape[1])]
    all_out, all_in = pcall(
        partial(assemble_kernel, outs, columns),
        (1,),
        [full(total.shape), full(high_in.shape)],
        [full(shape) for shape in shapes],
        [shape_of(shape) for shape in shapes],
        [],
        (total, high_in),
        nbytes=4 * 1024 * 1024,
    )
    table = jnp.concatenate(collected, 1)
    table = jnp.pad(table, ((0, 0), (0, -table.shape[1] % 8), (0, 0)))
    table = lax.all_to_all(table, AXES, split_axis=0, concat_axis=0, tiled=True)
    mine = lambda whole: (LAYERS, whole.shape[1] // devices) + whole.shape[2:]
    shapes = [mine(norm_gain), mine(conv_weight), mine(conv_bias)] + [(LAYERS, HEADS)] * 3 + [mine(gate_gain)]
    norm_gain_grad, conv_w_grad, conv_b_grad, decay_grad, bias_grad, skip_grad, gain_grad = pcall(
        small_kernel,
        (1,),
        [full(table.shape)],
        [full(shape) for shape in shapes],
        [shape_of(shape) for shape in shapes],
        [],
        (table,),
        nbytes=4 * table.size,
    )
    return (
        hidden[None],
        gradient[None],
        norm_gain_grad,
        all_in,
        conv_w_grad,
        conv_b_grad,
        decay_grad,
        bias_grad,
        skip_grad,
        gain_grad,
        all_out,
    )


def solution(mesh):
    in_specs = (
        P("rows", "seq", None),
        P("rows", None),
        P(),
        P(),
        P(),
        P(),
        P(),
        P(),
        P(),
        P(),
        P(),
        P("rows", "seq", None),
    )
    out_specs = (
        P("rows", "seq", None),
        P("rows", "seq", None),
        P(None, ("seq", "rows")),
        P(None, ("seq", "rows"), None),
        P(None, ("seq", "rows"), None),
        P(None, ("seq", "rows")),
        P(),
        P(),
        P(),
        P(None, ("seq", "rows")),
        P(None, ("seq", "rows"), None),
    )
    return jax.shard_map(local, mesh=mesh, in_specs=in_specs, out_specs=out_specs, check_vma=False)
```

```python
from functools import partial

import jax
import jax.numpy as jnp
from jax import lax
from jax.experimental import pallas as pl
from jax.experimental.pallas import tpu as pltpu
from jax.sharding import PartitionSpec as P

DI = 2048
STATE = 128
HEAD_DIM = 64
HEADS = DI // HEAD_DIM
KW = 4
SMALL_ROWS = 6 + KW
GROUP = 256
LAYERS = 2
CHANNELS = DI + 2 * STATE
TILE = 512
HEADS_AT = TILE // HEAD_DIM
MAPS = 2 * STATE
ROWS_STEP = 256
SUM_ROWS = 512
LAG = 3
AHEAD = 6
EVERY = 6
HALO = 8
HALF = 128
LOG2E = 1.4426950408889634
ROWS_AT = 64
ROWS_CONV = 64
VMEM_BYTES = 60 * 1024 * 1024

EPS = 1e-05
HIGHEST = lax.Precision.HIGHEST
AXES = ("seq", "rows")


def pcall(body, grid, in_specs, out_specs, out_shape, scratch, args, flops=0, nbytes=0, after=(), aliases={}):
    taken = len(args)

    def run(*refs):
        body(*refs[:taken], *refs[taken + len(after) :])

    return pl.pallas_call(
        run,
        grid=grid,
        in_specs=list(in_specs) + [pl.BlockSpec(memory_space=pltpu.HBM)] * len(after),
        out_specs=out_specs,
        out_shape=out_shape,
        scratch_shapes=scratch,
        input_output_aliases=aliases,
        compiler_params=pltpu.CompilerParams(vmem_limit_bytes=VMEM_BYTES),
        cost_estimate=pl.CostEstimate(flops=flops, bytes_accessed=nbytes, transcendentals=0),
    )(*args, *after)


def dot(a, b, dims=(((1,), (0,)), ((), ()))):
    return lax.dot_general(
        a.astype(jnp.bfloat16), b.astype(jnp.bfloat16), dims, preferred_element_type=jnp.float32
    )


def dot_nt(a, b):
    return dot(a, b, (((1,), (1,)), ((), ())))


def dot_exact(a, b):
    return jnp.dot(a, b, precision=HIGHEST, preferred_element_type=jnp.float32)


def sigmoid(v):
    return 0.5 * jnp.tanh(0.5 * v) + 0.5


def lane_iota(shape):
    return lax.broadcasted_iota(jnp.int32, shape, 1)


def low_half(rows):
    return lane_iota((rows, 128)) < HEAD_DIM


def to_heads(cols, first, pairs):
    rows = cols.shape[0]
    low = low_half(rows)
    parts = []
    for pair in range(pairs):
        at = first + 2 * pair
        parts.append(
            jnp.where(
                low,
                jnp.broadcast_to(cols[:, at : at + 1], (rows, 128)),
                jnp.broadcast_to(cols[:, at + 1 : at + 2], (rows, 128)),
            )
        )
    return jnp.concatenate(parts, 1) if pairs > 1 else parts[0]


def spread_heads(cols, pairs):
    pick = (
        lax.broadcasted_iota(jnp.int32, (128, 128 * pairs), 0) == lane_iota((128, 128 * pairs)) // HEAD_DIM
    ).astype(jnp.bfloat16)
    high = cols.astype(jnp.bfloat16)
    return dot(high, pick) + dot(cols - high.astype(jnp.float32), pick)


def head_pick(first, heads):
    shape = (128, HEAD_DIM * heads)
    return (lax.broadcasted_iota(jnp.int32, shape, 0) == first + lane_iota(shape) // HEAD_DIM).astype(jnp.bfloat16)


def picked_heads(cols, pick):
    high = cols.astype(jnp.bfloat16)
    return dot(high, pick) + dot(cols - high.astype(jnp.float32), pick)


def head_sums(first):
    channel = lax.broadcasted_iota(jnp.int32, (TILE, 128), 0)
    return (channel // HEAD_DIM + first == lane_iota((TILE, 128))).astype(jnp.bfloat16)


def keep_marks(marks_ref, aux_ref, lanes):
    for at, lane in enumerate(lanes):
        marks_ref[at] = jnp.broadcast_to(aux_ref[:, lane : lane + 1], marks_ref.shape[1:])


def conv_rows(x_ref, w_ref, marks_ref, first, count, lanes):
    total = w_ref[4:5, lanes] + w_ref[3:4, lanes] * x_ref[first + 8 : first + 8 + count, lanes]
    for tap in range(KW - 1):
        match = marks_ref[tap, first : first + count, :]
        total = total + w_ref[tap : tap + 1, lanes] * (x_ref[first + 5 + tap : first + 5 + tap + count, lanes] * match)
    return total


def chunks_of(rows, width):
    for pair in range(width // 128):
        for first in range(0, rows, ROWS_AT):
            yield first, slice(first, first + ROWS_AT), slice(pair * 128, (pair + 1) * 128)


def states_kernel(
    x_ref, xbc_ref, rate_ref, aux_ref, w_ref, wbc_ref, hp_ref,
    v_ref, bc_ref, col_ref, cumr_ref, made_ref, kx_ref, pay_ref, slope_ref, slope_bc_ref,
    bt_ref, marks_ref,
):
    turn = pl.program_id(0)
    span = v_ref.shape[0]
    count = span // GROUP

    @pl.when(turn == 0)
    def _():
        keep_marks(marks_ref, aux_ref, range(KW - 1))
        for first, rows, lanes in chunks_of(span, MAPS):
            conv = conv_rows(xbc_ref, wbc_ref, marks_ref, first, ROWS_AT, lanes)
            sig = sigmoid(conv)
            bc_ref[rows, lanes] = conv * sig
            slope_bc_ref[rows, lanes] = sig * (1.0 + conv * (1.0 - sig))
        tri = (
            lax.broadcasted_iota(jnp.int32, (GROUP, GROUP), 0) >= lane_iota((GROUP, GROUP))
        ).astype(jnp.float32)
        for block in range(count):
            rows = slice(block * GROUP, (block + 1) * GROUP)
            bt_ref[block] = bc_ref[rows, :STATE].T.astype(jnp.bfloat16)
            raw = rate_ref[HALO + block * GROUP : HALO + (block + 1) * GROUP, :] + hp_ref[0:1, :]
            step = jnp.maximum(raw, 0.0) + jnp.log1p(jnp.exp(-jnp.abs(raw)))
            cum = dot_exact(tri, hp_ref[1:2, :] * step)
            last = cum[GROUP - 1 :, :]
            col_ref[0, rows, :] = cum
            col_ref[1, rows, :] = step
            col_ref[2, rows, :] = jnp.exp(cum) * aux_ref[rows, 3:4]
            col_ref[3, rows, :] = jnp.exp(last - cum) * aux_ref[rows, 4:5]
            cumr_ref[:, rows] = cum.T

    for first, rows, lanes in chunks_of(span, TILE):
        conv = conv_rows(x_ref, w_ref, marks_ref, first, ROWS_AT, lanes)
        sig = sigmoid(conv)
        v_ref[rows, lanes] = conv * sig
        slope_ref[rows, lanes] = sig * (1.0 + conv * (1.0 - sig))
    pick = head_pick(turn * HEADS_AT, HEADS_AT)
    made = []
    keep = []
    for block in range(count):
        rows = slice(block * GROUP, (block + 1) * GROUP)
        weight = picked_heads(col_ref[3, rows, :] * col_ref[1, rows, :], pick)
        made.append(dot(bt_ref[block], weight * v_ref[rows, :]))
        ends = col_ref[2, (block + 1) * GROUP - 8 : (block + 1) * GROUP, :]
        keep.append(picked_heads(ends, pick)[7:8, :])
    made_ref[...] = made[0]
    kx_ref[...] = jnp.concatenate([keep[0], keep[1], jnp.zeros((6, TILE), jnp.float32)], 0)
    final = keep[1] * made[0] + made[1]
    total = jnp.broadcast_to(keep[0] * keep[1], (8, TILE))
    pairs = TILE // 128
    chunks = pay_ref.shape[0] // pairs
    size = STATE // chunks
    for pair in range(pairs):
        lanes = slice(pair * 128, (pair + 1) * 128)
        for chunk in range(chunks):
            pay_ref[pair * chunks + chunk, :size, :] = final[chunk * size : (chunk + 1) * size, lanes]
            pay_ref[pair * chunks + chunk, size:, :] = total[:, lanes]


def inner_kernel(bc_ref, v_ref, col_ref, cumr_ref, aux_ref, auxr_ref, y_ref, g_ref):
    scores = dot_nt(bc_ref[:, STATE:], bc_ref[:, :STATE])
    allowed = (aux_ref[:, 5:6] == auxr_ref[0:1, :]) & (
        lax.broadcasted_iota(jnp.int32, (GROUP, GROUP), 0) >= lane_iota((GROUP, GROUP))
    )
    g_ref[...] = jnp.where(allowed, scores, 0.0)
    low = low_half(GROUP)
    cum = LOG2E * col_ref[0]
    cum_row = LOG2E * cumr_ref[:HEADS, :]
    steps = picked_heads(col_ref[1], head_pick(0, HEADS))
    for pair in range(HEADS // 2):
        lanes = slice(pair * 128, (pair + 1) * 128)
        scaled = steps[:, lanes] * v_ref[:, lanes]
        result = None
        for half in range(2):
            head = 2 * pair + half
            row = cum_row[head : head + 1, :]
            tops, bottoms = [], []
            for first in range(0, GROUP, 64):
                width = HALF if first < HALF else GROUP
                spread = cum[first : first + 64, head : head + 1] - row[:, :width]
                decay = jnp.exp2(jnp.minimum(spread, 0.0))
                mixing = (g_ref[first : first + 64, :width] * decay).astype(jnp.bfloat16)
                (tops if first < HALF else bottoms).append(mixing)
            picked = jnp.where(low if half == 0 else ~low, scaled, 0.0).astype(jnp.bfloat16)
            top = dot(jnp.concatenate(tops, 0), picked[:HALF])
            bottom = dot(jnp.concatenate(bottoms, 0), picked)
            result = (top, bottom) if result is None else (result[0] + top, result[1] + bottom)
        y_ref[:HALF, lanes] = result[0]
        y_ref[HALF:, lanes] = result[1]


def finish_kernel(
    yi_ref, v_ref, gate_ref, bc_ref, col_ref, sin_ref, made_ref, kx_ref, ch_ref,
    y_ref, out_ref,
    gated_ref,
):
    later = pl.program_id(0) * ROWS_STEP >= GROUP
    out_map = bc_ref[:, STATE:].astype(jnp.bfloat16)
    entering = picked_heads(col_ref[2], head_pick(0, HEADS))
    total = [jnp.zeros((ROWS_AT, 128), jnp.float32) for _ in range(ROWS_STEP // ROWS_AT)]
    for pair in range(HEADS // 2):
        lanes = slice(pair * 128, (pair + 1) * 128)
        state = sin_ref[pair]
        state = jnp.where(later, kx_ref[0:1, lanes] * state + made_ref[:, lanes], state)
        outer = entering[:, lanes] * dot(out_map, state)
        for at in range(ROWS_STEP // ROWS_AT):
            rows = slice(at * ROWS_AT, (at + 1) * ROWS_AT)
            result = yi_ref[rows, lanes] + outer[rows] + ch_ref[0:1, lanes] * v_ref[rows, lanes]
            y_ref[rows, lanes] = result
            gate = gate_ref[rows, lanes]
            gated = result * (gate * sigmoid(gate))
            gated_ref[rows, lanes] = gated
            total[at] = total[at] + gated * gated
    for at in range(ROWS_STEP // ROWS_AT):
        rows = slice(at * ROWS_AT, (at + 1) * ROWS_AT)
        scale = lax.rsqrt(jnp.sum(total[at], 1, keepdims=True) / DI + EPS)
        out_ref[rows, :] = (gated_ref[rows, :] * scale * ch_ref[1:2, :]).astype(jnp.bfloat16)


def gate_back_kernel(
    dno_ref, y_ref, gate_ref, v_ref, bc_ref, col_ref, kx_ref, ch_ref,
    dy_ref, dgate_ref, sum_ref, d1_ref, pay_ref,
    gated_ref, silu_ref,
):
    at_step = pl.program_id(0)
    later = at_step * ROWS_STEP >= GROUP
    parts = ROWS_STEP // ROWS_AT
    square = [jnp.zeros((ROWS_AT, 128), jnp.float32) for _ in range(parts)]
    cross = [jnp.zeros((ROWS_AT, 128), jnp.float32) for _ in range(parts)]
    for first, rows, lanes in chunks_of(ROWS_STEP, DI):
        gate = gate_ref[rows, lanes]
        sig = sigmoid(gate)
        silu = gate * sig
        y = y_ref[rows, lanes]
        gated = y * silu
        gated_ref[rows, lanes] = gated
        silu_ref[0, rows, lanes] = silu
        silu_ref[1, rows, lanes] = y * (sig * (1.0 + gate * (1.0 - sig)))
        at = first // ROWS_AT
        square[at] = square[at] + gated * gated
        cross[at] = cross[at] + gated * (dno_ref[rows, lanes] * ch_ref[1:2, lanes])
    scales = [lax.rsqrt(jnp.sum(part, 1, keepdims=True) / DI + EPS) for part in square]
    pulls = [scale * scale * scale * (jnp.sum(part, 1, keepdims=True) / DI) for scale, part in zip(scales, cross)]
    out_t = bc_ref[:, STATE:].T.astype(jnp.bfloat16)
    entering = picked_heads(col_ref[2], head_pick(0, HEADS))
    pairs = DI // 128
    chunks = pay_ref.shape[0] // pairs
    size = STATE // chunks

    @pl.when(at_step == 0)
    def _():
        sum_ref[...] = jnp.zeros_like(sum_ref)
        pay_ref[...] = jnp.zeros_like(pay_ref)

    @pl.when((at_step == 0) | (at_step * ROWS_STEP == GROUP))
    def _():
        d1_ref[...] = jnp.zeros_like(d1_ref)

    for pair in range(pairs):
        lanes = slice(pair * 128, (pair + 1) * 128)
        gain_sum = jnp.zeros((8, 128), jnp.float32)
        skip_sum = jnp.zeros((8, 128), jnp.float32)
        weighted = []
        for at in range(parts):
            rows = slice(at * ROWS_AT, (at + 1) * ROWS_AT)
            gated = gated_ref[rows, lanes]
            dno = dno_ref[rows, lanes] * scales[at]
            dgated = dno * ch_ref[1:2, lanes] - gated * pulls[at]
            dy = dgated * silu_ref[0, rows, lanes]
            dy_ref[rows, lanes] = dy
            dgate_ref[rows, lanes] = (dgated * silu_ref[1, rows, lanes]).astype(jnp.bfloat16)
            gain_sum = gain_sum + jnp.sum((dno * gated).reshape(-1, 8, 128), 0)
            skip_sum = skip_sum + jnp.sum((dy * v_ref[rows, lanes]).reshape(-1, 8, 128), 0)
            weighted.append((entering[rows, lanes] * dy).astype(jnp.bfloat16))
        sum_ref[0:1, lanes] += jnp.sum(gain_sum, 0, keepdims=True)
        sum_ref[1:2, lanes] += jnp.sum(skip_sum, 0, keepdims=True)
        fresh = dot(out_t, jnp.concatenate(weighted, 0))
        d1_ref[:, lanes] += fresh
        more = jnp.where(later, kx_ref[0:1, lanes], 1.0) * fresh
        for chunk in range(chunks):
            pay_ref[pair * chunks + chunk] += more[chunk * size : (chunk + 1) * size]


def inner_back_kernel(
    bc_ref, v_ref, dy_ref, col_ref, cumr_ref, aux_ref, auxr_ref,
    x_ref, dbc_ref,
    g_ref, dg_ref,
):
    allowed = (aux_ref[:, 5:6] == auxr_ref[0:1, :]) & (
        lax.broadcasted_iota(jnp.int32, (GROUP, GROUP), 0) <= lane_iota((GROUP, GROUP))
    )
    g_ref[...] = jnp.where(allowed, dot_nt(bc_ref[:, :STATE], bc_ref[:, STATE:]), 0.0)
    dg_ref[...] = jnp.zeros_like(dg_ref)
    low = low_half(GROUP)
    cum = LOG2E * col_ref[0]
    cum_row = LOG2E * cumr_ref[:HEADS, :]
    steps = picked_heads(col_ref[1], head_pick(0, HEADS))
    for pair in range(HEADS // 2):
        lanes = slice(pair * 128, (pair + 1) * 128)
        scaled = steps[:, lanes] * v_ref[:, lanes]
        dy = dy_ref[:, lanes]
        dy_low = dy.astype(jnp.bfloat16)
        result = None
        grads = {}
        for half in range(2):
            head = 2 * pair + half
            row = cum_row[head : head + 1, :]
            mine = low if half == 0 else ~low
            picked = jnp.where(mine, scaled, 0.0).astype(jnp.bfloat16)
            top_grad = dot_nt(picked[:HALF], dy_low)
            bottom_grad = dot_nt(picked[HALF:], dy_low[HALF:])
            tops, bottoms = [], []
            for first in range(0, GROUP, 64):
                rows = slice(first, first + 64)
                top = first < HALF
                across = slice(0 if top else HALF, GROUP)
                spread = row[:, across] - cum[rows, head : head + 1]
                decay = jnp.exp2(jnp.minimum(spread, 0.0))
                (tops if top else bottoms).append((g_ref[rows, across] * decay).astype(jnp.bfloat16))
                part = (top_grad[rows] if top else bottom_grad[first - HALF : first - HALF + 64]) * decay
                if half == 0:
                    grads[first] = part
                else:
                    dg_ref[rows, across] += grads[first] + part
            dy_mine = jnp.where(mine, dy, 0.0).astype(jnp.bfloat16)
            top = dot(jnp.concatenate(tops, 0), dy_mine)
            bottom = dot(jnp.concatenate(bottoms, 0), dy_mine[HALF:])
            result = (top, bottom) if result is None else (result[0] + top, result[1] + bottom)
        x_ref[:HALF, lanes] = result[0]
        x_ref[HALF:, lanes] = result[1]
    dg = jnp.where(allowed, dg_ref[...], 0.0)
    dbc_ref[:, :STATE] = dot(dg, bc_ref[:, STATE:])
    dbc_ref[:, STATE:] = dot(dg.T, bc_ref[:, :STATE])


def states_pre_kernel(
    xi_ref, v_ref, dy_ref, yi_ref, bc_ref, col_ref, sin_ref, made_ref, kx_ref, dbc_ref, ch_ref,
    base_ref, ds_ref, dc_ref, dmap_ref,
):
    turn = pl.program_id(0)
    count = v_ref.shape[0] // GROUP

    @pl.when(turn == 0)
    def _():
        ds_ref[...] = jnp.zeros_like(ds_ref)
        dc_ref[...] = jnp.zeros_like(dc_ref)
        dmap_ref[...] = dbc_ref[...]

    sums = head_sums(turn * HEADS_AT)
    pick = head_pick(turn * HEADS_AT, HEADS_AT)
    state = jnp.concatenate([sin_ref[pair] for pair in range(TILE // 128)], 1)
    starts = [state, kx_ref[0:1, :] * state + made_ref[...]]
    for block in range(count):
        at = slice(block * GROUP, (block + 1) * GROUP)
        step = picked_heads(col_ref[1, at, :], pick)
        entering = picked_heads(col_ref[2, at, :], pick)
        outer = dot(bc_ref[at, STATE:], starts[block])
        kinds = {name: [] for name in ("ds", "dc", "low", "dy")}
        for first in range(0, GROUP, ROWS_AT):
            local = slice(first, first + ROWS_AT)
            rows = slice(block * GROUP + first, block * GROUP + first + ROWS_AT)
            pieces = {name: [] for name in kinds}
            for pair in range(TILE // 128):
                lanes = slice(pair * 128, (pair + 1) * 128)
                v = v_ref[rows, lanes]
                dy = dy_ref[rows, lanes]
                xi = xi_ref[rows, lanes]
                scaled = step[local, lanes] * v
                low = dy.astype(jnp.bfloat16).astype(jnp.float32)
                inside = low * yi_ref[rows, lanes] - scaled.astype(jnp.bfloat16).astype(jnp.float32) * xi
                inside = inside + dy * (entering[local, lanes] * outer[local, lanes])
                high = inside.astype(jnp.bfloat16)
                pieces["dc"].append(high)
                pieces["low"].append((inside - high.astype(jnp.float32)).astype(jnp.bfloat16))
                pieces["ds"].append((v * xi).astype(jnp.bfloat16))
                pieces["dy"].append((entering[local, lanes] * dy).astype(jnp.bfloat16))
                base_ref[rows, lanes] = step[local, lanes] * xi + ch_ref[0:1, lanes] * dy
            for name in kinds:
                kinds[name].append(jnp.concatenate(pieces[name], 1))
        whole = {name: jnp.concatenate(parts, 0) for name, parts in kinds.items()}
        ds_ref[at, :] += dot(whole["ds"], sums)
        dc_ref[at, :] += dot(whole["dc"], sums) + dot(whole["low"], sums)
        dmap_ref[at, STATE:] += dot_nt(whole["dy"], starts[block])


def states_back_kernel(
    base_ref, v_ref, slope_ref, slope_bc_ref, bc_ref, col_ref, dso_ref, sin_ref, made_ref, d1_ref,
    kx_ref, ds0_ref, dc_ref, dmap0_ref, hp_ref, rate_ref,
    dconv_ref, dconv_bc_ref, drate_ref, sum_ref,
    ds_ref, z_ref, kd_ref, dmap_ref,
):
    turn = pl.program_id(0)
    span = v_ref.shape[0]
    count = span // GROUP

    @pl.when(turn == 0)
    def _():
        ds_ref[...] = ds0_ref[...]
        z_ref[...] = jnp.zeros_like(z_ref)
        kd_ref[...] = jnp.zeros_like(kd_ref)
        dmap_ref[...] = dmap0_ref[...]

    sums = head_sums(turn * HEADS_AT)
    pick = head_pick(turn * HEADS_AT, HEADS_AT)
    end_grad = jnp.concatenate([dso_ref[pair] for pair in range(TILE // 128)], 1)
    state = jnp.concatenate([sin_ref[pair] for pair in range(TILE // 128)], 1)
    ends = [d1_ref[...] + kx_ref[1:2, :] * end_grad, end_grad]
    starts = [state, kx_ref[0:1, :] * state + made_ref[...]]
    for block in range(count):
        at = slice(block * GROUP, (block + 1) * GROUP)
        step = picked_heads(col_ref[1, at, :], pick)
        tail = picked_heads(col_ref[3, at, :], pick)
        from_end = dot(bc_ref[at, :STATE], ends[block])
        kinds = {name: [] for name in ("ds", "z", "values")}
        for first in range(0, GROUP, ROWS_AT):
            local = slice(first, first + ROWS_AT)
            rows = slice(block * GROUP + first, block * GROUP + first + ROWS_AT)
            pieces = {name: [] for name in kinds}
            for pair in range(TILE // 128):
                lanes = slice(pair * 128, (pair + 1) * 128)
                v = v_ref[rows, lanes]
                scaled = step[local, lanes] * v
                ended = tail[local, lanes] * from_end[local, lanes]
                pieces["ds"].append((v * ended).astype(jnp.bfloat16))
                pieces["z"].append((scaled * ended).astype(jnp.bfloat16))
                pieces["values"].append((tail[local, lanes] * scaled).astype(jnp.bfloat16))
                grad = base_ref[rows, lanes] + step[local, lanes] * ended
                dconv_ref[rows, lanes] = grad * slope_ref[rows, lanes]
            for name in kinds:
                kinds[name].append(jnp.concatenate(pieces[name], 1))
        whole = {name: jnp.concatenate(parts, 0) for name, parts in kinds.items()}
        ds_ref[at, :] += dot(whole["ds"], sums)
        z_ref[at, :] += dot(whole["z"], sums)
        dmap_ref[at, :STATE] += dot_nt(whole["values"], ends[block])
        kept = kx_ref[block : block + 1, :] * jnp.sum(ends[block] * starts[block], 0, keepdims=True)
        kd_ref[block] += dot_exact(jnp.broadcast_to(kept, (8, TILE)), sums.astype(jnp.float32))

    @pl.when(turn == pl.num_programs(0) - 1)
    def _():
        here = lax.broadcasted_iota(jnp.int32, (GROUP, GROUP), 0)
        after = (here <= lane_iota((GROUP, GROUP))).astype(jnp.float32)
        before = (here > lane_iota((GROUP, GROUP))).astype(jnp.float32)
        bias_sum = jnp.zeros((1, 128), jnp.float32)
        decay_sum = jnp.zeros((1, 128), jnp.float32)
        for first, rows, lanes in chunks_of(span, MAPS):
            dconv_bc_ref[rows, lanes] = dmap_ref[rows, lanes] * slope_bc_ref[rows, lanes]
        for block in range(count):
            rows = slice(block * GROUP, (block + 1) * GROUP)
            da = dot_exact(after, dc_ref[rows, :]) + kd_ref[block, 0:1, :]
            da = da + dot_exact(before, z_ref[rows, :])
            ds = ds_ref[rows, :] + hp_ref[1:2, :] * da
            drate = ds * sigmoid(rate_ref[HALO + block * GROUP : HALO + (block + 1) * GROUP, :] + hp_ref[0:1, :])
            drate_ref[rows, :] = drate.astype(jnp.bfloat16)
            bias_sum = bias_sum + jnp.sum(drate, 0, keepdims=True)
            decay_sum = decay_sum + jnp.sum(da * hp_ref[1:2, :] * col_ref[1, rows, :], 0, keepdims=True)
        sum_ref[...] = jnp.concatenate([bias_sum, decay_sum, jnp.zeros((6, 128), jnp.float32)], 0)


def conv_back_kernel(
    dconv_ref, dconv_bc_ref, drate_ref, next_ref, x_ref, aux_ref, w_ref, dx_ref, sum_ref, marks_ref
):
    turn = pl.program_id(0)
    last = pl.num_programs(0) - 1
    span = dconv_ref.shape[0]

    @pl.when(turn == 0)
    def _():
        keep_marks(marks_ref, aux_ref, (6, 7, 8))

    def tile(source_ref, width):
        for pair in range(width // 128):
            lanes = slice(pair * 128, (pair + 1) * 128)
            sums = [jnp.zeros((8, 128), jnp.float32) for _ in range(KW + 1)]
            weights = [jnp.broadcast_to(w_ref[tap : tap + 1, lanes], (8, 128)) for tap in range(KW)]
            for first in range(0, span, ROWS_CONV):
                rows = slice(first, first + ROWS_CONV)
                following = next_ref if first + ROWS_CONV == span else source_ref
                at = 0 if first + ROWS_CONV == span else first + ROWS_CONV
                here = source_ref[rows, lanes]
                whole = jnp.concatenate([here, following[at : at + 8, lanes]], 0)
                x = x_ref[HALO + first : HALO + first + ROWS_CONV, lanes]
                split = lambda v: v.reshape(ROWS_CONV // 8, 8, 128)
                x8, here8 = split(x), split(here)
                grad = weights[KW - 1] * here8
                sums[KW] = sums[KW] + jnp.sum(here8, 0)
                sums[KW - 1] = sums[KW - 1] + jnp.sum(here8 * x8, 0)
                for ahead in range(1, KW):
                    later = split(whole[ahead : ahead + ROWS_CONV] * marks_ref[ahead - 1, rows, :])
                    tap = KW - 1 - ahead
                    grad = grad + weights[tap] * later
                    sums[tap] = sums[tap] + jnp.sum(later * x8, 0)
                dx_ref[rows, lanes] = grad.reshape(ROWS_CONV, 128).astype(jnp.bfloat16)
            sums = [jnp.sum(part, 0, keepdims=True) for part in sums]
            sum_ref[:, lanes] = jnp.concatenate(sums + [jnp.zeros((3, 128), jnp.float32)], 0)

    @pl.when(turn < last)
    def _():
        tile(dconv_ref, TILE)

    @pl.when(turn == last)
    def _():
        tile(dconv_bc_ref, MAPS)
        sum_ref[:, MAPS:] = jnp.zeros_like(sum_ref[:, MAPS:])
        dx_ref[:, MAPS : MAPS + 128] = drate_ref[...]
        dx_ref[:, MAPS + 128 :] = jnp.zeros_like(drate_ref)


def scan_kernel(reverse, rows, in_ref, keep_ref, out_ref):
    peers = out_ref.shape[0]
    carried = jnp.zeros((rows, 128), jnp.float32)
    for at in range(peers):
        peer = peers - 1 - at if reverse else at
        out_ref[peer] = carried
        carried = keep_ref[peer, 0:1, :] * carried + in_ref[peer, :rows, :]


def weight_kernel(each, left_ref, right_ref, send_ref, keep_ref):
    slabs, size = send_ref.shape[0], SUM_ROWS
    total = dot(left_ref[...], right_ref[...])
    half = total.shape[0] // 2
    for out_ref, rows in ((keep_ref, total[:half]), (send_ref, total[half:])):
        if slabs == 1:
            out_ref[0] = rows
        else:
            split = rows.reshape(-1, slabs, each // slabs, rows.shape[1])
            for part in range(slabs):
                out_ref[part] = split[:, part].reshape(size, rows.shape[1])


def sums_kernel(counts, orders, *refs):
    pieces = len(counts)
    sends, keeps, out_ref, kept_ref = refs[:pieces], refs[pieces : 2 * pieces], refs[2 * pieces], refs[2 * pieces + 1]
    stages = len(orders[0])
    got = refs[2 * pieces + 2 : 2 * pieces + 2 + stages]
    load_sem, send_sem, recv_sem = refs[2 * pieces + 2 + stages :]
    chunks = sum(counts)
    seq, row = lax.axis_index("seq"), lax.axis_index("rows")
    odd = lax.rem(row, 2)

    def over(at, mask):
        return at + mask * (1 - 2 * lax.rem(at // mask, 2))

    routes = []
    for masks in orders:
        partners = []
        for axis, even_mask, odd_mask in masks:
            if axis == "rows":
                partners.append((seq, over(row, even_mask)))
            else:
                one, two = over(seq, even_mask), over(seq, odd_mask)
                partners.append((one + odd * (two - one), row))
        routes.append(partners)

    barrier = pltpu.get_barrier_semaphore()
    for partner in routes[0]:
        pl.semaphore_signal(
            barrier,
            inc=1,
            device_id={"seq": partner[0], "rows": partner[1]},
            device_id_type=pl.DeviceIdType.MESH,
        )
    pl.semaphore_wait(barrier, stages)

    def second(chunk):
        return (EVERY - lax.rem(chunk, EVERY)) // EVERY

    def copy(stage, chunk, source=None):
        size = SUM_ROWS >> stage
        other = second(chunk)
        main, side = routes[0][stage], routes[1][stage]
        if source is None:
            source = kept_ref.at[chunk] if stage == 0 else kept_ref.at[chunk, pl.ds(size, size)]
        return pltpu.make_async_remote_copy(
            src_ref=source,
            dst_ref=got[stage].at[chunk],
            send_sem=send_sem.at[stage, chunk],
            recv_sem=recv_sem.at[stage, chunk],
            device_id={
                "seq": main[0] + other * (side[0] - main[0]),
                "rows": main[1] + other * (side[1] - main[1]),
            },
            device_id_type=pl.DeviceIdType.MESH,
        )

    def load(chunk, source):
        return pltpu.make_async_copy(source, kept_ref.at[chunk], load_sem.at[chunk])

    def begin(chunk):
        side = second(chunk)
        inner = chunk - chunk // EVERY - 1

        @pl.when((side == 1) & (chunk < chunks))
        def _():
            copy(0, chunk, sends[0].at[chunk // EVERY]).start()
            load(chunk, keeps[0].at[chunk // EVERY]).start()

        base = 0
        for count, send_ref, keep_ref in zip(counts[1:], sends[1:], keeps[1:]):

            @pl.when((side == 0) & (inner >= base) & (inner < base + count))
            def _(base=base, send_ref=send_ref, keep_ref=keep_ref):
                copy(0, chunk, send_ref.at[inner - base]).start()
                load(chunk, keep_ref.at[inner - base]).start()

            base += count

    def first(chunk, _):
        begin(chunk)
        return 0

    lax.fori_loop(0, AHEAD, first, 0)

    def turn(at, _):
        begin(at + AHEAD)
        for stage in range(stages):
            chunk = at - LAG * stage

            @pl.when((chunk >= 0) & (chunk < chunks))
            def _():
                size = SUM_ROWS >> stage
                if stage == 0:
                    load(chunk, keeps[0].at[0]).wait()
                copy(stage, chunk, sends[0].at[0] if stage == 0 else None).wait_recv()
                total = kept_ref[chunk, :size] + got[stage][chunk]
                if stage + 1 < stages:
                    kept_ref[chunk, :size] = total
                    copy(stage + 1, chunk).start()
                else:
                    out_ref[chunk] = total

        return 0

    lax.fori_loop(0, chunks + LAG * (stages - 1), turn, 0)

    def ended(chunk, _):
        for stage in range(stages):
            copy(stage, chunk, sends[0].at[0] if stage == 0 else None).wait_send()
        return 0

    lax.fori_loop(0, chunks, ended, 0)


def edge(weights, width, first):
    row = lax.broadcasted_iota(jnp.int32, weights.shape, 0)
    return jnp.where(first + row < width, weights, jnp.zeros_like(weights))


def project_kernel(width, first_block, x_ref, before_ref, gain_ref, w_ref, normed_ref, out_ref, ext_ref):
    turn = pl.program_id(0)
    last = pl.num_programs(0) - 1

    @pl.when(turn == 0)
    def _():
        def scaled(values):
            scale = lax.rsqrt(jnp.mean(values * values, 1, keepdims=True) + EPS)
            return (values * scale * gain_ref[...]).astype(jnp.bfloat16)

        for first in range(0, x_ref.shape[0], ROWS_AT):
            rows = slice(first, first + ROWS_AT)
            normed_ref[rows, :] = scaled(x_ref[rows, :])
        ext_ref[...] = jnp.concatenate([scaled(before_ref[...]), normed_ref[...]], 0)

    @pl.when(turn < last)
    def _():
        out_ref[...] = dot_nt(ext_ref[...], w_ref[0])

    @pl.when(turn == last)
    def _():
        out_ref[...] = dot_nt(ext_ref[...], edge(w_ref[0], width, (first_block + last) * TILE))


def gate_kernel(normed_ref, w_ref, out_ref):
    out_ref[...] = dot_nt(normed_ref[...], w_ref[0])


def project_back_gate_kernel(dgate_ref, w_ref, out_ref):
    @pl.when(pl.program_id(0) == 0)
    def _():
        out_ref[...] = dot(dgate_ref[...], w_ref[0])

    @pl.when(pl.program_id(0) > 0)
    def _():
        out_ref[...] += dot(dgate_ref[...], w_ref[0])


def project_back_kernel(
    width, first_block, part_ref, dmixed_ref, w_ref, x_ref, grad_ref, gain_ref,
    new_ref, low_ref, sum_ref,
    acc_ref,
):
    turn = pl.program_id(0)
    last = pl.num_programs(0) - 1

    @pl.when(turn == 0)
    def _():
        acc_ref[...] = part_ref[...] + dot(dmixed_ref[...], w_ref[0])

    @pl.when((turn > 0) & (turn < last))
    def _():
        acc_ref[...] += dot(dmixed_ref[...], w_ref[0])

    @pl.when(turn == last)
    def _():
        acc_ref[...] += dot(dmixed_ref[...], edge(w_ref[0], width, (first_block + last) * TILE))
        total = jnp.zeros((8, x_ref.shape[1]), jnp.float32)
        for first in range(0, x_ref.shape[0], 16):
            rows = slice(first, first + 16)
            x = x_ref[rows, :]
            grad = acc_ref[rows, :]
            scale = lax.rsqrt(jnp.mean(x * x, 1, keepdims=True) + EPS)
            pulled = grad * gain_ref[...]
            cross = jnp.mean(pulled * x, 1, keepdims=True)
            scaled = x * scale
            total = total + grad[:8] * scaled[:8] + grad[8:] * scaled[8:]
            new = grad_ref[rows, :] + (scale * pulled - x * (scale * scale * scale * cross))
            new_ref[rows, :] = new
            low_ref[rows, :] = new.astype(jnp.bfloat16)
        sum_ref[...] = total


def plain_weight_kernel(left_ref, right_ref, *refs):
    out_ref = refs[-1]
    out_ref[...] = dot(left_ref[...], right_ref[...], (((0,), (0,)), ((), ())))


def sort_kernel(source_ref, values_ref, out_ref):
    pick = (source_ref[...] == lane_iota((source_ref.shape[0], values_ref.shape[1]))).astype(jnp.bfloat16)
    out_ref[...] = dot_nt(pick, values_ref[...]).astype(jnp.bfloat16)


def assemble_kernel(outs, ins, total_ref, in_ref, all_out_ref, all_in_ref):
    rows = total_ref.shape[1]
    for level, parts in enumerate(outs):
        for part, places in enumerate(parts):
            for at, place in enumerate(places):
                lanes = slice(at * 256, (at + 1) * 256)
                all_out_ref[level, part * rows : (part + 1) * rows, lanes] = total_ref[place]
    columns = all_in_ref.shape[2]
    for at, place in enumerate(ins):
        size = min(256, columns - at * 256)
        all_in_ref[0, :, at * 256 : at * 256 + size] = total_ref[place, :, :size]
    all_in_ref[1] = in_ref[:, :columns]


def small_kernel(in_ref, gain_ref, conv_ref, bias_ref, decay_ref, dt_ref, skip_ref, gate_ref):
    total = jnp.sum(in_ref[...], 0)
    for level in range(LAYERS):
        at = SMALL_ROWS * level
        row = lambda place, ref: total[at + place : at + place + 1, : ref.shape[1]]
        here = slice(level, level + 1)
        gain_ref[here, :] = row(0, gain_ref)
        taps = jnp.concatenate([total[at + 1 : at + 1 + KW], jnp.zeros((128 - KW, 128), jnp.float32)], 0)
        conv_ref[level] = taps.T[: conv_ref.shape[1], :KW]
        bias_ref[here, :] = row(1 + KW, bias_ref)
        gate_ref[here, :] = row(2 + KW, gate_ref)
        decay_ref[here, :] = row(3 + KW, decay_ref)
        dt_ref[here, :] = row(4 + KW, dt_ref)
        skip_ref[here, :] = row(5 + KW, skip_ref)


def full(shape):
    return pl.BlockSpec(shape, lambda *at: (0,) * len(shape))


def shape_of(dims, dtype=jnp.float32):
    return jax.ShapeDtypeStruct(dims, dtype)


def vmem(dims, dtype=jnp.float32):
    return pltpu.VMEM(dims, dtype)


def make_states(peers, mixed_ext, aux, conv, hp):
    span = aux.shape[0]
    rate = pl.BlockSpec((span + HALO, 128), lambda g: (0, CHANNELS // 128))
    groups = DI // TILE
    chunks = peers * 128 // DI
    tile = lambda rows: pl.BlockSpec((rows, TILE), lambda g: (0, g))
    maps = lambda rows: pl.BlockSpec((rows, MAPS), lambda g: (0, DI // MAPS))
    pay = (TILE // 128 * chunks, STATE // chunks + 8, 128)
    return pcall(
        states_kernel,
        (groups,),
        [tile(span + HALO), maps(span + HALO), rate, full((span, 128)), tile(8), maps(8), full((8, 128))],
        [
            tile(span),
            full((span, MAPS)),
            full((4, span, 128)),
            full((128, span)),
            tile(STATE),
            tile(8),
            pl.BlockSpec(pay, lambda g: (g, 0, 0)),
            tile(span),
            full((span, MAPS)),
        ],
        [
            shape_of((span, DI)),
            shape_of((span, MAPS)),
            shape_of((4, span, 128)),
            shape_of((128, span)),
            shape_of((STATE, DI)),
            shape_of((8, DI)),
            shape_of((peers,) + pay[1:]),
            shape_of((span, DI)),
            shape_of((span, MAPS)),
        ],
        [vmem((span // GROUP, STATE, GROUP), jnp.bfloat16), vmem((KW - 1, span, 128))],
        (mixed_ext, mixed_ext, mixed_ext, aux, conv, conv, hp),
        flops=2 * span * DI * STATE,
        nbytes=12 * span * DI,
    )


def block_rows(span):
    wide = pl.BlockSpec((GROUP, DI), lambda b: (b, 0))
    maps = pl.BlockSpec((GROUP, MAPS), lambda b: (b, 0))
    col = pl.BlockSpec((4, GROUP, 128), lambda b: (0, b, 0))
    row = pl.BlockSpec((128, GROUP), lambda b: (0, b))
    aux = pl.BlockSpec((GROUP, 128), lambda b: (b, 0))
    auxr = pl.BlockSpec((8, GROUP), lambda b: (0, b))
    return wide, maps, col, row, aux, auxr


def inner(bc, values, col, cumr, aux, auxr):
    span = values.shape[0]
    wide, maps, cols, row, auxs, auxrs = block_rows(span)
    return pcall(
        inner_kernel,
        (span // GROUP,),
        [maps, wide, cols, row, auxs, auxrs],
        wide,
        shape_of((span, DI)),
        [vmem((GROUP, GROUP))],
        (bc, values, col, cumr, aux, auxr),
        flops=2 * span * GROUP * DI * 4,
        nbytes=8 * span * DI,
    )


def finish(yi, values, gate, bc, col, state_in, made, kx, ch):
    span = values.shape[0]
    wide = pl.BlockSpec((ROWS_STEP, DI), lambda b: (b, 0))
    maps = pl.BlockSpec((ROWS_STEP, MAPS), lambda b: (b, 0))
    cols = pl.BlockSpec((4, ROWS_STEP, 128), lambda b: (0, b, 0))
    return pcall(
        finish_kernel,
        (span // ROWS_STEP,),
        [wide, wide, wide, maps, cols, full((DI // 128, STATE, 128)), full((STATE, DI)), full((8, DI)), full((8, DI))],
        [wide, wide],
        [shape_of((span, DI)), shape_of((span, DI), jnp.bfloat16)],
        [vmem((ROWS_STEP, DI))],
        (yi, values, gate, bc, col, state_in, made, kx, ch),
        flops=2 * span * DI * STATE,
        nbytes=18 * span * DI,
    )


def gate_back(peers, dno, y, gate, values, bc, col, kx, ch, after=()):
    span = values.shape[0]
    chunks = peers * 128 // DI
    wide = pl.BlockSpec((ROWS_STEP, DI), lambda b: (b, 0))
    maps = pl.BlockSpec((ROWS_STEP, MAPS), lambda b: (b, 0))
    cols = pl.BlockSpec((4, ROWS_STEP, 128), lambda b: (0, b, 0))
    pay = (peers, STATE // chunks, 128)
    return pcall(
        gate_back_kernel,
        (span // ROWS_STEP,),
        [wide, wide, wide, wide, maps, cols, full((8, DI)), full((8, DI))],
        [wide, wide, full((8, DI)), full((STATE, DI)), full(pay)],
        [
            shape_of((span, DI)),
            shape_of((span, DI), jnp.bfloat16),
            shape_of((8, DI)),
            shape_of((STATE, DI)),
            shape_of(pay),
        ],
        [vmem((ROWS_STEP, DI)), vmem((2, ROWS_STEP, DI))],
        (dno, y, gate, values, bc, col, kx, ch),
        flops=2 * span * DI * STATE,
        nbytes=22 * span * DI,
        after=after,
    )


def inner_back(bc, values, dy, col, cumr, aux, auxr, after=()):
    span = values.shape[0]
    wide, maps, cols, row, auxs, auxrs = block_rows(span)
    return pcall(
        inner_back_kernel,
        (span // GROUP,),
        [maps, wide, wide, cols, row, auxs, auxrs],
        [wide, maps],
        [shape_of((span, DI)), shape_of((span, MAPS))],
        [vmem((GROUP, GROUP)), vmem((GROUP, GROUP))],
        (bc, values, dy, col, cumr, aux, auxr),
        flops=2 * span * GROUP * DI * 8,
        nbytes=12 * span * DI,
        after=after,
    )


def states_pre(xi, values, dy, yi, bc, col, state_in, made, kx, dbc, ch):
    span = values.shape[0]
    tile = lambda rows: pl.BlockSpec((rows, TILE), lambda g: (0, g))
    state = pl.BlockSpec((TILE // 128, STATE, 128), lambda g: (g, 0, 0))
    small, maps = full((span, 128)), full((span, MAPS))
    return pcall(
        states_pre_kernel,
        (DI // TILE,),
        [
            tile(span), tile(span), tile(span), tile(span), maps, full((4, span, 128)),
            state, tile(STATE), tile(8), maps, tile(8),
        ],
        [tile(span), small, small, maps],
        [shape_of((span, DI)), shape_of((span, 128)), shape_of((span, 128)), shape_of((span, MAPS))],
        [],
        (xi, values, dy, yi, bc, col, state_in, made, kx, dbc, ch),
        flops=4 * span * DI * STATE,
        nbytes=20 * span * DI,
    )


def states_back(base, values, slope, slope_bc, bc, col, dso, state_in, made, d1, kx, ds, dc, dmap, hp, mixed_ext):
    span = values.shape[0]
    tile = lambda rows: pl.BlockSpec((rows, TILE), lambda g: (0, g))
    state = pl.BlockSpec((TILE // 128, STATE, 128), lambda g: (g, 0, 0))
    small, maps = full((span, 128)), full((span, MAPS))
    rate = pl.BlockSpec((span + HALO, 128), lambda g: (0, CHANNELS // 128))
    return pcall(
        states_back_kernel,
        (DI // TILE,),
        [
            tile(span), tile(span), tile(span), maps, maps, full((4, span, 128)),
            state, state, tile(STATE), tile(STATE), tile(8), small, small, maps, full((8, 128)), rate,
        ],
        [tile(span), maps, small, full((8, 128))],
        [shape_of((span, DI)), shape_of((span, MAPS)), shape_of((span, 128), jnp.bfloat16), shape_of((8, 128))],
        [vmem((span, 128)), vmem((span, 128)), vmem((span // GROUP, 8, 128)), vmem((span, MAPS))],
        (base, values, slope, slope_bc, bc, col, dso, state_in, made, d1, kx, ds, dc, dmap, hp, mixed_ext),
        flops=4 * span * DI * STATE,
        nbytes=16 * span * DI,
    )


def conv_back(dconv, dconv_bc, drate, following, mixed_ext, aux, conv, after=()):
    span = dconv.shape[0]
    groups = DI // TILE
    tile = lambda rows: pl.BlockSpec((rows, TILE), lambda g: (0, g))
    return pcall(
        conv_back_kernel,
        (groups + 1,),
        [
            pl.BlockSpec((span, TILE), lambda g: (0, jnp.minimum(g, groups - 1))),
            full((span, MAPS)), full((span, 128)), tile(HALO), tile(span + HALO), full((span, 128)), tile(8),
        ],
        [tile(span), tile(8)],
        [shape_of((span, DI + TILE), jnp.bfloat16), shape_of((8, DI + TILE))],
        [vmem((KW - 1, span, 128))],
        (dconv, dconv_bc, drate, following, mixed_ext, aux, conv),
        flops=8 * span * DI,
        nbytes=10 * span * DI,
        after=after,
    )


def project(depth, hidden, before, gain, weight):
    span, width = hidden.shape
    columns = weight.shape[1]
    first, blocks = DI // TILE, pl.cdiv(columns - DI, TILE)
    return pcall(
        partial(project_kernel, columns, first),
        (blocks,),
        [
            full((span, width)), full((HALO, width)), full((1, width)),
            pl.BlockSpec((1, TILE, width), lambda g: (depth, first + g, 0)),
        ],
        [full((span, width)), pl.BlockSpec((span + HALO, TILE), lambda g: (0, g))],
        [shape_of((span, width), jnp.bfloat16), shape_of((span + HALO, blocks * TILE))],
        [vmem((span + HALO, width), jnp.bfloat16)],
        (hidden, before, gain[None], weight),
        flops=2 * span * width * blocks * TILE,
        nbytes=4 * span * blocks * TILE,
    )


def project_gate(depth, normed, weight):
    span, width = normed.shape
    return pcall(
        gate_kernel,
        (DI // TILE,),
        [full((span, width)), pl.BlockSpec((1, TILE, width), lambda g: (depth, g, 0))],
        pl.BlockSpec((span, TILE), lambda g: (0, g)),
        shape_of((span, DI)),
        [],
        (normed, weight),
        flops=2 * span * width * DI,
        nbytes=4 * span * DI,
    )


def project_back_gate(depth, dgate, weight, after=()):
    span, width = dgate.shape[0], weight.shape[2]
    return pcall(
        project_back_gate_kernel,
        (DI // TILE,),
        [pl.BlockSpec((span, TILE), lambda g: (0, g)), pl.BlockSpec((1, TILE, width), lambda g: (depth, g, 0))],
        full((span, width)),
        shape_of((span, width)),
        [],
        (dgate, weight),
        flops=2 * span * width * DI,
        nbytes=2 * width * DI,
        after=after,
    )


def project_back(depth, part, dmixed, weight, entry, gradient, gain, after=()):
    span, width = entry.shape
    columns = weight.shape[1]
    first, blocks = DI // TILE, pl.cdiv(columns - DI, TILE)
    return pcall(
        partial(project_back_kernel, columns, first),
        (blocks,),
        [
            full((span, width)),
            pl.BlockSpec((span, TILE), lambda g: (0, g)),
            pl.BlockSpec((1, TILE, width), lambda g: (depth, first + g, 0)),
            full((span, width)), full((span, width)), full((1, width)),
        ],
        [full((span, width)), full((span, width)), full((8, width))],
        [shape_of((span, width)), shape_of((span, width), jnp.bfloat16), shape_of((8, width))],
        [vmem((span, width))],
        (part, dmixed, weight, entry, gradient, gain[None]),
        flops=2 * span * width * (columns - DI),
        nbytes=4 * span * columns,
        after=after,
    )


def plain_weight(left, right, first, tiles, total=None, after=()):
    span, width = left.shape
    columns = right.shape[1]
    return pcall(
        plain_weight_kernel,
        (columns // 256,),
        [full((span, width)), pl.BlockSpec((span, 256), lambda g: (0, g))]
        + ([] if total is None else [pl.BlockSpec(memory_space=pltpu.HBM)]),
        pl.BlockSpec((width, 256), lambda g: (0, first + g)),
        shape_of((width, 256 * tiles)),
        [],
        (left, right) if total is None else (left, right, total),
        flops=2 * span * width * columns,
        nbytes=4 * width * columns,
        after=after,
        aliases={} if total is None else {2: 0},
    )


def scan_states(received, keeps, reverse, after=()):
    peers = received.shape[0]
    rows = STATE * DI // 128 // peers
    return pcall(
        partial(scan_kernel, reverse, rows),
        (1,),
        [full(received.shape), full(keeps.shape)],
        full((peers, rows, 128)),
        shape_of((peers, rows, 128)),
        [],
        (received, keeps),
        nbytes=8 * peers * rows * 128,
        after=after,
    )


def exchange(parts):
    return lax.all_to_all(parts, "seq", split_axis=0, concat_axis=0, tiled=True)


def shifted(value, steps):
    count = lax.axis_size("seq")
    first, last = max(0, -steps), min(count, count - steps)
    return lax.ppermute(value, "seq", [(source, source + steps) for source in range(first, last)])


def doc_table(lengths, first, count):
    starts = jnp.cumsum(lengths, -1) - lengths
    places = first + jnp.arange(count, dtype=jnp.int32)
    return jnp.sum((starts[None, :] <= places[:, None]).astype(jnp.int32), -1) - 1


def token_marks(lengths, span):
    docs_all = doc_table(lengths, lax.axis_index("seq") * span - HALO, span + 2 * HALO)
    docs = docs_all[HALO : HALO + span]
    ends = docs_all[HALO - 1 : HALO + span : GROUP]
    prior, final = jnp.repeat(ends[:-1], GROUP), jnp.repeat(ends[1:], GROUP)
    near = lambda step: docs_all[HALO + step : HALO + step + span] == docs
    marks = [near(-3), near(-2), near(-1), docs == prior, docs == final, docs, near(1), near(2), near(3)]
    marks = jnp.stack([mark.astype(jnp.float32) for mark in marks], 1)
    aux = jnp.pad(marks, ((0, 0), (0, 128 - marks.shape[1])))
    auxr = jnp.broadcast_to(docs.astype(jnp.float32)[None, :], (8, span))
    return aux, auxr


def halving(count, rows, turned=False):
    masks = [rows << bit for bit in range(count.bit_length() - 1)]
    near, far = masks[:2], masks[2:]
    pick = lambda pair: far + pair if turned else pair + far
    return [1 << bit for bit in range(rows.bit_length() - 1)], pick(near), pick(near[::-1])


def slab_order(turned=False):
    count, rows = lax.axis_size("seq"), lax.axis_size("rows")
    row_masks, even, odd = halving(count, rows, turned)
    stages = len(row_masks) + len(even)
    place = jnp.arange(count * rows, dtype=jnp.int32)
    bit = lambda stage: (place >> (stages - 1 - stage)) & 1
    slab = lax.axis_index("seq") * rows + lax.axis_index("rows") + 0 * place
    for stage, mask in enumerate(row_masks):
        slab = slab ^ (bit(stage) * mask)
    swapped = slab & 1
    for at, (one, two) in enumerate(zip(even, odd)):
        slab = slab ^ (bit(len(row_masks) + at) * jnp.where(swapped == 1, two, one))
    return slab


def in_order(values, order, after=()):
    span, width = values.shape
    size = width // order.shape[0]
    source = (order[:, None] * size + jnp.arange(size, dtype=jnp.int32)[None, :]).reshape(-1, 1)
    return pcall(
        sort_kernel,
        (width // 256,),
        [pl.BlockSpec((256, 1), lambda g: (g, 0)), full((span, width))],
        pl.BlockSpec((256, span), lambda g: (g, 0)),
        shape_of((width, span), jnp.bfloat16),
        [],
        (source, values),
        flops=2 * span * width * width,
        nbytes=4 * span * width,
        after=after,
    )


def weight_sums(devices, left, right, first=0, tiles=None, after=()):
    width, span = left.shape
    columns = right.shape[1] if tiles is None else 256 * tiles
    slabs = width // 2 // SUM_ROWS
    out = pl.BlockSpec((slabs, SUM_ROWS, 256), lambda g: (g, 0, 0))
    return pcall(
        partial(weight_kernel, width // devices),
        (columns // 256,),
        [full((width, span)), pl.BlockSpec((span, 256), lambda g: (0, first + g))],
        [out, out],
        [shape_of((columns // 256 * slabs, SUM_ROWS, 256))] * 2,
        [],
        (left, right),
        flops=2 * span * width * columns,
        nbytes=4 * width * columns,
        after=after,
    )


def summed(parts, after=()):
    count, rows = lax.axis_size("seq"), lax.axis_size("rows")
    orders = []
    for turned in (False, True):
        row_masks, even, odd = halving(count, rows, turned)
        masks = [("rows", mask, mask) for mask in row_masks]
        orders.append(masks + [("seq", one // rows, two // rows) for one, two in zip(even, odd)])
    counts = [send.shape[0] for send, _ in parts]
    chunks, stages = sum(counts), len(orders[0])
    last = SUM_ROWS >> (stages - 1)
    anywhere = pl.BlockSpec(memory_space=pltpu.HBM)

    def run(*refs):
        taken = 2 * len(parts)
        sums_kernel(counts, orders, *refs[:taken], *refs[taken + len(after) :])

    return pl.pallas_call(
        run,
        in_specs=[anywhere] * (2 * len(parts) + len(after)),
        out_specs=pl.BlockSpec(memory_space=pltpu.VMEM),
        out_shape=shape_of((chunks, last, 256)),
        scratch_shapes=[vmem((chunks, SUM_ROWS, 256))]
        + [vmem((chunks, SUM_ROWS >> stage, 256)) for stage in range(stages)]
        + [
            pltpu.SemaphoreType.DMA((chunks,)),
            pltpu.SemaphoreType.DMA((stages, chunks)),
            pltpu.SemaphoreType.DMA((stages, chunks)),
        ],
        compiler_params=pltpu.CompilerParams(
            vmem_limit_bytes=VMEM_BYTES, collective_id=0, has_side_effects=True
        ),
        cost_estimate=pl.CostEstimate(flops=0, bytes_accessed=400 * 1024 * 1024, transcendentals=0),
    )(*[send for send, _ in parts], *[keep for _, keep in parts], *after)


def scattered(total):
    return lax.psum_scatter(total, AXES, scatter_dimension=0, tiled=True)


def matmul(a, b):
    return jnp.dot(a, b, preferred_element_type=jnp.float32)


def matmul_tn(a, b):
    return jnp.einsum("tn,tm->nm", a, b, preferred_element_type=jnp.float32)


def matmul_nt(a, b):
    return jnp.einsum("tn,mn->tm", a, b, preferred_element_type=jnp.float32)


def padded(rows, width):
    table = jnp.stack([jnp.pad(row, (0, width - row.shape[0])) for row in rows])
    return jnp.pad(table, ((0, 8 - len(rows)), (0, 0)))


def local(
    inputs,
    lengths,
    norm_gain,
    in_weight,
    conv_weight,
    conv_bias,
    log_decay,
    dt_bias,
    skip,
    gate_gain,
    out_weight,
    cotangent,
):
    _, span, width = inputs.shape
    peers = lax.axis_size("seq")
    aux, auxr = token_marks(lengths[0], span)
    order = slab_order()
    in_weight = jnp.swapaxes(in_weight, 1, 2)
    hidden = inputs[0]
    saved = []
    for depth in range(LAYERS):
        conv = jnp.concatenate([conv_weight[depth].T, conv_bias[depth][None], jnp.zeros((3, CHANNELS), jnp.float32)])
        conv = jnp.pad(conv, ((0, 0), (0, DI + TILE - CHANNELS)))
        hp = padded([dt_bias[depth], -jnp.exp(log_decay[depth])], 128)
        ch = padded([jnp.repeat(skip[depth], HEAD_DIM), gate_gain[depth]], DI)
        before = shifted(hidden[span - HALO :], 1)
        normed, mixed_ext = project(depth, hidden, before, norm_gain[depth], in_weight)
        values, bc, col, cumr, made, kx, pay, slope, slope_bc = make_states(peers, mixed_ext, aux, conv, hp)
        received = exchange(pay)
        gate = project_gate(depth, normed, in_weight)
        keeps = received[:, -8:]
        waits = (gate,)
        if depth:
            ready = [in_order(values, by, after=(pay,)) for values, by in sorting]
            waits += tuple(ready)
        scanned = scan_states(received, keeps, False, after=waits)
        state_in = exchange(scanned).reshape(DI // 128, STATE, 128)
        yi = inner(bc, values, col, cumr, aux, auxr)
        y, out_low = finish(yi, values, gate, bc, col, state_in, made, kx, ch)
        saved.append(
            (hidden, normed, mixed_ext, gate, values, bc, col, cumr, made, kx, keeps, state_in, y, out_low, yi)
            + (slope, slope_bc, conv, hp, ch)
        )
        sorting = [(out_low, order), (normed, order), (normed, slab_order(True))]
        hidden = hidden + matmul(out_low, out_weight[depth])
    gradient = cotangent[0]
    grad_low = gradient.astype(jnp.bfloat16)
    devices = lax.axis_size(AXES)
    collected = [None] * LAYERS
    for depth in reversed(range(LAYERS)):
        entry, normed, mixed_ext, gate, values, bc, col, cumr, made, kx, keeps, state_in, y, out_low, yi = saved[depth][:15]
        slope, slope_bc, conv, hp, ch = saved[depth][15:]
        dno = matmul_nt(grad_low, out_weight[depth])
        dy, dgate, gate_sums, d1, pay = gate_back(peers, dno, y, gate, values, bc, col, kx, ch)
        received = exchange(pay)
        if depth:
            out_sorted = in_order(out_low, order, after=(pay,))
            high_chunks = weight_sums(devices, out_sorted, grad_low)
            waits = high_chunks[:1]
        else:
            out_sorted, normed_sorted, turned_sorted = ready
            out_chunks = weight_sums(devices, out_sorted, grad_low, after=(pay,))
            gate_chunks = weight_sums(devices, normed_sorted, dgate, after=out_chunks[:1])
            waits = (gate_chunks[0],)
        scanned = scan_states(received, keeps, True, after=waits)
        dso = exchange(scanned).reshape(DI // 128, STATE, 128)
        tiles = (DI + DI + TILE) // 256
        in_total = plain_weight(normed, dgate, 0, tiles, after=(scanned,)) if depth else None
        xi, dbc = inner_back(bc, values, dy, col, cumr, aux, auxr, after=(in_total,) if depth else ())
        base, ds, dc, dmap = states_pre(xi, values, dy, yi, bc, col, state_in, made, kx, dbc, ch)
        dconv, dconv_bc, drate, head_rows = states_back(
            base, values, slope, slope_bc, bc, col, dso, state_in, made, d1, kx, ds, dc, dmap, hp, mixed_ext
        )
        following = shifted(jnp.concatenate([dconv[:HALO], dconv_bc[:HALO]], 1), -1)
        part = project_back_gate(depth, dgate, in_weight, after=(head_rows,))
        dmixed, conv_sums = conv_back(dconv, dconv_bc, drate, following, mixed_ext, aux, conv, after=(part,))
        if depth:
            in_total = plain_weight(normed, dmixed, DI // 256, tiles, in_total)
            high_in = scattered(in_total)
            waits = (in_total,)
        else:
            others = [high_chunks, out_chunks, gate_chunks]
            count = sum(part[0].shape[0] for part in others) + dmixed.shape[1] // 256
            turned_tiles = pl.cdiv(count, EVERY)
            waits = ()
        gradient, grad_low, gain_sums = project_back(
            depth, part, dmixed, in_weight, entry, gradient, norm_gain[depth], after=waits
        )
        if depth == 0:
            turned_chunks = weight_sums(devices, turned_sorted, dmixed, 0, turned_tiles, after=(gain_sums,))
            rest_tiles = dmixed.shape[1] // 256 - turned_tiles
            rest_chunks = weight_sums(
                devices, normed_sorted, dmixed, turned_tiles, rest_tiles, after=turned_chunks[:1]
            )
        gain_grad = jnp.sum(gain_sums, 0)
        spread = lambda part: jnp.moveaxis(part.reshape(part.shape[0], devices, -1), 0, 1)
        widened = lambda part: jnp.pad(part, ((0, 0), (0, 0), (0, 128 - part.shape[2])))
        skip_sums = jnp.sum(gate_sums[1].reshape(HEADS, HEAD_DIM), 1)
        heads = jnp.stack([head_rows[1], head_rows[0], jnp.pad(skip_sums, (0, 128 - HEADS))])
        collected[depth] = jnp.concatenate(
            [
                widened(spread(gain_grad[None])),
                widened(spread(conv_sums[: KW + 1, :CHANNELS])),
                widened(spread(gate_sums[:1])),
                jnp.broadcast_to(heads, (devices,) + heads.shape),
            ],
            1,
        )
    total = summed([turned_chunks, high_chunks, out_chunks, gate_chunks, rest_chunks], after=(gradient,))
    places = list(range(total.shape[0]))
    between = [place for place in places if place % EVERY]
    n_out = out_chunks[0].shape[0]
    n_gate = 2 * n_out + gate_chunks[0].shape[0]
    slabs = n_out * 256 // out_weight.shape[2]
    columns = between[2 * n_out : n_gate] + places[::EVERY] + between[n_gate:]
    columns = columns[: pl.cdiv(in_weight.shape[1], 256)]
    outs = [[between[first + part : first + n_out : slabs] for part in range(slabs)] for first in (n_out, 0)]
    shapes = [(LAYERS, slabs * total.shape[1], out_weight.shape[2]), (LAYERS, high_in.shape[0], in_weight.shape[1])]
    all_out, all_in = pcall(
        partial(assemble_kernel, outs, columns),
        (1,),
        [full(total.shape), full(high_in.shape)],
        [full(shape) for shape in shapes],
        [shape_of(shape) for shape in shapes],
        [],
        (total, high_in),
        nbytes=4 * 1024 * 1024,
    )
    table = jnp.concatenate(collected, 1)
    table = jnp.pad(table, ((0, 0), (0, -table.shape[1] % 8), (0, 0)))
    table = lax.all_to_all(table, AXES, split_axis=0, concat_axis=0, tiled=True)
    mine = lambda whole: (LAYERS, whole.shape[1] // devices) + whole.shape[2:]
    shapes = [mine(norm_gain), mine(conv_weight), mine(conv_bias)] + [(LAYERS, HEADS)] * 3 + [mine(gate_gain)]
    norm_gain_grad, conv_w_grad, conv_b_grad, decay_grad, bias_grad, skip_grad, gain_grad = pcall(
        small_kernel,
        (1,),
        [full(table.shape)],
        [full(shape) for shape in shapes],
        [shape_of(shape) for shape in shapes],
        [],
        (table,),
        nbytes=4 * table.size,
    )
    return (
        hidden[None],
        gradient[None],
        norm_gain_grad,
        all_in,
        conv_w_grad,
        conv_b_grad,
        decay_grad,
        bias_grad,
        skip_grad,
        gain_grad,
        all_out,
    )


def solution(mesh):
    in_specs = (
        P("rows", "seq", None),
        P("rows", None),
        P(),
        P(),
        P(),
        P(),
        P(),
        P(),
        P(),
        P(),
        P(),
        P("rows", "seq", None),
    )
    out_specs = (
        P("rows", "seq", None),
        P("rows", "seq", None),
        P(None, ("seq", "rows")),
        P(None, ("seq", "rows"), None),
        P(None, ("seq", "rows"), None),
        P(None, ("seq", "rows")),
        P(),
        P(),
        P(),
        P(None, ("seq", "rows")),
        P(None, ("seq", "rows"), None),
    )
    return jax.shard_map(local, mesh=mesh, in_specs=in_specs, out_specs=out_specs, check_vma=False)
```
